512 devices in a mesh: dom: 128 (over z, y, core), grp: 4 (over x).
Axes of the slice: x: 4, y: 8, z: 8, core: 2. Of those that a mesh axis runs over, the one named last changes fastest.
Arguments:
- source_emb: float32 [400, 65536], P(None, ('dom', 'grp')), may hold values from -2.5 to 2.5
- source_state: float32 [65536], P(('dom', 'grp')), may hold values from 0.005 to 0.1
- dest_emb: float32 [400, 65536], P(None, ('dom', 'grp')), may hold values from -2.5 to 2.5
- dest_state: float32 [65536], P(('dom', 'grp')), may hold values from 0.005 to 0.1
- relations: float32 [400, 768], replicated, may hold values from -4 to 4
- relation_state: float32 [768], replicated, may hold values from 1 to 30
- partner: int32 [128, 4], P('dom', 'grp'), may hold values from 0 to 127, as said below
- edge_count: int32 [128, 4], P('dom', 'grp'), may hold values from 1 to 1024, as said below
- source_rows: int32 [128, 4, 1024], P('dom', 'grp'), may hold values from 0 to 127
- target_rows: int32 [128, 4, 1024], P('dom', 'grp'), may hold values from 0 to 127
- relation_index: int32 [128, 4, 1024], P('dom', 'grp'), may hold values from 0 to 767
- negative_rows: int32 [128, 4, 2048], P('dom', 'grp'), may hold values from 0 to 127
Outputs:
- source_out: float32 [400, 65536], P(None, ('dom', 'grp'))
- source_state_out: float32 [65536], P(('dom', 'grp'))
- dest_out: float32 [400, 65536], P(None, ('dom', 'grp'))
- dest_state_out: float32 [65536], P(('dom', 'grp'))
- relations_out: float32 [400, 768], replicated
- relation_state_out: float32 [768], replicated
The draws below stay inside these ranges and needn't reach their ends.
Inputs may be any that keep to these rules, and one draw needn't show every extreme that they name: For each grp index g, partner[:, g] is a permutation of 0 .. 127. `edge_count`: some device has all 1024 edges live.
All inputs are finite; a program needn't handle non-finite values.
Results may differ from the reference program's by a relative error of at most 0.0013.
The reference program's roundings to bfloat16 on the way (of `noise` and `grad_neg`) count: a program that leaves them out, or rounds other values in their place, can miss the bound.
Values sent between devices are 32-bit elements; how exact they have to be, the bound alone decides.
No kernel may reach another device: no remote copies, remote signals or barrier semaphores. Data moves between devices by JAX's collectives and lax.ppermute only.
A program may use at most 64 MiB of HBM per device.

```python
import math
import jax
import jax.numpy as jnp
from jax import lax

DIM = 400
HALF = 200
NREL = 768
BLOCK = 128
SPAN = 512
SPANS = 2
NEG = 1024
DOMAINS = 128
GROUPS = 4
EDGES = 1024
ENTITIES = 65536


def draw_partner(key, part):
    key = jax.random.fold_in(key, 3)
    keys = jax.random.split(key, GROUPS)
    orders = jax.vmap(lambda single: jax.random.permutation(single, DOMAINS))(keys)
    return orders.T.astype(jnp.int32)


def draw_edge_count(key, part):
    key = jax.random.fold_in(key, 7)
    first_key, second_key = jax.random.split(key)
    counts = jax.random.randint(first_key, (DOMAINS * GROUPS,), 1, EDGES + 1, dtype=jnp.int32)
    chosen = jax.random.randint(second_key, (), 0, DOMAINS * GROUPS, dtype=jnp.int32)
    counts = jnp.where(jnp.arange(DOMAINS * GROUPS, dtype=jnp.int32) == chosen, EDGES, counts)
    return counts.reshape(DOMAINS, GROUPS).astype(jnp.int32)


def place_ends(drawn, own_key, low, largest):
    longest = drawn.shape.index(max(drawn.shape))
    spots = []
    for shift in (0, 1):
        where = [jax.random.randint(jax.random.fold_in(own_key, axis), (), 0, length) for axis, length in enumerate(drawn.shape)]
        where[longest] = (where[longest] + shift) % drawn.shape[longest]
        spots.append(tuple(where))
    return drawn.at[spots[0]].set(low).at[spots[1]].set(largest)


def block_levels(stream_key, extent, shards, smallest, high):
    def one(dim, blocks):
        heights = jax.random.uniform(jax.random.fold_in(jax.random.fold_in(stream_key, 6), dim), (blocks,), jnp.float32, smallest / len(shards), high / len(shards))
        return jnp.repeat(jnp.exp(heights), extent[dim] // blocks).reshape((-1,) + (1,) * (len(extent) - dim - 1))

    factor_of = one(*shards[0])
    for cut in shards[1:]:
        factor_of = factor_of * one(*cut)
    return factor_of


def normal_values(rng, extent, deviation, bound, pieces=(), kind=jnp.bfloat16):
    entries = jax.random.normal(rng, extent, jnp.float32) * deviation
    if len(pieces) > 0:
        entries = block_levels(rng, extent, pieces, -0.22, 0.18) * entries
    return jnp.clip(entries, min=-bound, max=bound).astype(kind)


def setup_inputs(seed: int = 0) -> dict:
    seeds = jax.random.split(jax.random.key(seed), 13)
    return {
        "source_emb": normal_values(seeds[0], (DIM, ENTITIES), 0.3, 2.5, ((1, 512),), jnp.float32),
        "source_state": jnp.clip(jnp.exp(math.log(0.1) - 2.9957323 * jax.random.uniform(seeds[1], (ENTITIES,), jnp.float32) ** block_levels(seeds[1], (ENTITIES,), ((0, 512),), -0.2, 0.2)), 0.005, 0.1),
        "dest_emb": normal_values(seeds[2], (DIM, ENTITIES), 0.3, 2.5, ((1, 512),), jnp.float32),
        "dest_state": jnp.clip(jnp.exp(math.log(0.1) - 2.9957323 * jax.random.uniform(seeds[3], (ENTITIES,), jnp.float32) ** block_levels(seeds[3], (ENTITIES,), ((0, 512),), -0.2, 0.2)), 0.005, 0.1),
        "relations": normal_values(seeds[4], (DIM, NREL), 0.8, 4.0, (), jnp.float32),
        "relation_state": jnp.clip(jnp.exp(jax.random.uniform(seeds[5], (NREL,), jnp.float32, math.log(1.0), math.log(30.0))), 1.0, 30.0),
        "partner": draw_partner(jax.random.fold_in(seeds[12], 71), 0),
        "edge_count": draw_edge_count(jax.random.fold_in(seeds[12], 71), 0),
        "source_rows": place_ends(jax.random.randint(seeds[8], (DOMAINS, GROUPS, EDGES), 0, BLOCK), jax.random.fold_in(seeds[8], 1), 0, BLOCK - 1).astype(jnp.int32),
        "target_rows": place_ends(jax.random.randint(seeds[9], (DOMAINS, GROUPS, EDGES), 0, BLOCK), jax.random.fold_in(seeds[9], 1), 0, BLOCK - 1).astype(jnp.int32),
        "relation_index": place_ends(jax.random.randint(seeds[10], (DOMAINS, GROUPS, EDGES), 0, NREL), jax.random.fold_in(seeds[10], 1), 0, NREL - 1).astype(jnp.int32),
        "negative_rows": place_ends(jax.random.randint(seeds[11], (DOMAINS, GROUPS, SPANS * NEG), 0, BLOCK), jax.random.fold_in(seeds[11], 1), 0, BLOCK - 1).astype(jnp.int32),
    }


learn_rate = 0.3
epsilon = 1e-08

def adagrad(param, state, grad):
    new_state = state + lax.optimization_barrier(jnp.mean(grad * grad, axis=0))
    return (param - learn_rate * grad / (jnp.sqrt(new_state) + epsilon), new_state)

def train_block(source, source_acc, target, target_acc, relation_bf, rows_s, rows_t, rows_r, rows_n, live):
    source_bf = source.astype(jnp.bfloat16)
    target_bf = target.astype(jnp.bfloat16)
    subject = source_bf[:, rows_s].astype(jnp.float32)
    operator = relation_bf[:, rows_r].astype(jnp.float32)
    objects = target_bf[:, rows_t].astype(jnp.float32)
    noise = target_bf[:, rows_n]
    subject_re, subject_im = (subject[:HALF], subject[HALF:])
    operator_re, operator_im = (operator[:HALF], operator[HALF:])
    query = jnp.concatenate([subject_re * operator_re - subject_im * operator_im, subject_re * operator_im + subject_im * operator_re], 0)
    positive = lax.optimization_barrier(jnp.sum(query * objects, axis=0))
    query_bf = query.astype(jnp.bfloat16)
    negative = jnp.dot(query_bf.T, noise, preferred_element_type=jnp.float32)
    grad_pos = -jax.nn.sigmoid(-positive) * live
    grad_neg = (jax.nn.sigmoid(negative) * (live[:, None] / NEG)).astype(jnp.bfloat16)
    grad_query = grad_pos[None, :] * objects + jnp.dot(noise, grad_neg.T, preferred_element_type=jnp.float32)
    grad_objects = grad_pos[None, :] * query
    grad_noise = jnp.dot(query_bf, grad_neg, preferred_element_type=jnp.float32)
    query_gre, query_gim = (grad_query[:HALF], grad_query[HALF:])
    grad_subject = jnp.concatenate([query_gre * operator_re + query_gim * operator_im, query_gim * operator_re - query_gre * operator_im], 0)
    grad_operator = jnp.concatenate([query_gre * subject_re + query_gim * subject_im, query_gim * subject_re - query_gre * subject_im], 0)
    grad_source = jnp.zeros_like(source).at[:, rows_s].add(grad_subject.astype(jnp.bfloat16).astype(jnp.float32))
    grad_target = jnp.zeros_like(target).at[:, rows_t].add(grad_objects.astype(jnp.bfloat16).astype(jnp.float32))
    grad_target = grad_target.at[:, rows_n].add(grad_noise.astype(jnp.bfloat16).astype(jnp.float32))
    grad_local = jnp.zeros((DIM, NREL), jnp.float32).at[:, rows_r].add(grad_operator.astype(jnp.bfloat16).astype(jnp.float32))
    new_source, new_source_acc = adagrad(source, source_acc, grad_source)
    new_target, new_target_acc = adagrad(target, target_acc, grad_target)
    return (new_source, new_source_acc, new_target, new_target_acc, grad_local)

def reference(source_emb, source_state, dest_emb, dest_state, relations, relation_state, partner, edge_count, source_rows, target_rows, relation_index, negative_rows):
    devices_all = DOMAINS * GROUPS

    def split_blocks(table):
        return table.reshape(DIM, devices_all, BLOCK).transpose(1, 0, 2)

    def join_blocks(stack):
        return stack.transpose(1, 0, 2).reshape(DIM, devices_all * BLOCK)
    group_prior = (jnp.arange(GROUPS, dtype=jnp.int32)[None, :] + GROUPS - 1) % GROUPS
    owner = (partner * GROUPS + group_prior).reshape(-1).astype(jnp.int32)
    sources = split_blocks(source_emb)
    source_accs = source_state.reshape(devices_all, BLOCK)
    targets = split_blocks(dest_emb)[owner]
    target_accs = dest_state.reshape(devices_all, BLOCK)[owner]
    all_source = source_rows.reshape(devices_all, EDGES)
    all_target = target_rows.reshape(devices_all, EDGES)
    all_relation = relation_index.reshape(devices_all, EDGES)
    all_negative = negative_rows.reshape(devices_all, SPANS * NEG)
    live_all = (jnp.arange(EDGES, dtype=jnp.int32)[None, :] < edge_count.reshape(devices_all, 1)).astype(jnp.float32)
    for step in range(SPANS):
        first = step * SPAN
        first_neg = step * NEG
        relation_bf = relations.astype(jnp.bfloat16)

        def per_device(total, inputs):
            source, source_acc, target, target_acc, rows_s, rows_t, rows_r, rows_n, live = inputs
            outcome = train_block(source, source_acc, target, target_acc, relation_bf, rows_s, rows_t, rows_r, rows_n, live)
            return (total + outcome[4], outcome[:4])
        inputs = (sources, source_accs, targets, target_accs, all_source[:, first:first + SPAN], all_target[:, first:first + SPAN], all_relation[:, first:first + SPAN], all_negative[:, first_neg:first_neg + NEG], live_all[:, first:first + SPAN])
        total, (sources, source_accs, targets, target_accs) = lax.scan(per_device, jnp.zeros((DIM, NREL), jnp.float32), inputs)
        relations, relation_state = adagrad(relations, relation_state, total)
    placed = jnp.zeros((devices_all, DIM, BLOCK), jnp.float32).at[owner].set(targets)
    placed_acc = jnp.zeros((devices_all, BLOCK), jnp.float32).at[owner].set(target_accs)
    return (join_blocks(sources), source_accs.reshape(-1), join_blocks(placed), placed_acc.reshape(-1), relations, relation_state)
```

```python
import jax
import jax.numpy as jnp
from jax import lax
from jax.experimental import pallas as pl
from jax.experimental.pallas import tpu as pltpu
from jax.sharding import Mesh
from jax.sharding import PartitionSpec as P

SPAN = 512
SPANS = 2
NEG = 1024
EDGES = 1024

ALL = ("z", "y", "core", "x")
DOM = ("z", "y", "core")

learn_rate = 0.3
epsilon = 1e-08


def passed_along(value, axis, steps):
    count = lax.axis_size(axis)
    pairs = [(source, (source + steps) % count) for source in range(count)]
    return lax.ppermute(value, axis, pairs)


def exchange(value, axis):
    return lax.all_to_all(value, axis, split_axis=0, concat_axis=0, tiled=True)


def gathered(value, axis):
    count = lax.axis_size(axis)
    return exchange(jnp.broadcast_to(value[None], (count,) + value.shape), axis)


def pick_body(index_ref, from_ref, to_ref):
    def one(i, _):
        to_ref[i] = from_ref[index_ref[i]]
        return 0

    lax.fori_loop(0, to_ref.shape[0], one, 0, unroll=8)


def place_body(index_ref, from_ref, to_ref):
    def one(i, _):
        to_ref[index_ref[i]] = from_ref[i]
        return 0

    lax.fori_loop(0, to_ref.shape[0], one, 0, unroll=8)


def rearranged(body, value, index):
    return pl.pallas_call(
        body,
        out_shape=jax.ShapeDtypeStruct(value.shape, value.dtype),
        in_specs=[
            pl.BlockSpec(memory_space=pltpu.SMEM),
            pl.BlockSpec(memory_space=pltpu.VMEM),
        ],
        out_specs=pl.BlockSpec(memory_space=pltpu.VMEM),
    )(index, value)


def adagrad(param, state, grad):
    new_state = state + jnp.mean(grad * grad, axis=0)
    return (param - learn_rate * grad / (jnp.sqrt(new_state) + epsilon), new_state)


def contract_last(left, right):
    return lax.dot_general(
        left, right, (((1,), (1,)), ((), ())), preferred_element_type=jnp.float32
    )


def selector(count, rows):
    return (jnp.arange(count, dtype=jnp.int32)[:, None] == rows[None, :]).astype(jnp.bfloat16)


def train_block(
    source, source_acc, target, target_acc, relation_bf, rows_s, rows_t, rows_r, rows_n, live
):
    half = source.shape[0] // 2
    block = source.shape[1]
    pick_source = selector(block, rows_s)
    pick_target = selector(block, rows_t)
    pick_relation = selector(relation_bf.shape[1], rows_r)
    count = jnp.sum(
        (jnp.arange(block, dtype=jnp.int32)[:, None] == rows_n[None, :]).astype(jnp.float32), axis=1
    )
    source_bf = source.astype(jnp.bfloat16)
    target_bf = target.astype(jnp.bfloat16)
    subject = jnp.dot(source_bf, pick_source, preferred_element_type=jnp.float32)
    operator = jnp.dot(relation_bf, pick_relation, preferred_element_type=jnp.float32)
    objects = jnp.dot(target_bf, pick_target, preferred_element_type=jnp.float32)
    subject_re, subject_im = (subject[:half], subject[half:])
    operator_re, operator_im = (operator[:half], operator[half:])
    query = jnp.concatenate(
        [
            subject_re * operator_re - subject_im * operator_im,
            subject_re * operator_im + subject_im * operator_re,
        ],
        0,
    )
    positive = jnp.sum(query * objects, axis=0)
    query_bf = query.astype(jnp.bfloat16)
    score = lax.dot_general(
        target_bf, query_bf, (((0,), (0,)), ((), ())), preferred_element_type=jnp.float32
    )
    grad_pos = -jax.nn.sigmoid(-positive) * live
    slope = lax.reduce_precision(jax.nn.sigmoid(score) * (live[None, :] / NEG), 8, 7)
    slope = slope.astype(jnp.bfloat16)
    weighted = lax.reduce_precision(slope.astype(jnp.float32), 8, 7) * count[:, None]
    upper = weighted.astype(jnp.bfloat16)
    lower = (weighted - upper.astype(jnp.float32)).astype(jnp.bfloat16)
    twice = jnp.concatenate([target_bf, target_bf], 1)
    grad_query = grad_pos[None, :] * objects + jnp.dot(
        twice, jnp.concatenate([upper, lower], 0), preferred_element_type=jnp.float32
    )
    grad_objects = grad_pos[None, :] * query
    grad_noise = contract_last(query_bf, slope)
    query_gre, query_gim = (grad_query[:half], grad_query[half:])
    grad_subject = jnp.concatenate(
        [
            query_gre * operator_re + query_gim * operator_im,
            query_gim * operator_re - query_gre * operator_im,
        ],
        0,
    )
    grad_operator = jnp.concatenate(
        [
            query_gre * subject_re + query_gim * subject_im,
            query_gim * subject_re - query_gre * subject_im,
        ],
        0,
    )
    grad_source = contract_last(grad_subject.astype(jnp.bfloat16), pick_source)
    grad_target = contract_last(grad_objects.astype(jnp.bfloat16), pick_target)
    grad_target = grad_target + lax.reduce_precision(grad_noise, 8, 7) * count[None, :]
    grad_local = contract_last(grad_operator.astype(jnp.bfloat16), pick_relation)
    new_source, new_source_acc = adagrad(source, source_acc, grad_source)
    new_target, new_target_acc = adagrad(target, target_acc, grad_target)
    return (new_source, new_source_acc, new_target, new_target_acc, grad_local)


def summed(grad):
    width, count = grad.shape
    lanes = 128
    chunks = count // lanes
    n_core, n_x, n_y = (lax.axis_size("core"), lax.axis_size("x"), lax.axis_size("y"))
    parts = n_core * n_x * n_y
    rows = -(-(width * chunks) // (parts * 8)) * 8
    flat = jnp.concatenate([grad[:, k * lanes : (k + 1) * lanes] for k in range(chunks)], 0)
    flat = jnp.pad(flat, ((0, parts * rows - width * chunks), (0, 0)))
    mine = lax.axis_index("core")
    flat = flat.reshape(n_core, n_x * n_y * rows, lanes)
    keep = lax.dynamic_index_in_dim(flat, mine, 0, keepdims=False)
    give = lax.dynamic_index_in_dim(flat, 1 - mine, 0, keepdims=False)
    part = keep + passed_along(give, "core", 1)
    part = jnp.sum(exchange(part.reshape(n_x, n_y * rows, lanes), "x"), 0)
    part = jnp.sum(exchange(part.reshape(n_y, rows, lanes), "y"), 0)
    part = jnp.sum(gathered(part, "z"), 0)
    part = gathered(part, "y").reshape(n_y * rows, lanes)
    part = gathered(part, "x").reshape(n_x * n_y * rows, lanes)
    other = passed_along(part, "core", 1)
    first = jnp.where(mine == 0, part, other)
    second = jnp.where(mine == 0, other, part)
    flat = jnp.concatenate([first, second], 0)
    return jnp.concatenate([flat[k * width : (k + 1) * width] for k in range(chunks)], 1)


def local(
    source_emb,
    source_state,
    dest_emb,
    dest_state,
    relations,
    relation_state,
    partner,
    edge_count,
    source_rows,
    target_rows,
    relation_index,
    negative_rows,
):
    width = source_emb.shape[0]
    block = source_emb.shape[1]
    members = block
    padded = 512
    arriving = passed_along(dest_emb, "x", 1)
    arriving_acc = passed_along(dest_state, "x", 1)
    own = jnp.broadcast_to(partner.reshape(1, 1).astype(jnp.float32), (members, 1))
    cargo = jnp.concatenate([arriving.T, arriving_acc[:, None], own], 1)
    cargo = jnp.pad(cargo, ((0, 0), (0, padded - width - 2))).reshape(members, padded // 128, 128)
    spread = exchange(cargo, DOM)
    partners = spread.reshape(members, padded)[:, width + 1].astype(jnp.int32)
    partners = jnp.clip(partners, 0, members - 1)
    spread = rearranged(pick_body, spread, partners)
    arrived = exchange(spread, DOM).reshape(members, padded)
    target = arrived[:, :width].T
    target_acc = arrived[:, width]
    source = source_emb
    source_acc = source_state
    live_all = (jnp.arange(EDGES, dtype=jnp.int32) < edge_count[0, 0]).astype(jnp.float32)
    for step in range(SPANS):
        first = step * SPAN
        first_neg = step * NEG
        relation_bf = relations.astype(jnp.bfloat16)
        source, source_acc, target, target_acc, grad_local = train_block(
            source,
            source_acc,
            target,
            target_acc,
            relation_bf,
            source_rows[0, 0, first : first + SPAN],
            target_rows[0, 0, first : first + SPAN],
            relation_index[0, 0, first : first + SPAN],
            negative_rows[0, 0, first_neg : first_neg + NEG],
            live_all[first : first + SPAN],
        )
        relations, relation_state = adagrad(relations, relation_state, summed(grad_local))
    cargo = jnp.concatenate([target.T, target_acc[:, None]], 1)
    cargo = jnp.pad(cargo, ((0, 0), (0, padded - width - 1))).reshape(members, padded // 128, 128)
    collected = exchange(cargo, DOM)
    collected = rearranged(place_body, collected, partners)
    returned = exchange(collected, DOM).reshape(members, padded)
    settled = passed_along(returned[:, :width].T, "x", -1)
    settled_acc = passed_along(returned[:, width], "x", -1)
    return (source, source_acc, settled, settled_acc, relations, relation_state)


def solution(mesh):
    fine = Mesh(mesh.devices.reshape(8, 8, 2, 4), ALL)
    in_specs = (
        P(None, ALL),
        P(ALL),
        P(None, ALL),
        P(ALL),
        P(),
        P(),
        P(DOM, "x"),
        P(DOM, "x"),
        P(DOM, "x", None),
        P(DOM, "x", None),
        P(DOM, "x", None),
        P(DOM, "x", None),
    )
    out_specs = (P(None, ALL), P(ALL), P(None, ALL), P(ALL), P(), P())
    return jax.shard_map(local, mesh=fine, in_specs=in_specs, out_specs=out_specs, check_vma=False)
```

```python
import jax
import jax.numpy as jnp
from jax import lax
from jax.experimental import pallas as pl
from jax.experimental.pallas import tpu as pltpu
from jax.sharding import Mesh
from jax.sharding import PartitionSpec as P

DIM = 400
HALF = 200
NREL = 768
BLOCK = 128
SPAN = 512
NEG = 1024
LANES = 128
CHUNKS = NREL // LANES
FLAT = 2560
HALF_FLAT = FLAT // 2
PIECE = 4

ALL = ("z", "y", "core", "x")
DOM = ("z", "y", "core")

learn_rate = 0.3
epsilon = 1e-08

f32 = jnp.float32
bf16 = jnp.bfloat16


def passed_along(value, axis, steps):
    count = lax.axis_size(axis)
    pairs = [(source, (source + steps) % count) for source in range(count)]
    return lax.ppermute(value, axis, pairs)


def exchange(value, axis):
    return lax.all_to_all(value, axis, split_axis=0, concat_axis=0, tiled=True)


def dealt(value, axis, count):
    rows, lanes = value.shape
    return exchange(value.reshape(count, rows // count, lanes), axis).reshape(rows, lanes)


def gathered(value, axis):
    count = lax.axis_size(axis)
    return exchange(jnp.broadcast_to(value[None], (count,) + value.shape), axis)


def kernel_call(body, outs, args, scratch=(), scalars=0):
    specs = [pl.BlockSpec(memory_space=pltpu.SMEM)] * scalars
    specs += [pl.BlockSpec(memory_space=pltpu.VMEM)] * (len(args) - scalars)
    return pl.pallas_call(
        body,
        out_shape=[jax.ShapeDtypeStruct(shape, dtype) for shape, dtype in outs],
        in_specs=specs,
        out_specs=[pl.BlockSpec(memory_space=pltpu.VMEM)] * len(outs),
        scratch_shapes=[pltpu.VMEM(shape, dtype) for shape, dtype in scratch],
        compiler_params=pltpu.CompilerParams(vmem_limit_bytes=40 * 2**20),
    )(*args)


def dot(left, right):
    return lax.dot_general(left, right, (((1,), (0,)), ((), ())), preferred_element_type=f32)


def dot_last(left, right):
    return lax.dot_general(left, right, (((1,), (1,)), ((), ())), preferred_element_type=f32)


def moved(pick, value):
    upper = value.astype(bf16)
    rest = value - upper.astype(f32)
    middle = rest.astype(bf16)
    lower = (rest - middle.astype(f32)).astype(bf16)
    return (dot(pick, upper) + dot(pick, middle)) + dot(pick, lower)


def one_hot(count, rows):
    hit = lax.broadcasted_iota(jnp.int32, (count, rows.shape[1]), 0) == rows
    return jnp.where(hit, 1.0, 0.0).astype(bf16)


def sigmoid(value):
    return 1.0 / (1.0 + jnp.exp(-value))


def stepped(param, state, grad):
    new_state = state + jnp.sum(grad * grad, axis=0, keepdims=True) * (1.0 / DIM)
    return (param - learn_rate * grad / (jnp.sqrt(new_state) + epsilon), new_state)


def spaced(start, size, stride):
    return pl.ds(start, size, stride=stride)


def pack_body(partner_ref, arriving_ref, state_ref, out_ref):
    for k in range(PIECE - 1):
        out_ref[spaced(k, BLOCK, PIECE), :] = arriving_ref[LANES * k : LANES * (k + 1), :].T
    tail = arriving_ref[LANES * (PIECE - 1) : DIM, :]
    state = jnp.broadcast_to(state_ref[...], (8, LANES))
    own = jnp.full((8, LANES), partner_ref[0, 0].astype(f32))
    zero = jnp.zeros((LANES - tail.shape[0] - 16, LANES), f32)
    out_ref[spaced(PIECE - 1, BLOCK, PIECE), :] = jnp.concatenate([tail, state, own, zero], 0).T


STATE_LANE = DIM - LANES * (PIECE - 1)
OWN_LANE = STATE_LANE + 8


def partner_pick(last):
    own = last[:, OWN_LANE : OWN_LANE + 1].astype(jnp.int32)
    lane = lax.broadcasted_iota(jnp.int32, (BLOCK, BLOCK), 1)
    return jnp.where(lane == own, 1.0, 0.0)


def pick_body(spread_ref, out_ref):
    last = spread_ref[spaced(PIECE - 1, BLOCK, PIECE), :]
    pick = partner_pick(last).astype(bf16)
    for k in range(PIECE - 1):
        rows = spaced(k, BLOCK, PIECE)
        out_ref[rows, :] = moved(pick, spread_ref[rows, :])
    out_ref[spaced(PIECE - 1, BLOCK, PIECE), :] = moved(pick, last)


def train(
    first,
    live_count,
    source,
    source_state,
    target,
    target_state,
    relation_bf,
    rows_s,
    rows_t,
    rows_r,
    rows_n,
    subject_ref,
    operator_ref,
    objects_ref,
    query_ref,
    slope_ref,
    flat_ref,
):
    pick_s = one_hot(BLOCK, rows_s)
    pick_t = one_hot(BLOCK, rows_t)
    pick_r = one_hot(NREL, rows_r)
    hits = lax.broadcasted_iota(jnp.int32, (BLOCK, NEG), 0) == rows_n
    count = jnp.sum(jnp.where(hits, 1.0, 0.0), axis=1, keepdims=True)
    count_row = jnp.broadcast_to(count, (BLOCK, BLOCK)).T[0:1, :]
    edge = lax.broadcasted_iota(jnp.int32, (1, SPAN), 1) + first
    live = jnp.where(edge < live_count, 1.0, 0.0)
    target_bf = target.astype(bf16)
    subject_ref[...] = dot(source.astype(bf16), pick_s)
    operator_ref[...] = dot(relation_bf, pick_r)
    objects_ref[...] = dot(target_bf, pick_t)

    def form(i, total):
        re = pl.ds(pl.multiple_of(8 * i, 8), 8)
        im = pl.ds(pl.multiple_of(HALF + 8 * i, 8), 8)
        subject_re, subject_im = (subject_ref[re, :], subject_ref[im, :])
        operator_re, operator_im = (operator_ref[re, :], operator_ref[im, :])
        query_re = subject_re * operator_re - subject_im * operator_im
        query_im = subject_re * operator_im + subject_im * operator_re
        query_ref[re, :] = query_re
        query_ref[im, :] = query_im
        return total + query_re * objects_ref[re, :] + query_im * objects_ref[im, :]

    total = lax.fori_loop(0, HALF // 8, form, jnp.zeros((8, SPAN), f32), unroll=5)
    positive = jnp.sum(total, axis=0, keepdims=True)
    query_bf = query_ref[...].astype(bf16)
    score = dot(target.T.astype(bf16), query_bf)
    grad_pos = -sigmoid(-positive) * live
    slope = (sigmoid(score) * (live * (1.0 / NEG))).astype(bf16)
    weighted = slope.astype(f32) * count
    upper = weighted.astype(bf16)
    lower = (weighted - upper.astype(f32)).astype(bf16)
    slope_ref[...] = dot(target_bf, upper) + dot(target_bf, lower)
    grad_noise = dot_last(query_bf, slope)

    def push(i, _):
        re = pl.ds(pl.multiple_of(8 * i, 8), 8)
        im = pl.ds(pl.multiple_of(HALF + 8 * i, 8), 8)
        query_gre = grad_pos * objects_ref[re, :] + slope_ref[re, :]
        query_gim = grad_pos * objects_ref[im, :] + slope_ref[im, :]
        subject_re, subject_im = (subject_ref[re, :], subject_ref[im, :])
        operator_re, operator_im = (operator_ref[re, :], operator_ref[im, :])
        subject_ref[re, :] = query_gre * operator_re + query_gim * operator_im
        subject_ref[im, :] = query_gim * operator_re - query_gre * operator_im
        operator_ref[re, :] = query_gre * subject_re + query_gim * subject_im
        operator_ref[im, :] = query_gim * subject_re - query_gre * subject_im
        query_ref[re, :] = grad_pos * query_ref[re, :]
        query_ref[im, :] = grad_pos * query_ref[im, :]
        return 0

    lax.fori_loop(0, HALF // 8, push, 0, unroll=5)
    grad_operator = operator_ref[...].astype(bf16)
    for k in range(0, CHUNKS, 2):
        pair = dot_last(grad_operator, pick_r[LANES * k : LANES * (k + 2), :])
        flat_ref[DIM * k : DIM * (k + 1), :] = pair[:, :LANES]
        flat_ref[DIM * (k + 1) : DIM * (k + 2), :] = pair[:, LANES:]
    flat_ref[DIM * CHUNKS : FLAT, :] = jnp.zeros((FLAT - DIM * CHUNKS, LANES), f32)
    grad_source = dot_last(subject_ref[...].astype(bf16), pick_s)
    grad_target = dot_last(query_ref[...].astype(bf16), pick_t)
    grad_target = grad_target + grad_noise.astype(bf16).astype(f32) * count_row
    source, source_state = stepped(source, source_state, grad_source)
    target, target_state = stepped(target, target_state, grad_target)
    return source, source_state, target, target_state


TRAIN_SCRATCH = [((DIM, SPAN), f32)] * 5 + [((FLAT, LANES), f32)]


def halves(mine, flat_ref, keep_ref, give_ref):
    keep_ref[0:HALF_FLAT, :] = flat_ref[pl.ds(pl.multiple_of(mine * HALF_FLAT, 8), HALF_FLAT), :]
    give_ref[0:HALF_FLAT, :] = flat_ref[
        pl.ds(pl.multiple_of((1 - mine) * HALF_FLAT, 8), HALF_FLAT), :
    ]


def first_body(
    mine_ref,
    live_ref,
    arrived_ref,
    source_ref,
    source_state_ref,
    relations_ref,
    rows_s_ref,
    rows_t_ref,
    rows_r_ref,
    rows_n_ref,
    source_out,
    source_state_out,
    target_out,
    target_state_out,
    keep_out,
    give_out,
    subject_ref,
    operator_ref,
    objects_ref,
    query_ref,
    slope_ref,
    flat_ref,
):
    last = arrived_ref[spaced(PIECE - 1, BLOCK, PIECE), :].T
    target = jnp.concatenate(
        [arrived_ref[spaced(k, BLOCK, PIECE), :].T for k in range(PIECE - 1)] + [last[:STATE_LANE, :]], 0
    )
    source, source_state, target, target_state = train(
        0,
        live_ref[0, 0],
        source_ref[...],
        source_state_ref[...],
        target,
        last[STATE_LANE : STATE_LANE + 1, :],
        relations_ref[...].astype(bf16),
        rows_s_ref[:, 0:SPAN],
        rows_t_ref[:, 0:SPAN],
        rows_r_ref[:, 0:SPAN],
        rows_n_ref[:, 0:NEG],
        subject_ref,
        operator_ref,
        objects_ref,
        query_ref,
        slope_ref,
        flat_ref,
    )
    source_out[...] = source
    source_state_out[...] = source_state
    target_out[...] = target
    target_state_out[...] = target_state
    halves(mine_ref[0, 0], flat_ref, keep_out, give_out)


def relation_update(mine, part_ref, other_ref, relations_ref, state_ref, out, state_out, flat_ref):
    flat_ref[pl.ds(pl.multiple_of(mine * HALF_FLAT, 8), HALF_FLAT), :] = part_ref[...]
    flat_ref[pl.ds(pl.multiple_of((1 - mine) * HALF_FLAT, 8), HALF_FLAT), :] = other_ref[...]
    for k in range(CHUNKS):
        lanes = slice(LANES * k, LANES * (k + 1))
        grad = flat_ref[DIM * k : DIM * (k + 1), :]
        new, new_state = stepped(relations_ref[:, lanes], state_ref[:, lanes], grad)
        out[:, lanes] = new
        state_out[:, lanes] = new_state


def second_body(
    mine_ref,
    live_ref,
    partner_ref,
    part_ref,
    other_ref,
    source_ref,
    source_state_ref,
    target_ref,
    target_state_ref,
    relations_ref,
    relation_state_ref,
    rows_s_ref,
    rows_t_ref,
    rows_r_ref,
    rows_n_ref,
    source_out,
    source_state_out,
    relations_out,
    relation_state_out,
    keep_out,
    give_out,
    subject_ref,
    operator_ref,
    objects_ref,
    query_ref,
    slope_ref,
    flat_ref,
    turned_ref,
):
    mine = mine_ref[0, 0]
    relation_update(
        mine,
        part_ref,
        other_ref,
        relations_ref,
        relation_state_ref,
        relations_out,
        relation_state_out,
        flat_ref,
    )
    source, source_state, target, target_state = train(
        SPAN,
        live_ref[0, 0],
        source_ref[...],
        source_state_ref[...],
        target_ref[...],
        target_state_ref[...],
        relations_out[...].astype(bf16),
        rows_s_ref[:, SPAN : 2 * SPAN],
        rows_t_ref[:, SPAN : 2 * SPAN],
        rows_r_ref[:, SPAN : 2 * SPAN],
        rows_n_ref[:, NEG : 2 * NEG],
        subject_ref,
        operator_ref,
        objects_ref,
        query_ref,
        slope_ref,
        flat_ref,
    )
    source_out[...] = source
    source_state_out[...] = source_state
    halves(mine, flat_ref, keep_out, give_out)
    for k in range(PIECE):
        if k < PIECE - 1:
            turned_ref[...] = target[LANES * k : LANES * (k + 1), :].T
        else:
            state = jnp.broadcast_to(target_state, (8, LANES))
            own = jnp.full((8, LANES), partner_ref[0, 0].astype(f32))
            zero = jnp.zeros((LANES - STATE_LANE - 16, LANES), f32)
            turned_ref[...] = jnp.concatenate([target[LANES * k : DIM, :], state, own, zero], 0).T
        rows = slice(HALF_FLAT + 64 * k, HALF_FLAT + 64 * (k + 1))
        keep_out[rows, :] = turned_ref[pl.ds(mine, 64, stride=2), :]
        give_out[rows, :] = turned_ref[pl.ds(1 - mine, 64, stride=2), :]


ROWS = 16
SUM_ROW = 8
SUM_ROWS = 5


def join_body(keep_ref, got_ref, sums_ref, block_ref):
    sums_ref[...] = keep_ref[0:HALF_FLAT, :] + got_ref[0:HALF_FLAT, :]
    block_ref[0 : 64 * PIECE, :] = keep_ref[HALF_FLAT:, :]
    block_ref[64 * PIECE :, :] = got_ref[HALF_FLAT:, :]


def merge_body(received_ref, block_ref, out_ref):
    for k in range(2 * PIECE):
        out_ref[spaced(k, 64, ROWS), :] = block_ref[64 * k : 64 * (k + 1), :]
    for k in range(SUM_ROWS):
        rows = slice(64 * k, 64 * (k + 1))
        total = received_ref[0, rows, :] + received_ref[1, rows, :]
        total = total + received_ref[2, rows, :] + received_ref[3, rows, :]
        out_ref[spaced(SUM_ROW + k, 64, ROWS), :] = total
    for k in range(SUM_ROW + SUM_ROWS, ROWS):
        out_ref[spaced(k, 64, ROWS), :] = jnp.zeros((64, LANES), f32)


def middle_body(mine_ref, received_ref, out_ref, turned_ref):
    mine = mine_ref[0, 0]
    here, there = (spaced(mine, 64, 2), spaced(1 - mine, 64, 2))
    back = None
    for k in reversed(range(PIECE)):
        turned_ref[here, :] = received_ref[spaced(k, 64, ROWS), :]
        turned_ref[there, :] = received_ref[spaced(PIECE + k, 64, ROWS), :]
        if back is None:
            back = partner_pick(turned_ref[...]).T.astype(bf16)
        turned_ref[...] = moved(back, turned_ref[...])
        out_ref[spaced(k, 64, ROWS), :] = turned_ref[here, :]
        out_ref[spaced(PIECE + k, 64, ROWS), :] = turned_ref[there, :]
    total = received_ref[SUM_ROW:ROWS, :]
    for q in range(1, 64):
        total = total + received_ref[ROWS * q + SUM_ROW : ROWS * (q + 1), :]
    for q in range(64):
        out_ref[ROWS * q + SUM_ROW : ROWS * (q + 1), :] = total


def parting_body(received_ref, sums_ref, block_ref):
    for k in range(2 * PIECE):
        block_ref[64 * k : 64 * (k + 1), :] = received_ref[spaced(k, 64, ROWS), :]
    for k in range(SUM_ROWS):
        rows = received_ref[spaced(SUM_ROW + k, 64, ROWS), :]
        for x in range(4):
            sums_ref[x, 64 * k : 64 * (k + 1), :] = rows


def settle_body(mine_ref, block_ref, other_ref, out_ref, state_out, turned_ref):
    mine = mine_ref[0, 0]
    for k in range(PIECE):
        rows = slice(64 * k, 64 * (k + 1))
        turned_ref[pl.ds(mine, 64, stride=2), :] = block_ref[rows, :]
        turned_ref[pl.ds(1 - mine, 64, stride=2), :] = other_ref[rows, :]
        turned = turned_ref[...].T
        if k < PIECE - 1:
            out_ref[LANES * k : LANES * (k + 1), :] = turned
        else:
            out_ref[LANES * k : DIM, :] = turned[:STATE_LANE, :]
            state_out[...] = turned[STATE_LANE : STATE_LANE + 1, :]


def final_body(
    mine_ref, part_ref, other_ref, relations_ref, state_ref, out_ref, state_out, flat_ref
):
    relation_update(
        mine_ref[0, 0], part_ref, other_ref, relations_ref, state_ref, out_ref, state_out, flat_ref
    )


def local(
    source_emb,
    source_state,
    dest_emb,
    dest_state,
    relations,
    relation_state,
    partner,
    edge_count,
    source_rows,
    target_rows,
    relation_index,
    negative_rows,
):
    mine = lax.axis_index("core").astype(jnp.int32).reshape(1, 1)
    turned = ((BLOCK, LANES), f32)
    arriving = passed_along(dest_emb, "x", 1)
    arriving_state = passed_along(dest_state.reshape(1, BLOCK), "x", 1)
    tile = ((BLOCK * PIECE, LANES), f32)
    (cargo,) = kernel_call(pack_body, [tile], [partner, arriving, arriving_state], scalars=1)
    spread = dealt(cargo, DOM, BLOCK)
    (spread,) = kernel_call(pick_body, [tile], [spread])
    arrived = dealt(spread, DOM, BLOCK)
    lists = [
        rows.reshape(1, -1) for rows in (source_rows, target_rows, relation_index, negative_rows)
    ]
    block = ((DIM, BLOCK), f32)
    line = ((1, BLOCK), f32)
    half = ((HALF_FLAT, LANES), f32)
    source, source_acc, target, target_acc, keep, give = kernel_call(
        first_body,
        [block, line, block, line, half, half],
        [mine, edge_count, arrived, source_emb, source_state.reshape(1, -1), relations] + lists,
        TRAIN_SCRATCH,
        scalars=2,
    )
    part = keep + passed_along(give, "core", 1)
    part = jnp.sum(exchange(part.reshape(4, 320, LANES), "x"), 0)
    part = jnp.sum(exchange(part.reshape(8, 40, LANES), "y"), 0)
    part = jnp.sum(gathered(part, "z"), 0)
    part = gathered(part, "y").reshape(320, LANES)
    part = gathered(part, "x").reshape(HALF_FLAT, LANES)
    other = passed_along(part, "core", 1)
    table = ((DIM, NREL), f32)
    types = ((1, NREL), f32)
    longer = ((HALF_FLAT + 64 * PIECE, LANES), f32)
    source, source_acc, relations, relation_acc, keep, give = kernel_call(
        second_body,
        [block, line, table, types, longer, longer],
        [mine, edge_count, partner, part, other, source, source_acc, target, target_acc, relations]
        + [relation_state.reshape(1, -1)]
        + lists,
        TRAIN_SCRATCH + [turned],
        scalars=3,
    )
    got = passed_along(give, "core", 1)
    part, leaving = kernel_call(join_body, [half, ((128 * PIECE, LANES), f32)], [keep, got])
    leaving = passed_along(leaving, "x", -1)
    received = exchange(part.reshape(4, 320, LANES), "x")
    packet = ((64 * ROWS, LANES), f32)
    (packed,) = kernel_call(merge_body, [packet], [received, leaving])
    packed = dealt(packed, ("z", "y"), 64)
    (packed,) = kernel_call(middle_body, [packet], [mine, packed], [turned], scalars=1)
    packed = dealt(packed, ("z", "y"), 64)
    sums, returned = kernel_call(
        parting_body, [((4, 320, LANES), f32), ((128 * PIECE, LANES), f32)], [packed]
    )
    sibling = passed_along(returned[64 * PIECE :], "core", 1)
    part = exchange(sums, "x").reshape(HALF_FLAT, LANES)
    other = passed_along(part, "core", 1)
    settled, settled_acc = kernel_call(
        settle_body, [block, line], [mine, returned, sibling], [turned], scalars=1
    )
    relations, relation_acc = kernel_call(
        final_body,
        [table, types],
        [mine, part, other, relations, relation_acc],
        [((FLAT, LANES), f32)],
        scalars=1,
    )
    return (
        source,
        source_acc.reshape(-1),
        settled,
        settled_acc.reshape(-1),
        relations,
        relation_acc.reshape(-1),
    )


def solution(mesh):
    fine = Mesh(mesh.devices.reshape(8, 8, 2, 4), ALL)
    in_specs = (
        P(None, ALL),
        P(ALL),
        P(None, ALL),
        P(ALL),
        P(),
        P(),
        P(DOM, "x"),
        P(DOM, "x"),
        P(DOM, "x", None),
        P(DOM, "x", None),
        P(DOM, "x", None),
        P(DOM, "x", None),
    )
    out_specs = (P(None, ALL), P(ALL), P(None, ALL), P(ALL), P(), P())
    return jax.shard_map(local, mesh=fine, in_specs=in_specs, out_specs=out_specs, check_vma=False)
```

```python
import jax
import jax.numpy as jnp
from jax import lax
from jax.experimental import pallas as pl
from jax.experimental.pallas import tpu as pltpu
from jax.sharding import Mesh
from jax.sharding import PartitionSpec as P

DIM = 400
HALF = 200
NREL = 768
BLOCK = 128
SPAN = 512
NEG = 1024
LANES = 128
CHUNKS = NREL // LANES
FLAT = 2560
HALF_FLAT = FLAT // 2
PIECE = 4

ALL = ("z", "y", "core", "x")
DOM = ("z", "y", "core")

learn_rate = 0.3
epsilon = 1e-08

f32 = jnp.float32
bf16 = jnp.bfloat16


def passed_along(value, axis, steps):
    count = lax.axis_size(axis)
    pairs = [(source, (source + steps) % count) for source in range(count)]
    return lax.ppermute(value, axis, pairs)


def exchange(value, axis):
    return lax.all_to_all(value, axis, split_axis=0, concat_axis=0, tiled=True)


def dealt(value, axis, count):
    rows, lanes = value.shape
    return exchange(value.reshape(count, rows // count, lanes), axis).reshape(rows, lanes)


def packets(value, axis, count):
    rows, lanes = value.shape
    parts = rows // (count * PIECE)
    return exchange(value.reshape(count, parts, PIECE, lanes), axis).reshape(rows, lanes)


def gathered(value, axis):
    count = lax.axis_size(axis)
    return exchange(jnp.broadcast_to(value[None], (count,) + value.shape), axis)


def kernel_call(body, outs, args, scratch=(), scalars=0):
    specs = [pl.BlockSpec(memory_space=pltpu.SMEM)] * scalars
    specs += [pl.BlockSpec(memory_space=pltpu.VMEM)] * (len(args) - scalars)
    return pl.pallas_call(
        body,
        out_shape=[jax.ShapeDtypeStruct(shape, dtype) for shape, dtype in outs],
        in_specs=specs,
        out_specs=[pl.BlockSpec(memory_space=pltpu.VMEM)] * len(outs),
        scratch_shapes=[pltpu.VMEM(shape, dtype) for shape, dtype in scratch],
        compiler_params=pltpu.CompilerParams(vmem_limit_bytes=24 * 2**20),
    )(*args)


def dot(left, right):
    return lax.dot_general(left, right, (((1,), (0,)), ((), ())), preferred_element_type=f32)


def dot_last(left, right):
    return lax.dot_general(left, right, (((1,), (1,)), ((), ())), preferred_element_type=f32)


def moved(pick, value):
    upper = value.astype(bf16)
    rest = value - upper.astype(f32)
    middle = rest.astype(bf16)
    lower = (rest - middle.astype(f32)).astype(bf16)
    return (dot(pick, upper) + dot(pick, middle)) + dot(pick, lower)


def one_hot(count, rows):
    hit = lax.broadcasted_iota(jnp.int32, (count, rows.shape[1]), 0) == rows
    return jnp.where(hit, 1.0, 0.0).astype(bf16)


def sigmoid(value):
    return 1.0 / (1.0 + jnp.exp(-value))


def stepped(param, state, grad):
    new_state = state + jnp.sum(grad * grad, axis=0, keepdims=True) * (1.0 / DIM)
    return (param - learn_rate * grad / (jnp.sqrt(new_state) + epsilon), new_state)


def spaced(start, size, stride):
    return pl.ds(start, size, stride=stride)


def pack_body(partner_ref, arriving_ref, state_ref, out_ref):
    for k in range(PIECE - 1):
        out_ref[spaced(k, BLOCK, PIECE), :] = arriving_ref[LANES * k : LANES * (k + 1), :].T
    tail = arriving_ref[LANES * (PIECE - 1) : DIM, :]
    state = jnp.broadcast_to(state_ref[...], (8, LANES))
    own = jnp.full((8, LANES), partner_ref[0, 0].astype(f32))
    zero = jnp.zeros((LANES - tail.shape[0] - 16, LANES), f32)
    out_ref[spaced(PIECE - 1, BLOCK, PIECE), :] = jnp.concatenate([tail, state, own, zero], 0).T


STATE_LANE = DIM - LANES * (PIECE - 1)
OWN_LANE = STATE_LANE + 8


def partner_pick(last):
    own = last[:, OWN_LANE : OWN_LANE + 1].astype(jnp.int32)
    lane = lax.broadcasted_iota(jnp.int32, (BLOCK, BLOCK), 1)
    return jnp.where(lane == own, 1.0, 0.0)


def pick_body(spread_ref, out_ref):
    last = spread_ref[spaced(PIECE - 1, BLOCK, PIECE), :]
    pick = partner_pick(last).astype(bf16)
    for k in range(PIECE - 1):
        rows = spaced(k, BLOCK, PIECE)
        out_ref[rows, :] = moved(pick, spread_ref[rows, :])
    out_ref[spaced(PIECE - 1, BLOCK, PIECE), :] = moved(pick, last)


def counted(rows_n):
    hits = lax.broadcasted_iota(jnp.int32, (BLOCK, NEG), 0) == rows_n
    count = jnp.sum(jnp.where(hits, 1.0, 0.0), axis=1, keepdims=True)
    return jnp.broadcast_to(count, (BLOCK, BLOCK))


def span_rows(i):
    re = pl.ds(pl.multiple_of(8 * i, 8), 8)
    im = pl.ds(pl.multiple_of(HALF + 8 * i, 8), 8)
    return re, im


def gradients(
    first,
    live_count,
    target,
    pick_r,
    count_wide,
    subject_ref,
    operator_ref,
    objects_ref,
    query_ref,
    slope_ref,
    flat_ref,
    grad_subject_ref,
):
    edge = lax.broadcasted_iota(jnp.int32, (1, SPAN), 1) + first
    live = jnp.where(edge < live_count, 1.0, 0.0)
    target_bf = target.astype(bf16)

    def form(i, total):
        re, im = span_rows(i)
        subject_re, subject_im = (subject_ref[re, :], subject_ref[im, :])
        operator_re, operator_im = (operator_ref[re, :], operator_ref[im, :])
        query_re = subject_re * operator_re - subject_im * operator_im
        query_im = subject_re * operator_im + subject_im * operator_re
        query_ref[re, :] = query_re
        query_ref[im, :] = query_im
        return total + query_re * objects_ref[re, :] + query_im * objects_ref[im, :]

    total = lax.fori_loop(0, HALF // 8, form, jnp.zeros((8, SPAN), f32), unroll=5)
    positive = jnp.sum(total, axis=0, keepdims=True)
    query_bf = query_ref[...].astype(bf16)
    score = dot(target.T.astype(bf16), query_bf)
    grad_pos = -sigmoid(-positive) * live
    slope = (sigmoid(score) * (live * (1.0 / NEG))).astype(bf16)
    weighted = slope.astype(f32) * count_wide[:, 0:1]
    upper = weighted.astype(bf16)
    lower = (weighted - upper.astype(f32)).astype(bf16)
    slope_ref[...] = dot(target_bf, upper) + dot(target_bf, lower)
    noise = dot_last(query_bf, slope).astype(bf16).astype(f32) * count_wide.T[0:1, :]

    def push(i, _):
        re, im = span_rows(i)
        query_gre = grad_pos * objects_ref[re, :] + slope_ref[re, :]
        query_gim = grad_pos * objects_ref[im, :] + slope_ref[im, :]
        subject_re, subject_im = (subject_ref[re, :], subject_ref[im, :])
        operator_re, operator_im = (operator_ref[re, :], operator_ref[im, :])
        grad_subject_ref[re, :] = query_gre * operator_re + query_gim * operator_im
        grad_subject_ref[im, :] = query_gim * operator_re - query_gre * operator_im
        operator_ref[re, :] = query_gre * subject_re + query_gim * subject_im
        operator_ref[im, :] = query_gim * subject_re - query_gre * subject_im
        query_ref[re, :] = grad_pos * query_ref[re, :]
        query_ref[im, :] = grad_pos * query_ref[im, :]
        return 0

    lax.fori_loop(0, HALF // 8, push, 0, unroll=5)
    grad_operator = operator_ref[...].astype(bf16)
    for k in range(0, CHUNKS, 2):
        pair = dot_last(grad_operator, pick_r[LANES * k : LANES * (k + 2), :])
        flat_ref[DIM * k : DIM * (k + 1), :] = pair[:, :LANES]
        flat_ref[DIM * (k + 1) : DIM * (k + 2), :] = pair[:, LANES:]
    flat_ref[DIM * CHUNKS : FLAT, :] = jnp.zeros((FLAT - DIM * CHUNKS, LANES), f32)
    return noise


WIDE = ((DIM, SPAN), f32)
FLAT_TABLE = ((FLAT, LANES), f32)


def halves(mine, flat_ref, keep_ref, give_ref):
    keep_ref[0:HALF_FLAT, :] = flat_ref[pl.ds(pl.multiple_of(mine * HALF_FLAT, 8), HALF_FLAT), :]
    give_ref[0:HALF_FLAT, :] = flat_ref[
        pl.ds(pl.multiple_of((1 - mine) * HALF_FLAT, 8), HALF_FLAT), :
    ]


def first_body(
    mine_ref,
    live_ref,
    arrived_ref,
    source_ref,
    source_state_ref,
    relations_ref,
    rows_s_ref,
    rows_t_ref,
    rows_r_ref,
    rows_n_ref,
    source_out,
    source_state_out,
    target_out,
    target_state_out,
    keep_out,
    give_out,
    subject_ref,
    operator_ref,
    objects_ref,
    query_ref,
    slope_ref,
    flat_ref,
):
    last = arrived_ref[spaced(PIECE - 1, BLOCK, PIECE), :].T
    target = jnp.concatenate(
        [arrived_ref[spaced(k, BLOCK, PIECE), :].T for k in range(PIECE - 1)]
        + [last[:STATE_LANE, :]],
        0,
    )
    source = source_ref[...]
    pick_s = one_hot(BLOCK, rows_s_ref[:, 0:SPAN])
    pick_t = one_hot(BLOCK, rows_t_ref[:, 0:SPAN])
    pick_r = one_hot(NREL, rows_r_ref[:, 0:SPAN])
    subject_ref[...] = dot(source.astype(bf16), pick_s)
    operator_ref[...] = dot(relations_ref[...].astype(bf16), pick_r)
    objects_ref[...] = dot(target.astype(bf16), pick_t)
    noise = gradients(
        0,
        live_ref[0, 0],
        target,
        pick_r,
        counted(rows_n_ref[:, 0:NEG]),
        subject_ref,
        operator_ref,
        objects_ref,
        query_ref,
        slope_ref,
        flat_ref,
        subject_ref,
    )
    halves(mine_ref[0, 0], flat_ref, keep_out, give_out)
    grad_source = dot_last(subject_ref[...].astype(bf16), pick_s)
    source_out[...], source_state_out[...] = stepped(source, source_state_ref[...], grad_source)
    grad_target = dot_last(query_ref[...].astype(bf16), pick_t) + noise
    target_out[...], target_state_out[...] = stepped(
        target, last[STATE_LANE : STATE_LANE + 1, :], grad_target
    )


def lookup_body(
    source_ref,
    target_ref,
    rows_s_ref,
    rows_t_ref,
    rows_r_ref,
    rows_n_ref,
    subject_ref,
    objects_ref,
    pick_r_ref,
    count_ref,
):
    pick_s = one_hot(BLOCK, rows_s_ref[:, SPAN : 2 * SPAN])
    pick_t = one_hot(BLOCK, rows_t_ref[:, SPAN : 2 * SPAN])
    subject_ref[...] = dot(source_ref[...].astype(bf16), pick_s)
    objects_ref[...] = dot(target_ref[...].astype(bf16), pick_t)
    pick_r_ref[...] = one_hot(NREL, rows_r_ref[:, SPAN : 2 * SPAN])
    count_ref[...] = counted(rows_n_ref[:, NEG : 2 * NEG])


def relation_update(mine, part_ref, other_ref, relations_ref, state_ref, out, state_out, flat_ref):
    flat_ref[pl.ds(pl.multiple_of(mine * HALF_FLAT, 8), HALF_FLAT), :] = part_ref[...]
    flat_ref[pl.ds(pl.multiple_of((1 - mine) * HALF_FLAT, 8), HALF_FLAT), :] = other_ref[...]
    for k in range(CHUNKS):
        lanes = slice(LANES * k, LANES * (k + 1))
        grad = flat_ref[DIM * k : DIM * (k + 1), :]
        new, new_state = stepped(relations_ref[:, lanes], state_ref[:, lanes], grad)
        out[:, lanes] = new
        state_out[:, lanes] = new_state


def second_body(
    mine_ref,
    live_ref,
    partner_ref,
    part_ref,
    other_ref,
    source_ref,
    source_state_ref,
    target_ref,
    target_state_ref,
    relations_ref,
    relation_state_ref,
    first_subject_ref,
    objects_ref,
    pick_r_ref,
    count_ref,
    rows_s_ref,
    rows_t_ref,
    source_out,
    source_state_out,
    relations_out,
    relation_state_out,
    keep_out,
    give_out,
    subject_ref,
    operator_ref,
    query_ref,
    slope_ref,
    flat_ref,
    turned_ref,
):
    mine = mine_ref[0, 0]
    relation_update(
        mine,
        part_ref,
        other_ref,
        relations_ref,
        relation_state_ref,
        relations_out,
        relation_state_out,
        flat_ref,
    )
    pick_r = pick_r_ref[...]
    operator_ref[...] = dot(relations_out[...].astype(bf16), pick_r)
    target = target_ref[...]
    noise = gradients(
        SPAN,
        live_ref[0, 0],
        target,
        pick_r,
        count_ref[...],
        first_subject_ref,
        operator_ref,
        objects_ref,
        query_ref,
        slope_ref,
        flat_ref,
        subject_ref,
    )
    halves(mine, flat_ref, keep_out, give_out)
    pick_s = one_hot(BLOCK, rows_s_ref[:, SPAN : 2 * SPAN])
    pick_t = one_hot(BLOCK, rows_t_ref[:, SPAN : 2 * SPAN])
    grad_source = dot_last(subject_ref[...].astype(bf16), pick_s)
    source_out[...], source_state_out[...] = stepped(
        source_ref[...], source_state_ref[...], grad_source
    )
    grad_target = dot_last(query_ref[...].astype(bf16), pick_t) + noise
    target, target_state = stepped(target, target_state_ref[...], grad_target)
    for k in range(PIECE):
        if k < PIECE - 1:
            turned_ref[...] = target[LANES * k : LANES * (k + 1), :].T
        else:
            state = jnp.broadcast_to(target_state, (8, LANES))
            own = jnp.full((8, LANES), partner_ref[0, 0].astype(f32))
            zero = jnp.zeros((LANES // 2 - STATE_LANE - 16, LANES), f32)
            tail = [target[LANES * k : DIM, :], state, own, zero]
            turned_ref[...] = jnp.concatenate(tail + tail, 0).T
        rows = slice(HALF_FLAT + 64 * k, HALF_FLAT + 64 * (k + 1))
        keep_out[rows, :] = turned_ref[spaced(mine, 64, 2), :]
        give_out[rows, :] = turned_ref[spaced(1 - mine, 64, 2), :]


FULL = PIECE - 1
TAIL = 2 * FULL
SUM_ROW = TAIL + 1
SUM_ROWS = 5
ROWS = SUM_ROW + SUM_ROWS


def low_lanes(shape):
    return lax.broadcasted_iota(jnp.int32, shape, 1) < LANES // 2


def swapped(value):
    return pltpu.roll(value, LANES // 2, 1)


def join_body(keep_ref, got_ref, sums_ref, block_ref):
    sums_ref[...] = keep_ref[0:HALF_FLAT, :] + got_ref[0:HALF_FLAT, :]
    full = 64 * FULL
    block_ref[0:full, :] = keep_ref[HALF_FLAT : HALF_FLAT + full, :]
    block_ref[full : 2 * full, :] = got_ref[HALF_FLAT : HALF_FLAT + full, :]
    block_ref[2 * full :, :] = jnp.where(
        low_lanes((64, LANES)), keep_ref[HALF_FLAT + full :, :], got_ref[HALF_FLAT + full :, :]
    )


def merge_body(received_ref, block_ref, out_ref):
    for k in range(SUM_ROW):
        out_ref[spaced(k, 64, ROWS), :] = block_ref[64 * k : 64 * (k + 1), :]
    for k in range(SUM_ROWS):
        rows = slice(64 * k, 64 * (k + 1))
        total = received_ref[0, rows, :] + received_ref[1, rows, :]
        total = total + received_ref[2, rows, :] + received_ref[3, rows, :]
        out_ref[spaced(SUM_ROW + k, 64, ROWS), :] = total


def middle_body(mine_ref, received_ref, out_ref, turned_ref):
    mine = mine_ref[0, 0]
    here, there = (spaced(mine, 64, 2), spaced(1 - mine, 64, 2))
    tail = received_ref[spaced(TAIL, 64, ROWS), :]
    turned_ref[here, :] = tail
    turned_ref[there, :] = swapped(tail)
    back = partner_pick(turned_ref[...]).T.astype(bf16)
    turned_ref[...] = moved(back, turned_ref[...])
    out_ref[spaced(TAIL, 64, ROWS), :] = jnp.where(
        low_lanes((64, LANES)), turned_ref[here, :], swapped(turned_ref[there, :])
    )
    for k in range(FULL):
        turned_ref[here, :] = received_ref[spaced(k, 64, ROWS), :]
        turned_ref[there, :] = received_ref[spaced(FULL + k, 64, ROWS), :]
        turned_ref[...] = moved(back, turned_ref[...])
        out_ref[spaced(k, 64, ROWS), :] = turned_ref[here, :]
        out_ref[spaced(FULL + k, 64, ROWS), :] = turned_ref[there, :]
    for k in range(SUM_ROW, ROWS):
        total = jnp.sum(received_ref[spaced(k, 64, ROWS), :], axis=0, keepdims=True)
        out_ref[spaced(k, 64, ROWS), :] = jnp.broadcast_to(total, (64, LANES))


def parting_body(received_ref, sums_ref, block_ref, give_ref):
    for k in range(FULL):
        rows = slice(64 * k, 64 * (k + 1))
        block_ref[rows, :] = received_ref[spaced(k, 64, ROWS), :]
        give_ref[rows, :] = received_ref[spaced(FULL + k, 64, ROWS), :]
    tail = received_ref[spaced(TAIL, 64, ROWS), :]
    block_ref[64 * FULL :, :] = tail
    give_ref[64 * FULL :, :] = swapped(tail)
    for k in range(SUM_ROWS):
        rows = received_ref[spaced(SUM_ROW + k, 64, ROWS), :]
        for x in range(4):
            sums_ref[x, 64 * k : 64 * (k + 1), :] = rows


def settle_body(mine_ref, block_ref, other_ref, out_ref, state_out, turned_ref):
    mine = mine_ref[0, 0]
    for k in range(PIECE):
        rows = slice(64 * k, 64 * (k + 1))
        turned_ref[spaced(mine, 64, 2), :] = block_ref[rows, :]
        turned_ref[spaced(1 - mine, 64, 2), :] = other_ref[rows, :]
        turned = turned_ref[...].T
        if k < PIECE - 1:
            out_ref[LANES * k : LANES * (k + 1), :] = turned
        else:
            out_ref[LANES * k : DIM, :] = turned[:STATE_LANE, :]
            state_out[...] = turned[STATE_LANE : STATE_LANE + 1, :]


def final_body(
    mine_ref, part_ref, other_ref, relations_ref, state_ref, out_ref, state_out, flat_ref
):
    relation_update(
        mine_ref[0, 0], part_ref, other_ref, relations_ref, state_ref, out_ref, state_out, flat_ref
    )


def local(
    source_emb,
    source_state,
    dest_emb,
    dest_state,
    relations,
    relation_state,
    partner,
    edge_count,
    source_rows,
    target_rows,
    relation_index,
    negative_rows,
):
    mine = lax.axis_index("core").astype(jnp.int32).reshape(1, 1)
    turned = ((BLOCK, LANES), f32)
    arriving = passed_along(dest_emb, "x", 1)
    arriving_state = passed_along(dest_state.reshape(1, BLOCK), "x", 1)
    tile = ((BLOCK * PIECE, LANES), f32)
    (cargo,) = kernel_call(pack_body, [tile], [partner, arriving, arriving_state], scalars=1)
    spread = dealt(cargo, DOM, BLOCK)
    (spread,) = kernel_call(pick_body, [tile], [spread])
    arrived = dealt(spread, DOM, BLOCK)
    lists = [
        rows.reshape(1, -1) for rows in (source_rows, target_rows, relation_index, negative_rows)
    ]
    block = ((DIM, BLOCK), f32)
    line = ((1, BLOCK), f32)
    half = ((HALF_FLAT, LANES), f32)
    picks_r = ((NREL, SPAN), bf16)
    square = ((BLOCK, BLOCK), f32)
    source, source_acc, target, target_acc, keep, give = kernel_call(
        first_body,
        [block, line, block, line, half, half],
        [mine, edge_count, arrived, source_emb, source_state.reshape(1, -1), relations] + lists,
        [WIDE] * 5 + [FLAT_TABLE],
        scalars=2,
    )
    subject, objects, pick_r, count = kernel_call(
        lookup_body, [WIDE, WIDE, picks_r, square], [source, target] + lists
    )
    part = keep + passed_along(give, "core", 1)
    part = jnp.sum(exchange(part.reshape(4, 320, LANES), "x"), 0)
    part = jnp.sum(exchange(part.reshape(8, 40, LANES), "y"), 0)
    part = jnp.sum(gathered(part, "z"), 0)
    part = gathered(part, "y").reshape(320, LANES)
    part = gathered(part, "x").reshape(HALF_FLAT, LANES)
    other = passed_along(part, "core", 1)
    table = ((DIM, NREL), f32)
    types = ((1, NREL), f32)
    longer = ((HALF_FLAT + 64 * PIECE, LANES), f32)
    source, source_acc, relations, relation_acc, keep, give = kernel_call(
        second_body,
        [block, line, table, types, longer, longer],
        [mine, edge_count, partner, part, other, source, source_acc, target, target_acc]
        + [relations, relation_state.reshape(1, -1), subject, objects, pick_r, count]
        + lists[:2],
        [WIDE] * 4 + [FLAT_TABLE, turned],
        scalars=3,
    )
    got = passed_along(give, "core", 1)
    part, leaving = kernel_call(join_body, [half, ((64 * SUM_ROW, LANES), f32)], [keep, got])
    leaving = passed_along(leaving, "x", -1)
    received = exchange(part.reshape(4, 320, LANES), "x")
    packet = ((64 * ROWS, LANES), f32)
    (packed,) = kernel_call(merge_body, [packet], [received, leaving])
    packed = packets(packed, ("z", "y"), 64)
    (packed,) = kernel_call(middle_body, [packet], [mine, packed], [turned], scalars=1)
    packed = packets(packed, ("z", "y"), 64)
    pieces = ((64 * PIECE, LANES), f32)
    sums, returned, sibling = kernel_call(
        parting_body, [((4, 320, LANES), f32), pieces, pieces], [packed]
    )
    sibling = passed_along(sibling, "core", 1)
    part = exchange(sums, "x").reshape(HALF_FLAT, LANES)
    settled, settled_acc = kernel_call(
        settle_body, [block, line], [mine, returned, sibling], [turned], scalars=1
    )
    part, settled, settled_acc = lax.optimization_barrier((part, settled, settled_acc))
    other = passed_along(part, "core", 1)
    relations, relation_acc = kernel_call(
        final_body,
        [table, types],
        [mine, part, other, relations, relation_acc],
        [((FLAT, LANES), f32)],
        scalars=1,
    )
    return (
        source,
        source_acc.reshape(-1),
        settled,
        settled_acc.reshape(-1),
        relations,
        relation_acc.reshape(-1),
    )


def solution(mesh):
    fine = Mesh(mesh.devices.reshape(8, 8, 2, 4), ALL)
    in_specs = (
        P(None, ALL),
        P(ALL),
        P(None, ALL),
        P(ALL),
        P(),
        P(),
        P(DOM, "x"),
        P(DOM, "x"),
        P(DOM, "x", None),
        P(DOM, "x", None),
        P(DOM, "x", None),
        P(DOM, "x", None),
    )
    out_specs = (P(None, ALL), P(ALL), P(None, ALL), P(ALL), P(), P())
    return jax.shard_map(local, mesh=fine, in_specs=in_specs, out_specs=out_specs, check_vma=False)
```

```python
import jax
import jax.numpy as jnp
from jax import lax
from jax.experimental import pallas as pl
from jax.experimental.pallas import tpu as pltpu
from jax.sharding import Mesh
from jax.sharding import PartitionSpec as P

DIM = 400
HALF = 200
NREL = 768
BLOCK = 128
SPAN = 512
NEG = 1024
LANES = 128
CHUNKS = NREL // LANES
FLAT = 2560
HALF_FLAT = FLAT // 2
PIECE = 4

ALL = ("z", "y", "core", "x")
DOM = ("z", "y", "core")

learn_rate = 0.3
epsilon = 1e-08

f32 = jnp.float32
bf16 = jnp.bfloat16


def passed_along(value, axis, steps):
    count = lax.axis_size(axis)
    pairs = [(source, (source + steps) % count) for source in range(count)]
    return lax.ppermute(value, axis, pairs)


def exchange(value, axis):
    return lax.all_to_all(value, axis, split_axis=0, concat_axis=0, tiled=True)


def dealt(value, axis, count):
    rows, lanes = value.shape
    return exchange(value.reshape(count, rows // count, lanes), axis).reshape(rows, lanes)


def packets(value, axis, count):
    rows, lanes = value.shape
    parts = rows // (count * PIECE)
    return exchange(value.reshape(count, parts, PIECE, lanes), axis).reshape(rows, lanes)


def gathered(value, axis):
    count = lax.axis_size(axis)
    return exchange(jnp.broadcast_to(value[None], (count,) + value.shape), axis)


def kernel_call(body, outs, args, scratch=(), scalars=0):
    specs = [pl.BlockSpec(memory_space=pltpu.SMEM)] * scalars
    specs += [pl.BlockSpec(memory_space=pltpu.VMEM)] * (len(args) - scalars)
    return pl.pallas_call(
        body,
        out_shape=[jax.ShapeDtypeStruct(shape, dtype) for shape, dtype in outs],
        in_specs=specs,
        out_specs=[pl.BlockSpec(memory_space=pltpu.VMEM)] * len(outs),
        scratch_shapes=[pltpu.VMEM(shape, dtype) for shape, dtype in scratch],
        compiler_params=pltpu.CompilerParams(vmem_limit_bytes=24 * 2**20),
    )(*args)


def dot(left, right):
    return lax.dot_general(left, right, (((1,), (0,)), ((), ())), preferred_element_type=f32)


def dot_last(left, right):
    return lax.dot_general(left, right, (((1,), (1,)), ((), ())), preferred_element_type=f32)


def moved(pick, value):
    upper = value.astype(bf16)
    rest = value - upper.astype(f32)
    middle = rest.astype(bf16)
    lower = (rest - middle.astype(f32)).astype(bf16)
    return (dot(pick, upper) + dot(pick, middle)) + dot(pick, lower)


def one_hot(count, rows):
    hit = lax.broadcasted_iota(jnp.int32, (count, rows.shape[1]), 0) == rows
    return jnp.where(hit, 1.0, 0.0).astype(bf16)


def sigmoid(value):
    return 1.0 / (1.0 + jnp.exp(-value))


def stepped(param, state, grad):
    new_state = state + jnp.sum(grad * grad, axis=0, keepdims=True) * (1.0 / DIM)
    return (param - learn_rate * grad / (jnp.sqrt(new_state) + epsilon), new_state)


def spaced(start, size, stride):
    return pl.ds(start, size, stride=stride)


def pack_body(partner_ref, dest_ref, state_ref, out_ref):
    for k in range(PIECE - 1):
        out_ref[spaced(k, BLOCK, PIECE), :] = dest_ref[LANES * k : LANES * (k + 1), :].T
    tail = dest_ref[LANES * (PIECE - 1) : DIM, :]
    state = jnp.broadcast_to(state_ref[...], (8, LANES))
    own = jnp.full((8, LANES), partner_ref[0, 0].astype(f32))
    zero = jnp.zeros((LANES - tail.shape[0] - 16, LANES), f32)
    out_ref[spaced(PIECE - 1, BLOCK, PIECE), :] = jnp.concatenate([tail, state, own, zero], 0).T


STATE_ROW = DIM
LIVE_ROW = DIM + 1
LIST_ROWS = (DIM + 8, DIM + 16, DIM + 24, DIM + 32)
BUCKET_ROWS = DIM + 48


def bucket_body(live_ref, source_ref, state_ref, list_s, list_t, list_r, list_n, out_ref):
    out_ref[0:DIM, :] = source_ref[...]
    live = jnp.full((7, LANES), live_ref[0, 0].astype(f32))
    out_ref[DIM : DIM + 8, :] = jnp.concatenate([state_ref[...], live], 0)
    for first, ref in zip(LIST_ROWS, (list_s, list_t, list_r, list_n)):
        for k in range(ref.shape[1] // LANES):
            row = ref[:, LANES * k : LANES * (k + 1)].astype(f32)
            out_ref[first + k : first + k + 1, :] = row


def listed(bucket_ref, which, span):
    count = (NEG if which == 3 else SPAN) // LANES
    first = LIST_ROWS[which] + count * span
    rows = [bucket_ref[first + k : first + k + 1, :] for k in range(count)]
    return jnp.concatenate(rows, 1).astype(jnp.int32)


STATE_LANE = DIM - LANES * (PIECE - 1)
OWN_LANE = STATE_LANE + 8


def partner_pick(last):
    own = last[:, OWN_LANE : OWN_LANE + 1].astype(jnp.int32)
    lane = lax.broadcasted_iota(jnp.int32, (BLOCK, BLOCK), 1)
    return jnp.where(lane == own, 1.0, 0.0)


def pick_body(spread_ref, out_ref):
    last = spread_ref[spaced(PIECE - 1, BLOCK, PIECE), :]
    pick = partner_pick(last).astype(bf16)
    for k in range(PIECE - 1):
        rows = spaced(k, BLOCK, PIECE)
        out_ref[rows, :] = moved(pick, spread_ref[rows, :])
    out_ref[spaced(PIECE - 1, BLOCK, PIECE), :] = moved(pick, last)


def counted(rows_n):
    hits = lax.broadcasted_iota(jnp.int32, (BLOCK, NEG), 0) == rows_n
    count = jnp.sum(jnp.where(hits, 1.0, 0.0), axis=1, keepdims=True)
    return jnp.broadcast_to(count, (BLOCK, BLOCK))


def span_rows(i):
    re = pl.ds(pl.multiple_of(8 * i, 8), 8)
    im = pl.ds(pl.multiple_of(HALF + 8 * i, 8), 8)
    return re, im


def gradients(
    first,
    bucket_ref,
    target,
    pick_r,
    count_wide,
    subject_ref,
    operator_ref,
    objects_ref,
    query_ref,
    slope_ref,
    flat_ref,
    grad_subject_ref,
):
    edge = lax.broadcasted_iota(jnp.int32, (1, SPAN), 1) + first
    live_count = bucket_ref[LIVE_ROW : LIVE_ROW + 1, :]
    live_count = jnp.concatenate([live_count] * (SPAN // LANES), 1).astype(jnp.int32)
    live = jnp.where(edge < live_count, 1.0, 0.0)
    target_bf = target.astype(bf16)

    def form(i, total):
        re, im = span_rows(i)
        subject_re, subject_im = (subject_ref[re, :], subject_ref[im, :])
        operator_re, operator_im = (operator_ref[re, :], operator_ref[im, :])
        query_re = subject_re * operator_re - subject_im * operator_im
        query_im = subject_re * operator_im + subject_im * operator_re
        query_ref[re, :] = query_re
        query_ref[im, :] = query_im
        return total + query_re * objects_ref[re, :] + query_im * objects_ref[im, :]

    total = lax.fori_loop(0, HALF // 8, form, jnp.zeros((8, SPAN), f32), unroll=5)
    positive = jnp.sum(total, axis=0, keepdims=True)
    query_bf = query_ref[...].astype(bf16)
    score = dot(target.T.astype(bf16), query_bf)
    grad_pos = -sigmoid(-positive) * live
    slope = (sigmoid(score) * (live * (1.0 / NEG))).astype(bf16)
    weighted = slope.astype(f32) * count_wide[:, 0:1]
    upper = weighted.astype(bf16)
    lower = (weighted - upper.astype(f32)).astype(bf16)
    slope_ref[...] = dot(target_bf, upper) + dot(target_bf, lower)
    noise = dot_last(query_bf, slope).astype(bf16).astype(f32) * count_wide.T[0:1, :]

    def push(i, _):
        re, im = span_rows(i)
        query_gre = grad_pos * objects_ref[re, :] + slope_ref[re, :]
        query_gim = grad_pos * objects_ref[im, :] + slope_ref[im, :]
        subject_re, subject_im = (subject_ref[re, :], subject_ref[im, :])
        operator_re, operator_im = (operator_ref[re, :], operator_ref[im, :])
        grad_subject_ref[re, :] = query_gre * operator_re + query_gim * operator_im
        grad_subject_ref[im, :] = query_gim * operator_re - query_gre * operator_im
        operator_ref[re, :] = query_gre * subject_re + query_gim * subject_im
        operator_ref[im, :] = query_gim * subject_re - query_gre * subject_im
        query_ref[re, :] = grad_pos * query_ref[re, :]
        query_ref[im, :] = grad_pos * query_ref[im, :]
        return 0

    lax.fori_loop(0, HALF // 8, push, 0, unroll=5)
    grad_operator = operator_ref[...].astype(bf16)
    for k in range(0, CHUNKS, 2):
        pair = dot_last(grad_operator, pick_r[LANES * k : LANES * (k + 2), :])
        flat_ref[DIM * k : DIM * (k + 1), :] = pair[:, :LANES]
        flat_ref[DIM * (k + 1) : DIM * (k + 2), :] = pair[:, LANES:]
    flat_ref[DIM * CHUNKS : FLAT, :] = jnp.zeros((FLAT - DIM * CHUNKS, LANES), f32)
    return noise


WIDE = ((DIM, SPAN), f32)
FLAT_TABLE = ((FLAT, LANES), f32)


def halves(mine, flat_ref, keep_ref, give_ref):
    keep_ref[0:HALF_FLAT, :] = flat_ref[pl.ds(pl.multiple_of(mine * HALF_FLAT, 8), HALF_FLAT), :]
    give_ref[0:HALF_FLAT, :] = flat_ref[
        pl.ds(pl.multiple_of((1 - mine) * HALF_FLAT, 8), HALF_FLAT), :
    ]


def first_body(
    mine_ref,
    arrived_ref,
    bucket_ref,
    relations_ref,
    source_out,
    source_state_out,
    target_out,
    target_state_out,
    keep_out,
    give_out,
    subject_ref,
    operator_ref,
    objects_ref,
    query_ref,
    slope_ref,
    flat_ref,
):
    last = arrived_ref[spaced(PIECE - 1, BLOCK, PIECE), :].T
    target = jnp.concatenate(
        [arrived_ref[spaced(k, BLOCK, PIECE), :].T for k in range(PIECE - 1)]
        + [last[:STATE_LANE, :]],
        0,
    )
    source = bucket_ref[0:DIM, :]
    pick_s = one_hot(BLOCK, listed(bucket_ref, 0, 0))
    pick_t = one_hot(BLOCK, listed(bucket_ref, 1, 0))
    pick_r = one_hot(NREL, listed(bucket_ref, 2, 0))
    subject_ref[...] = dot(source.astype(bf16), pick_s)
    operator_ref[...] = dot(relations_ref[...].astype(bf16), pick_r)
    objects_ref[...] = dot(target.astype(bf16), pick_t)
    noise = gradients(
        0,
        bucket_ref,
        target,
        pick_r,
        counted(listed(bucket_ref, 3, 0)),
        subject_ref,
        operator_ref,
        objects_ref,
        query_ref,
        slope_ref,
        flat_ref,
        subject_ref,
    )
    halves(mine_ref[0, 0], flat_ref, keep_out, give_out)
    grad_source = dot_last(subject_ref[...].astype(bf16), pick_s)
    source_out[...], source_state_out[...] = stepped(
        source, bucket_ref[STATE_ROW : STATE_ROW + 1, :], grad_source
    )
    grad_target = dot_last(query_ref[...].astype(bf16), pick_t) + noise
    target_out[...], target_state_out[...] = stepped(
        target, last[STATE_LANE : STATE_LANE + 1, :], grad_target
    )


def lookup_body(
    source_ref,
    target_ref,
    bucket_ref,
    subject_ref,
    objects_ref,
    pick_r_ref,
    count_ref,
):
    pick_s = one_hot(BLOCK, listed(bucket_ref, 0, 1))
    pick_t = one_hot(BLOCK, listed(bucket_ref, 1, 1))
    subject_ref[...] = dot(source_ref[...].astype(bf16), pick_s)
    objects_ref[...] = dot(target_ref[...].astype(bf16), pick_t)
    pick_r_ref[...] = one_hot(NREL, listed(bucket_ref, 2, 1))
    count_ref[...] = counted(listed(bucket_ref, 3, 1))


def relation_update(mine, part_ref, other_ref, relations_ref, state_ref, out, state_out, flat_ref):
    flat_ref[pl.ds(pl.multiple_of(mine * HALF_FLAT, 8), HALF_FLAT), :] = part_ref[...]
    flat_ref[pl.ds(pl.multiple_of((1 - mine) * HALF_FLAT, 8), HALF_FLAT), :] = other_ref[...]
    for k in range(CHUNKS):
        lanes = slice(LANES * k, LANES * (k + 1))
        grad = flat_ref[DIM * k : DIM * (k + 1), :]
        new, new_state = stepped(relations_ref[:, lanes], state_ref[:, lanes], grad)
        out[:, lanes] = new
        state_out[:, lanes] = new_state


def second_body(
    mine_ref,
    partner_ref,
    part_ref,
    other_ref,
    source_ref,
    source_state_ref,
    target_ref,
    target_state_ref,
    relations_ref,
    relation_state_ref,
    first_subject_ref,
    objects_ref,
    pick_r_ref,
    count_ref,
    bucket_ref,
    source_out,
    relations_out,
    relation_state_out,
    keep_out,
    give_out,
    subject_ref,
    operator_ref,
    query_ref,
    slope_ref,
    flat_ref,
    turned_ref,
):
    mine = mine_ref[0, 0]
    relation_update(
        mine,
        part_ref,
        other_ref,
        relations_ref,
        relation_state_ref,
        relations_out,
        relation_state_out,
        flat_ref,
    )
    pick_r = pick_r_ref[...]
    operator_ref[...] = dot(relations_out[...].astype(bf16), pick_r)
    target = target_ref[...]
    noise = gradients(
        SPAN,
        bucket_ref,
        target,
        pick_r,
        count_ref[...],
        first_subject_ref,
        operator_ref,
        objects_ref,
        query_ref,
        slope_ref,
        flat_ref,
        subject_ref,
    )
    halves(mine, flat_ref, keep_out, give_out)
    pick_s = one_hot(BLOCK, listed(bucket_ref, 0, 1))
    pick_t = one_hot(BLOCK, listed(bucket_ref, 1, 1))
    grad_source = dot_last(subject_ref[...].astype(bf16), pick_s)
    source, source_state = stepped(source_ref[...], source_state_ref[...], grad_source)
    source_out[0:DIM, :] = source
    source_out[DIM : DIM + 8, :] = jnp.broadcast_to(source_state, (8, LANES))
    grad_target = dot_last(query_ref[...].astype(bf16), pick_t) + noise
    target, target_state = stepped(target, target_state_ref[...], grad_target)
    for k in range(PIECE):
        if k < PIECE - 1:
            turned_ref[...] = target[LANES * k : LANES * (k + 1), :].T
        else:
            state = jnp.broadcast_to(target_state, (8, LANES))
            own = jnp.full((8, LANES), partner_ref[0, 0].astype(f32))
            zero = jnp.zeros((LANES // 2 - STATE_LANE - 16, LANES), f32)
            tail = [target[LANES * k : DIM, :], state, own, zero]
            turned_ref[...] = jnp.concatenate(tail + tail, 0).T
        rows = slice(HALF_FLAT + 64 * k, HALF_FLAT + 64 * (k + 1))
        keep_out[rows, :] = turned_ref[spaced(mine, 64, 2), :]
        give_out[rows, :] = turned_ref[spaced(1 - mine, 64, 2), :]


FULL = PIECE - 1
TAIL = 2 * FULL
SUM_ROW = TAIL + 1
SUM_ROWS = 5
ROWS = SUM_ROW + SUM_ROWS


def low_lanes(shape):
    return lax.broadcasted_iota(jnp.int32, shape, 1) < LANES // 2


def swapped(value):
    return pltpu.roll(value, LANES // 2, 1)


def merge_body(received_ref, keep_ref, got_ref, out_ref):
    for k in range(FULL):
        rows = slice(HALF_FLAT + 64 * k, HALF_FLAT + 64 * (k + 1))
        out_ref[spaced(k, 64, ROWS), :] = keep_ref[rows, :]
        out_ref[spaced(FULL + k, 64, ROWS), :] = got_ref[rows, :]
    rows = slice(HALF_FLAT + 64 * FULL, HALF_FLAT + 64 * PIECE)
    out_ref[spaced(TAIL, 64, ROWS), :] = jnp.where(
        low_lanes((64, LANES)), keep_ref[rows, :], got_ref[rows, :]
    )
    for k in range(SUM_ROWS):
        rows = slice(64 * k, 64 * (k + 1))
        total = received_ref[0, rows, :] + received_ref[1, rows, :]
        total = total + received_ref[2, rows, :] + received_ref[3, rows, :]
        out_ref[spaced(SUM_ROW + k, 64, ROWS), :] = total


def middle_body(mine_ref, received_ref, out_ref, turned_ref):
    mine = mine_ref[0, 0]
    here, there = (spaced(mine, 64, 2), spaced(1 - mine, 64, 2))
    tail = received_ref[spaced(TAIL, 64, ROWS), :]
    turned_ref[here, :] = tail
    turned_ref[there, :] = swapped(tail)
    back = partner_pick(turned_ref[...]).T.astype(bf16)
    turned_ref[...] = moved(back, turned_ref[...])
    out_ref[spaced(TAIL, 64, ROWS), :] = jnp.where(
        low_lanes((64, LANES)), turned_ref[here, :], swapped(turned_ref[there, :])
    )
    for k in range(FULL):
        turned_ref[here, :] = received_ref[spaced(k, 64, ROWS), :]
        turned_ref[there, :] = received_ref[spaced(FULL + k, 64, ROWS), :]
        turned_ref[...] = moved(back, turned_ref[...])
        out_ref[spaced(k, 64, ROWS), :] = turned_ref[here, :]
        out_ref[spaced(FULL + k, 64, ROWS), :] = turned_ref[there, :]
    for k in range(SUM_ROW, ROWS):
        total = jnp.sum(received_ref[spaced(k, 64, ROWS), :], axis=0, keepdims=True)
        out_ref[spaced(k, 64, ROWS), :] = jnp.broadcast_to(total, (64, LANES))


def parting_body(received_ref, sums_ref, block_ref, give_ref):
    for k in range(FULL):
        rows = slice(64 * k, 64 * (k + 1))
        block_ref[rows, :] = received_ref[spaced(k, 64, ROWS), :]
        give_ref[rows, :] = received_ref[spaced(FULL + k, 64, ROWS), :]
    tail = received_ref[spaced(TAIL, 64, ROWS), :]
    block_ref[64 * FULL :, :] = tail
    give_ref[64 * FULL :, :] = swapped(tail)
    for k in range(SUM_ROWS):
        rows = received_ref[spaced(SUM_ROW + k, 64, ROWS), :]
        for x in range(4):
            sums_ref[x, 64 * k : 64 * (k + 1), :] = rows


def settle_body(mine_ref, block_ref, other_ref, out_ref, state_out, turned_ref):
    mine = mine_ref[0, 0]
    for k in range(PIECE):
        rows = slice(64 * k, 64 * (k + 1))
        turned_ref[spaced(mine, 64, 2), :] = block_ref[rows, :]
        turned_ref[spaced(1 - mine, 64, 2), :] = other_ref[rows, :]
        turned = turned_ref[...].T
        if k < PIECE - 1:
            out_ref[LANES * k : LANES * (k + 1), :] = turned
        else:
            out_ref[LANES * k : DIM, :] = turned[:STATE_LANE, :]
            state_out[...] = turned[STATE_LANE : STATE_LANE + 1, :]


def final_body(
    mine_ref,
    part_ref,
    other_ref,
    relations_ref,
    state_ref,
    source_ref,
    out_ref,
    state_out,
    source_out,
    source_state_out,
    flat_ref,
):
    source_out[...] = source_ref[0:DIM, :]
    source_state_out[...] = source_ref[DIM : DIM + 1, :]
    relation_update(
        mine_ref[0, 0], part_ref, other_ref, relations_ref, state_ref, out_ref, state_out, flat_ref
    )


def local(
    source_emb,
    source_state,
    dest_emb,
    dest_state,
    relations,
    relation_state,
    partner,
    edge_count,
    source_rows,
    target_rows,
    relation_index,
    negative_rows,
):
    mine = lax.axis_index("core").astype(jnp.int32).reshape(1, 1)
    turned = ((BLOCK, LANES), f32)
    partner = passed_along(partner, "x", -1)
    tile = ((BLOCK * PIECE, LANES), f32)
    (cargo,) = kernel_call(
        pack_body, [tile], [partner, dest_emb, dest_state.reshape(1, -1)], scalars=1
    )
    lists = [
        rows.reshape(1, -1) for rows in (source_rows, target_rows, relation_index, negative_rows)
    ]
    (bucket,) = kernel_call(
        bucket_body,
        [((BUCKET_ROWS, LANES), f32)],
        [edge_count, source_emb, source_state.reshape(1, -1)] + lists,
        scalars=1,
    )
    bucket = passed_along(bucket, "x", -1)
    spread = dealt(cargo, DOM, BLOCK)
    (spread,) = kernel_call(pick_body, [tile], [spread])
    arrived = dealt(spread, DOM, BLOCK)
    block = ((DIM, BLOCK), f32)
    line = ((1, BLOCK), f32)
    half = ((HALF_FLAT, LANES), f32)
    picks_r = ((NREL, SPAN), bf16)
    square = ((BLOCK, BLOCK), f32)
    source, source_acc, target, target_acc, keep, give = kernel_call(
        first_body,
        [block, line, block, line, half, half],
        [mine, arrived, bucket, relations],
        [WIDE] * 5 + [FLAT_TABLE],
        scalars=1,
    )
    subject, objects, pick_r, count = kernel_call(
        lookup_body, [WIDE, WIDE, picks_r, square], [source, target, bucket]
    )
    part = keep + passed_along(give, "core", 1)
    part = jnp.sum(exchange(part.reshape(4, 320, LANES), "x"), 0)
    part = jnp.sum(exchange(part.reshape(8, 40, LANES), "y"), 0)
    part = jnp.sum(gathered(part, "z"), 0)
    part = gathered(part, "y").reshape(320, LANES)
    part = gathered(part, "x").reshape(HALF_FLAT, LANES)
    other = passed_along(part, "core", 1)
    table = ((DIM, NREL), f32)
    types = ((1, NREL), f32)
    longer = ((HALF_FLAT + 64 * PIECE, LANES), f32)
    source, relations, relation_acc, keep, give = kernel_call(
        second_body,
        [((DIM + 8, BLOCK), f32), table, types, longer, longer],
        [mine, partner, part, other, source, source_acc, target, target_acc]
        + [relations, relation_state.reshape(1, -1), subject, objects, pick_r, count, bucket],
        [WIDE] * 4 + [FLAT_TABLE, turned],
        scalars=2,
    )
    got = passed_along(give, "core", 1)
    source = passed_along(source, "x", 1)
    part = keep[:HALF_FLAT] + got[:HALF_FLAT]
    received = exchange(part.reshape(4, 320, LANES), "x")
    packet = ((64 * ROWS, LANES), f32)
    (packed,) = kernel_call(merge_body, [packet], [received, keep, got])
    packed = packets(packed, ("z", "y"), 64)
    packed, source = lax.optimization_barrier((packed, source))
    (packed,) = kernel_call(middle_body, [packet], [mine, packed], [turned], scalars=1)
    packed = packets(packed, ("z", "y"), 64)
    pieces = ((64 * PIECE, LANES), f32)
    sums, returned, sibling = kernel_call(
        parting_body, [((4, 320, LANES), f32), pieces, pieces], [packed]
    )
    sibling = passed_along(sibling, "core", 1)
    part = exchange(sums, "x").reshape(HALF_FLAT, LANES)
    settled, settled_acc = kernel_call(
        settle_body, [block, line], [mine, returned, sibling], [turned], scalars=1
    )
    part, settled, settled_acc = lax.optimization_barrier((part, settled, settled_acc))
    other = passed_along(part, "core", 1)
    relations, relation_acc, source, source_acc = kernel_call(
        final_body,
        [table, types, block, line],
        [mine, part, other, relations, relation_acc, source],
        [((FLAT, LANES), f32)],
        scalars=1,
    )
    return (
        source,
        source_acc.reshape(-1),
        settled,
        settled_acc.reshape(-1),
        relations,
        relation_acc.reshape(-1),
    )


def solution(mesh):
    fine = Mesh(mesh.devices.reshape(8, 8, 2, 4), ALL)
    in_specs = (
        P(None, ALL),
        P(ALL),
        P(None, ALL),
        P(ALL),
        P(),
        P(),
        P(DOM, "x"),
        P(DOM, "x"),
        P(DOM, "x", None),
        P(DOM, "x", None),
        P(DOM, "x", None),
        P(DOM, "x", None),
    )
    out_specs = (P(None, ALL), P(ALL), P(None, ALL), P(ALL), P(), P())
    return jax.shard_map(local, mesh=fine, in_specs=in_specs, out_specs=out_specs, check_vma=False)
```

```python
import jax
import jax.numpy as jnp
from jax import lax
from jax.experimental import pallas as pl
from jax.experimental.pallas import tpu as pltpu
from jax.sharding import Mesh
from jax.sharding import PartitionSpec as P

DIM = 400
HALF = 200
NREL = 768
BLOCK = 128
SPAN = 512
NEG = 1024
LANES = 128
CHUNKS = NREL // LANES
FLAT = 2560
HALF_FLAT = FLAT // 2
PIECE = 4

ALL = ("z", "y", "core", "x")
DOM = ("z", "y", "core")

learn_rate = 0.3
epsilon = 1e-08

f32 = jnp.float32
bf16 = jnp.bfloat16


def passed_along(value, axis, steps):
    count = lax.axis_size(axis)
    pairs = [(source, (source + steps) % count) for source in range(count)]
    return lax.ppermute(value, axis, pairs)


def exchange(value, axis):
    return lax.all_to_all(value, axis, split_axis=0, concat_axis=0, tiled=True)


def dealt(value, axis, count):
    rows, lanes = value.shape
    return exchange(value.reshape(count, rows // count, lanes), axis).reshape(rows, lanes)


def packets(value, axis, count):
    rows, lanes = value.shape
    parts = rows // (count * PIECE)
    return exchange(value.reshape(count, parts, PIECE, lanes), axis).reshape(rows, lanes)


def gathered(value, axis):
    count = lax.axis_size(axis)
    return exchange(jnp.broadcast_to(value[None], (count,) + value.shape), axis)


def kernel_call(body, outs, args, scratch=(), scalars=0):
    specs = [pl.BlockSpec(memory_space=pltpu.SMEM)] * scalars
    specs += [pl.BlockSpec(memory_space=pltpu.VMEM)] * (len(args) - scalars)
    return pl.pallas_call(
        body,
        out_shape=[jax.ShapeDtypeStruct(shape, dtype) for shape, dtype in outs],
        in_specs=specs,
        out_specs=[pl.BlockSpec(memory_space=pltpu.VMEM)] * len(outs),
        scratch_shapes=[pltpu.VMEM(shape, dtype) for shape, dtype in scratch],
        compiler_params=pltpu.CompilerParams(vmem_limit_bytes=24 * 2**20),
    )(*args)


def dot(left, right):
    return lax.dot_general(left, right, (((1,), (0,)), ((), ())), preferred_element_type=f32)


def dot_last(left, right):
    return lax.dot_general(left, right, (((1,), (1,)), ((), ())), preferred_element_type=f32)


def moved(pick, value):
    upper = value.astype(bf16)
    rest = value - upper.astype(f32)
    middle = rest.astype(bf16)
    lower = (rest - middle.astype(f32)).astype(bf16)
    return (dot(pick, upper) + dot(pick, middle)) + dot(pick, lower)


def one_hot(count, rows):
    hit = lax.broadcasted_iota(jnp.int32, (count, rows.shape[1]), 0) == rows
    return jnp.where(hit, 1.0, 0.0).astype(bf16)


def sigmoid(value):
    return 1.0 / (1.0 + jnp.exp(-value))


def stepped(param, state, grad):
    new_state = state + jnp.sum(grad * grad, axis=0, keepdims=True) * (1.0 / DIM)
    return (param - learn_rate * grad / (jnp.sqrt(new_state) + epsilon), new_state)


def spaced(start, size, stride):
    return pl.ds(start, size, stride=stride)


def pack_body(dest_ref, state_ref, out_ref):
    for k in range(PIECE - 1):
        out_ref[spaced(k, BLOCK, PIECE), :] = dest_ref[LANES * k : LANES * (k + 1), :].T
    tail = dest_ref[LANES * (PIECE - 1) : DIM, :]
    state = jnp.broadcast_to(state_ref[...], (8, LANES))
    zero = jnp.zeros((LANES - tail.shape[0] - 8, LANES), f32)
    out_ref[spaced(PIECE - 1, BLOCK, PIECE), :] = jnp.concatenate([tail, state, zero], 0).T


def stamp_body(partner_ref, cargo_ref, out_ref):
    rows = spaced(PIECE - 1, BLOCK, PIECE)
    lane = lax.broadcasted_iota(jnp.int32, (BLOCK, LANES), 1)
    own = partner_ref[0, 0].astype(f32)
    out_ref[...] = cargo_ref[...]
    out_ref[rows, :] = jnp.where(lane == OWN_LANE, own, cargo_ref[rows, :])


STATE_ROW = DIM
LIVE_ROW = DIM + 1
LIST_ROWS = (DIM + 8, DIM + 16, DIM + 24, DIM + 32)
BUCKET_ROWS = DIM + 48


def bucket_body(live_ref, source_ref, state_ref, list_s, list_t, list_r, list_n, out_ref):
    out_ref[0:DIM, :] = source_ref[...]
    live = jnp.full((7, LANES), live_ref[0, 0].astype(f32))
    out_ref[DIM : DIM + 8, :] = jnp.concatenate([state_ref[...], live], 0)
    for first, ref in zip(LIST_ROWS, (list_s, list_t, list_r, list_n)):
        for k in range(ref.shape[1] // LANES):
            row = ref[:, LANES * k : LANES * (k + 1)].astype(f32)
            out_ref[first + k : first + k + 1, :] = row


def listed(bucket_ref, which, span):
    count = (NEG if which == 3 else SPAN) // LANES
    first = LIST_ROWS[which] + count * span
    rows = [bucket_ref[first + k : first + k + 1, :] for k in range(count)]
    return jnp.concatenate(rows, 1).astype(jnp.int32)


STATE_LANE = DIM - LANES * (PIECE - 1)
OWN_LANE = STATE_LANE + 8


def partner_pick(last):
    own = last[:, OWN_LANE : OWN_LANE + 1].astype(jnp.int32)
    lane = lax.broadcasted_iota(jnp.int32, (BLOCK, BLOCK), 1)
    return jnp.where(lane == own, 1.0, 0.0)


def pick_body(spread_ref, out_ref):
    last = spread_ref[spaced(PIECE - 1, BLOCK, PIECE), :]
    pick = partner_pick(last).astype(bf16)
    for k in range(PIECE - 1):
        rows = spaced(k, BLOCK, PIECE)
        out_ref[rows, :] = moved(pick, spread_ref[rows, :])
    out_ref[spaced(PIECE - 1, BLOCK, PIECE), :] = moved(pick, last)


def counted(rows_n):
    hits = lax.broadcasted_iota(jnp.int32, (BLOCK, NEG), 0) == rows_n
    count = jnp.sum(jnp.where(hits, 1.0, 0.0), axis=1, keepdims=True)
    return jnp.broadcast_to(count, (BLOCK, BLOCK))


def span_rows(i):
    re = pl.ds(pl.multiple_of(8 * i, 8), 8)
    im = pl.ds(pl.multiple_of(HALF + 8 * i, 8), 8)
    return re, im


HALF_CHUNKS = CHUNKS // 2
HALF_REL = NREL // 2


def flat_row(chunk):
    return HALF_FLAT * (chunk // HALF_CHUNKS) + DIM * (chunk % HALF_CHUNKS)


def half_update(grad_ref, param_of, state_of, out_ref, state_out):
    for k in range(HALF_CHUNKS):
        lanes = slice(LANES * k, LANES * (k + 1))
        grad = grad_ref[DIM * k : DIM * (k + 1), :]
        out_ref[:, lanes], state_out[:, lanes] = stepped(param_of(k), state_of(k), grad)


def chunk_reader(ref, which):
    def read(k):
        first = pl.multiple_of(which * HALF_REL + LANES * k, LANES)
        return ref[:, pl.ds(first, LANES)]

    return read


def static_reader(ref):
    return lambda k: ref[:, LANES * k : LANES * (k + 1)]


def gradients(
    first,
    bucket_ref,
    target,
    pick_r,
    count_wide,
    subject_ref,
    operator_ref,
    objects_ref,
    query_ref,
    slope_ref,
    flat_ref,
    grad_subject_ref,
):
    edge = lax.broadcasted_iota(jnp.int32, (1, SPAN), 1) + first
    live_count = bucket_ref[LIVE_ROW : LIVE_ROW + 1, :]
    live_count = jnp.concatenate([live_count] * (SPAN // LANES), 1).astype(jnp.int32)
    live = jnp.where(edge < live_count, 1.0, 0.0)
    target_bf = target.astype(bf16)

    def form(i, total):
        re, im = span_rows(i)
        subject_re, subject_im = (subject_ref[re, :], subject_ref[im, :])
        operator_re, operator_im = (operator_ref[re, :], operator_ref[im, :])
        query_re = subject_re * operator_re - subject_im * operator_im
        query_im = subject_re * operator_im + subject_im * operator_re
        query_ref[re, :] = query_re
        query_ref[im, :] = query_im
        return total + query_re * objects_ref[re, :] + query_im * objects_ref[im, :]

    total = lax.fori_loop(0, HALF // 8, form, jnp.zeros((8, SPAN), f32), unroll=5)
    positive = jnp.sum(total, axis=0, keepdims=True)
    query_bf = query_ref[...].astype(bf16)
    score = dot(target.T.astype(bf16), query_bf)
    grad_pos = -sigmoid(-positive) * live
    slope = (sigmoid(score) * (live * (1.0 / NEG))).astype(bf16)
    weighted = slope.astype(f32) * count_wide[:, 0:1]
    upper = weighted.astype(bf16)
    lower = (weighted - upper.astype(f32)).astype(bf16)
    slope_ref[...] = dot(target_bf, upper) + dot(target_bf, lower)
    noise = dot_last(query_bf, slope).astype(bf16).astype(f32) * count_wide.T[0:1, :]

    def push(i, _):
        re, im = span_rows(i)
        query_gre = grad_pos * objects_ref[re, :] + slope_ref[re, :]
        query_gim = grad_pos * objects_ref[im, :] + slope_ref[im, :]
        subject_re, subject_im = (subject_ref[re, :], subject_ref[im, :])
        operator_re, operator_im = (operator_ref[re, :], operator_ref[im, :])
        grad_subject_ref[re, :] = query_gre * operator_re + query_gim * operator_im
        grad_subject_ref[im, :] = query_gim * operator_re - query_gre * operator_im
        operator_ref[re, :] = query_gre * subject_re + query_gim * subject_im
        operator_ref[im, :] = query_gim * subject_re - query_gre * subject_im
        query_ref[re, :] = grad_pos * query_ref[re, :]
        query_ref[im, :] = grad_pos * query_ref[im, :]
        return 0

    lax.fori_loop(0, HALF // 8, push, 0, unroll=5)
    grad_operator = operator_ref[...].astype(bf16)
    for k in range(0, CHUNKS, 2):
        pair = dot_last(grad_operator, pick_r[LANES * k : LANES * (k + 2), :])
        for c in range(2):
            first = flat_row(k + c)
            flat_ref[first : first + DIM, :] = pair[:, LANES * c : LANES * (c + 1)]
    rest = HALF_FLAT - DIM * HALF_CHUNKS
    for h in range(1, 3):
        flat_ref[HALF_FLAT * h - rest : HALF_FLAT * h, :] = jnp.zeros((rest, LANES), f32)
    return noise


WIDE = ((DIM, SPAN), f32)
FLAT_TABLE = ((FLAT, LANES), f32)


def halves(mine, flat_ref, keep_ref, give_ref):
    keep_ref[0:HALF_FLAT, :] = flat_ref[pl.ds(pl.multiple_of(mine * HALF_FLAT, 8), HALF_FLAT), :]
    give_ref[0:HALF_FLAT, :] = flat_ref[
        pl.ds(pl.multiple_of((1 - mine) * HALF_FLAT, 8), HALF_FLAT), :
    ]


def first_body(
    mine_ref,
    arrived_ref,
    bucket_ref,
    relations_ref,
    grad_subject_ref,
    query_ref,
    target_out,
    target_state_out,
    noise_out,
    keep_out,
    give_out,
    subject_ref,
    operator_ref,
    objects_ref,
    slope_ref,
    flat_ref,
):
    last = arrived_ref[spaced(PIECE - 1, BLOCK, PIECE), :].T
    target = jnp.concatenate(
        [arrived_ref[spaced(k, BLOCK, PIECE), :].T for k in range(PIECE - 1)]
        + [last[:STATE_LANE, :]],
        0,
    )
    source = bucket_ref[0:DIM, :]
    pick_s = one_hot(BLOCK, listed(bucket_ref, 0, 0))
    pick_t = one_hot(BLOCK, listed(bucket_ref, 1, 0))
    pick_r = one_hot(NREL, listed(bucket_ref, 2, 0))
    subject_ref[...] = dot(source.astype(bf16), pick_s)
    operator_ref[...] = dot(relations_ref[...].astype(bf16), pick_r)
    objects_ref[...] = dot(target.astype(bf16), pick_t)
    noise_out[...] = gradients(
        0,
        bucket_ref,
        target,
        pick_r,
        counted(listed(bucket_ref, 3, 0)),
        subject_ref,
        operator_ref,
        objects_ref,
        query_ref,
        slope_ref,
        flat_ref,
        grad_subject_ref,
    )
    halves(mine_ref[0, 0], flat_ref, keep_out, give_out)
    target_out[...] = target
    target_state_out[...] = last[STATE_LANE : STATE_LANE + 1, :]


def update_body(
    bucket_ref,
    grad_subject_ref,
    grad_objects_ref,
    target_ref,
    target_state_ref,
    noise_ref,
    source_out,
    source_state_out,
    target_out,
    target_state_out,
):
    pick_s = one_hot(BLOCK, listed(bucket_ref, 0, 0))
    pick_t = one_hot(BLOCK, listed(bucket_ref, 1, 0))
    grad_source = dot_last(grad_subject_ref[...].astype(bf16), pick_s)
    source_out[...], source_state_out[...] = stepped(
        bucket_ref[0:DIM, :], bucket_ref[STATE_ROW : STATE_ROW + 1, :], grad_source
    )
    grad_target = dot_last(grad_objects_ref[...].astype(bf16), pick_t) + noise_ref[...]
    target_out[...], target_state_out[...] = stepped(
        target_ref[...], target_state_ref[...], grad_target
    )


def last_source_body(bucket_ref, grad_subject_ref, source_ref, source_state_ref, source_out):
    pick_s = one_hot(BLOCK, listed(bucket_ref, 0, 1))
    grad_source = dot_last(grad_subject_ref[...].astype(bf16), pick_s)
    source, source_state = stepped(source_ref[...], source_state_ref[...], grad_source)
    source_out[0:DIM, :] = source
    source_out[DIM : DIM + 8, :] = jnp.broadcast_to(source_state, (8, LANES))


def lookup_body(
    mine_ref,
    part_ref,
    relations_ref,
    relation_state_ref,
    source_ref,
    target_ref,
    bucket_ref,
    subject_ref,
    objects_ref,
    pick_r_ref,
    count_ref,
    own_ref,
    own_state_ref,
):
    mine = mine_ref[0, 0]
    half_update(
        part_ref,
        chunk_reader(relations_ref, mine),
        chunk_reader(relation_state_ref, mine),
        own_ref,
        own_state_ref,
    )
    pick_s = one_hot(BLOCK, listed(bucket_ref, 0, 1))
    pick_t = one_hot(BLOCK, listed(bucket_ref, 1, 1))
    subject_ref[...] = dot(source_ref[...].astype(bf16), pick_s)
    objects_ref[...] = dot(target_ref[...].astype(bf16), pick_t)
    pick_r_ref[...] = one_hot(NREL, listed(bucket_ref, 2, 1))
    count_ref[...] = counted(listed(bucket_ref, 3, 1))


def second_body(
    mine_ref,
    partner_ref,
    own_ref,
    other_ref,
    target_ref,
    target_state_ref,
    relations_ref,
    relation_state_ref,
    first_subject_ref,
    objects_ref,
    pick_r_ref,
    count_ref,
    bucket_ref,
    subject_ref,
    far_out,
    far_state_out,
    keep_out,
    give_out,
    operator_ref,
    query_ref,
    slope_ref,
    flat_ref,
    turned_ref,
):
    mine = mine_ref[0, 0]
    half_update(
        other_ref,
        chunk_reader(relations_ref, 1 - mine),
        chunk_reader(relation_state_ref, 1 - mine),
        far_out,
        far_state_out,
    )
    near_rows = pl.ds(pl.multiple_of(mine * HALF_REL, LANES), HALF_REL)
    far_rows = pl.ds(pl.multiple_of((1 - mine) * HALF_REL, LANES), HALF_REL)
    operator_ref[...] = dot(own_ref[...].astype(bf16), pick_r_ref[near_rows, :]) + dot(
        far_out[...].astype(bf16), pick_r_ref[far_rows, :]
    )
    target = target_ref[...]
    noise = gradients(
        SPAN,
        bucket_ref,
        target,
        pick_r_ref[...],
        count_ref[...],
        first_subject_ref,
        operator_ref,
        objects_ref,
        query_ref,
        slope_ref,
        flat_ref,
        subject_ref,
    )
    halves(mine, flat_ref, keep_out, give_out)
    pick_t = one_hot(BLOCK, listed(bucket_ref, 1, 1))
    grad_target = dot_last(query_ref[...].astype(bf16), pick_t) + noise
    target, target_state = stepped(target, target_state_ref[...], grad_target)
    for k in range(PIECE):
        if k < PIECE - 1:
            turned_ref[...] = target[LANES * k : LANES * (k + 1), :].T
        else:
            state = jnp.broadcast_to(target_state, (8, LANES))
            own = jnp.full((8, LANES), partner_ref[0, 0].astype(f32))
            zero = jnp.zeros((LANES // 2 - STATE_LANE - 16, LANES), f32)
            tail = [target[LANES * k : DIM, :], state, own, zero]
            turned_ref[...] = jnp.concatenate(tail + tail, 0).T
        rows = slice(HALF_FLAT + 64 * k, HALF_FLAT + 64 * (k + 1))
        keep_out[rows, :] = turned_ref[spaced(mine, 64, 2), :]
        give_out[rows, :] = turned_ref[spaced(1 - mine, 64, 2), :]


FULL = PIECE - 1
TAIL = 2 * FULL
SUM_ROW = TAIL + 1
SUM_ROWS = 5
ROWS = SUM_ROW + SUM_ROWS


def low_lanes(shape):
    return lax.broadcasted_iota(jnp.int32, shape, 1) < LANES // 2


def swapped(value):
    return pltpu.roll(value, LANES // 2, 1)


def merge_body(received_ref, keep_ref, got_ref, out_ref):
    for k in range(FULL):
        rows = slice(HALF_FLAT + 64 * k, HALF_FLAT + 64 * (k + 1))
        out_ref[spaced(k, 64, ROWS), :] = keep_ref[rows, :]
        out_ref[spaced(FULL + k, 64, ROWS), :] = got_ref[rows, :]
    rows = slice(HALF_FLAT + 64 * FULL, HALF_FLAT + 64 * PIECE)
    out_ref[spaced(TAIL, 64, ROWS), :] = jnp.where(
        low_lanes((64, LANES)), keep_ref[rows, :], got_ref[rows, :]
    )
    for k in range(SUM_ROWS):
        rows = slice(64 * k, 64 * (k + 1))
        total = received_ref[0, rows, :] + received_ref[1, rows, :]
        total = total + received_ref[2, rows, :] + received_ref[3, rows, :]
        out_ref[spaced(SUM_ROW + k, 64, ROWS), :] = total


def middle_body(mine_ref, received_ref, out_ref, turned_ref):
    mine = mine_ref[0, 0]
    here, there = (spaced(mine, 64, 2), spaced(1 - mine, 64, 2))
    tail = received_ref[spaced(TAIL, 64, ROWS), :]
    turned_ref[here, :] = tail
    turned_ref[there, :] = swapped(tail)
    back = partner_pick(turned_ref[...]).T.astype(bf16)
    turned_ref[...] = moved(back, turned_ref[...])
    out_ref[spaced(TAIL, 64, ROWS), :] = jnp.where(
        low_lanes((64, LANES)), turned_ref[here, :], swapped(turned_ref[there, :])
    )
    for k in range(FULL):
        turned_ref[here, :] = received_ref[spaced(k, 64, ROWS), :]
        turned_ref[there, :] = received_ref[spaced(FULL + k, 64, ROWS), :]
        turned_ref[...] = moved(back, turned_ref[...])
        out_ref[spaced(k, 64, ROWS), :] = turned_ref[here, :]
        out_ref[spaced(FULL + k, 64, ROWS), :] = turned_ref[there, :]
    for k in range(SUM_ROW, ROWS):
        total = jnp.sum(received_ref[spaced(k, 64, ROWS), :], axis=0, keepdims=True)
        out_ref[spaced(k, 64, ROWS), :] = jnp.broadcast_to(total, (64, LANES))


def parting_body(received_ref, sums_ref, block_ref, give_ref):
    for k in range(FULL):
        rows = slice(64 * k, 64 * (k + 1))
        block_ref[rows, :] = received_ref[spaced(k, 64, ROWS), :]
        give_ref[rows, :] = received_ref[spaced(FULL + k, 64, ROWS), :]
    tail = received_ref[spaced(TAIL, 64, ROWS), :]
    block_ref[64 * FULL :, :] = tail
    give_ref[64 * FULL :, :] = swapped(tail)
    for k in range(SUM_ROWS):
        rows = received_ref[spaced(SUM_ROW + k, 64, ROWS), :]
        for x in range(4):
            sums_ref[x, 64 * k : 64 * (k + 1), :] = rows


def settle_body(mine_ref, block_ref, other_ref, out_ref, state_out, turned_ref):
    mine = mine_ref[0, 0]
    for k in range(PIECE):
        rows = slice(64 * k, 64 * (k + 1))
        turned_ref[spaced(mine, 64, 2), :] = block_ref[rows, :]
        turned_ref[spaced(1 - mine, 64, 2), :] = other_ref[rows, :]
        turned = turned_ref[...].T
        if k < PIECE - 1:
            out_ref[LANES * k : LANES * (k + 1), :] = turned
        else:
            out_ref[LANES * k : DIM, :] = turned[:STATE_LANE, :]
            state_out[...] = turned[STATE_LANE : STATE_LANE + 1, :]


def near_body(part_ref, near_ref, near_state_ref, out_ref, state_out):
    half_update(
        part_ref, static_reader(near_ref), static_reader(near_state_ref), out_ref, state_out
    )


def final_body(
    mine_ref,
    near_ref,
    near_state_ref,
    other_ref,
    far_ref,
    far_state_ref,
    source_ref,
    out_ref,
    state_out,
    source_out,
    source_state_out,
):
    source_out[...] = source_ref[0:DIM, :]
    source_state_out[...] = source_ref[DIM : DIM + 1, :]
    mine = mine_ref[0, 0]
    for k in range(HALF_CHUNKS):
        lanes = slice(LANES * k, LANES * (k + 1))
        near = pl.ds(pl.multiple_of(mine * HALF_REL + LANES * k, LANES), LANES)
        far = pl.ds(pl.multiple_of((1 - mine) * HALF_REL + LANES * k, LANES), LANES)
        out_ref[:, near] = near_ref[:, lanes]
        state_out[:, near] = near_state_ref[:, lanes]
        grad = other_ref[DIM * k : DIM * (k + 1), :]
        out_ref[:, far], state_out[:, far] = stepped(
            far_ref[:, lanes], far_state_ref[:, lanes], grad
        )


def local(
    source_emb,
    source_state,
    dest_emb,
    dest_state,
    relations,
    relation_state,
    partner,
    edge_count,
    source_rows,
    target_rows,
    relation_index,
    negative_rows,
):
    mine = lax.axis_index("core").astype(jnp.int32).reshape(1, 1)
    turned = ((BLOCK, LANES), f32)
    partner = passed_along(partner, "x", -1)
    tile = ((BLOCK * PIECE, LANES), f32)
    (cargo,) = kernel_call(pack_body, [tile], [dest_emb, dest_state.reshape(1, -1)])
    (cargo,) = kernel_call(stamp_body, [tile], [partner, cargo], scalars=1)
    lists = [
        rows.reshape(1, -1) for rows in (source_rows, target_rows, relation_index, negative_rows)
    ]
    (bucket,) = kernel_call(
        bucket_body,
        [((BUCKET_ROWS, LANES), f32)],
        [edge_count, source_emb, source_state.reshape(1, -1)] + lists,
        scalars=1,
    )
    bucket = passed_along(bucket, "x", -1)
    spread = dealt(cargo, DOM, BLOCK)
    (spread,) = kernel_call(pick_body, [tile], [spread])
    arrived = dealt(spread, DOM, BLOCK)
    block = ((DIM, BLOCK), f32)
    line = ((1, BLOCK), f32)
    half = ((HALF_FLAT, LANES), f32)
    picks_r = ((NREL, SPAN), bf16)
    square = ((BLOCK, BLOCK), f32)
    half_table = ((DIM, HALF_REL), f32)
    half_types = ((1, HALF_REL), f32)
    relation_acc = relation_state.reshape(1, -1)
    grad_subject, grad_objects, target, target_acc, noise, keep, give = kernel_call(
        first_body,
        [WIDE, WIDE, block, line, block, half, half],
        [mine, arrived, bucket, relations],
        [WIDE] * 4 + [FLAT_TABLE],
        scalars=1,
    )
    source, source_acc, target, target_acc = kernel_call(
        update_body,
        [block, line, block, line],
        [bucket, grad_subject, grad_objects, target, target_acc, noise],
    )
    got, source, source_acc, target, target_acc = lax.optimization_barrier(
        (passed_along(give, "core", 1), source, source_acc, target, target_acc)
    )
    part = keep + got
    part = jnp.sum(exchange(part.reshape(4, 320, LANES), "x"), 0)
    part = jnp.sum(exchange(part.reshape(8, 40, LANES), "y"), 0)
    part = jnp.sum(gathered(part, "z"), 0)
    part = gathered(part, "y").reshape(320, LANES)
    part = gathered(part, "x").reshape(HALF_FLAT, LANES)
    other = passed_along(part, "core", 1)
    subject, objects, pick_r, count, near, near_acc = kernel_call(
        lookup_body,
        [WIDE, WIDE, picks_r, square, half_table, half_types],
        [mine, part, relations, relation_acc, source, target, bucket],
        scalars=1,
    )
    table = ((DIM, NREL), f32)
    types = ((1, NREL), f32)
    longer = ((HALF_FLAT + 64 * PIECE, LANES), f32)
    grad_subject, far, far_acc, keep, give = kernel_call(
        second_body,
        [WIDE, half_table, half_types, longer, longer],
        [mine, partner, near, other, target, target_acc, relations, relation_acc]
        + [subject, objects, pick_r, count, bucket],
        [WIDE] * 3 + [FLAT_TABLE, turned],
        scalars=2,
    )
    (source,) = kernel_call(
        last_source_body,
        [((DIM + 8, BLOCK), f32)],
        [bucket, grad_subject, source, source_acc],
    )
    got, source = lax.optimization_barrier((passed_along(give, "core", 1), source))
    source = passed_along(source, "x", 1)
    part = keep[:HALF_FLAT] + got[:HALF_FLAT]
    received = exchange(part.reshape(4, 320, LANES), "x")
    packet = ((64 * ROWS, LANES), f32)
    (packed,) = kernel_call(merge_body, [packet], [received, keep, got])
    packed = packets(packed, ("z", "y"), 64)
    packed, source = lax.optimization_barrier((packed, source))
    (packed,) = kernel_call(middle_body, [packet], [mine, packed], [turned], scalars=1)
    packed = packets(packed, ("z", "y"), 64)
    pieces = ((64 * PIECE, LANES), f32)
    sums, returned, sibling = kernel_call(
        parting_body, [((4, 320, LANES), f32), pieces, pieces], [packed]
    )
    sibling = passed_along(sibling, "core", 1)
    part = exchange(sums, "x").reshape(HALF_FLAT, LANES)
    settled, settled_acc = kernel_call(
        settle_body, [block, line], [mine, returned, sibling], [turned], scalars=1
    )
    part, settled, settled_acc = lax.optimization_barrier((part, settled, settled_acc))
    other = passed_along(part, "core", 1)
    near, near_acc = kernel_call(near_body, [half_table, half_types], [part, near, near_acc])
    relations, relation_acc, source, source_acc = kernel_call(
        final_body,
        [table, types, block, line],
        [mine, near, near_acc, other, far, far_acc, source],
        scalars=1,
    )
    return (
        source,
        source_acc.reshape(-1),
        settled,
        settled_acc.reshape(-1),
        relations,
        relation_acc.reshape(-1),
    )


def solution(mesh):
    fine = Mesh(mesh.devices.reshape(8, 8, 2, 4), ALL)
    in_specs = (
        P(None, ALL),
        P(ALL),
        P(None, ALL),
        P(ALL),
        P(),
        P(),
        P(DOM, "x"),
        P(DOM, "x"),
        P(DOM, "x", None),
        P(DOM, "x", None),
        P(DOM, "x", None),
        P(DOM, "x", None),
    )
    out_specs = (P(None, ALL), P(ALL), P(None, ALL), P(ALL), P(), P())
    return jax.shard_map(local, mesh=fine, in_specs=in_specs, out_specs=out_specs, check_vma=False)
```

```python
import jax
import jax.numpy as jnp
from jax import lax
from jax.experimental import pallas as pl
from jax.experimental.pallas import tpu as pltpu
from jax.sharding import Mesh
from jax.sharding import PartitionSpec as P

DIM = 400
HALF = 200
NREL = 768
BLOCK = 128
SPAN = 512
NEG = 1024
LANES = 128
CHUNKS = NREL // LANES
FLAT = 2560
HALF_FLAT = FLAT // 2
PIECE = 4

ALL = ("z", "y", "core", "x")
DOM = ("z", "y", "core")

learn_rate = 0.3
epsilon = 1e-08

f32 = jnp.float32
bf16 = jnp.bfloat16


def passed_along(value, axis, steps):
    count = lax.axis_size(axis)
    pairs = [(source, (source + steps) % count) for source in range(count)]
    return lax.ppermute(value, axis, pairs)


def exchange(value, axis):
    return lax.all_to_all(value, axis, split_axis=0, concat_axis=0, tiled=True)


def dealt(value, axis, count):
    rows, lanes = value.shape
    return exchange(value.reshape(count, rows // count, lanes), axis).reshape(rows, lanes)


def packets(value, axis, count):
    rows, lanes = value.shape
    parts = rows // (count * PIECE)
    return exchange(value.reshape(count, parts, PIECE, lanes), axis).reshape(rows, lanes)


def gathered(value, axis):
    count = lax.axis_size(axis)
    return exchange(jnp.broadcast_to(value[None], (count,) + value.shape), axis)


def kernel_call(body, outs, args, scratch=(), scalars=0):
    specs = [pl.BlockSpec(memory_space=pltpu.SMEM)] * scalars
    specs += [pl.BlockSpec(memory_space=pltpu.VMEM)] * (len(args) - scalars)
    return pl.pallas_call(
        body,
        out_shape=[jax.ShapeDtypeStruct(shape, dtype) for shape, dtype in outs],
        in_specs=specs,
        out_specs=[pl.BlockSpec(memory_space=pltpu.VMEM)] * len(outs),
        scratch_shapes=[pltpu.VMEM(shape, dtype) for shape, dtype in scratch],
        compiler_params=pltpu.CompilerParams(vmem_limit_bytes=24 * 2**20),
    )(*args)


def dot(left, right):
    return lax.dot_general(left, right, (((1,), (0,)), ((), ())), preferred_element_type=f32)


def dot_last(left, right):
    return lax.dot_general(left, right, (((1,), (1,)), ((), ())), preferred_element_type=f32)


def moved(pick, value):
    upper = value.astype(bf16)
    rest = value - upper.astype(f32)
    middle = rest.astype(bf16)
    lower = (rest - middle.astype(f32)).astype(bf16)
    return (dot(pick, upper) + dot(pick, middle)) + dot(pick, lower)


def one_hot(count, rows):
    hit = lax.broadcasted_iota(jnp.int32, (count, rows.shape[1]), 0) == rows
    return jnp.where(hit, 1.0, 0.0).astype(bf16)


def sigmoid(value):
    return 1.0 / (1.0 + jnp.exp(-value))


def stepped(param, state, grad):
    new_state = state + jnp.sum(grad * grad, axis=0, keepdims=True) * (1.0 / DIM)
    return (param - learn_rate * grad / (jnp.sqrt(new_state) + epsilon), new_state)


def spaced(start, size, stride):
    return pl.ds(start, size, stride=stride)


def pack_body(dest_ref, state_ref, out_ref):
    for k in range(PIECE - 1):
        out_ref[spaced(k, BLOCK, PIECE), :] = dest_ref[LANES * k : LANES * (k + 1), :].T
    tail = dest_ref[LANES * (PIECE - 1) : DIM, :]
    state = jnp.broadcast_to(state_ref[...], (8, LANES))
    zero = jnp.zeros((LANES - tail.shape[0] - 8, LANES), f32)
    out_ref[spaced(PIECE - 1, BLOCK, PIECE), :] = jnp.concatenate([tail, state, zero], 0).T


def stamp_body(partner_ref, cargo_ref, out_ref):
    rows = spaced(PIECE - 1, BLOCK, PIECE)
    lane = lax.broadcasted_iota(jnp.int32, (BLOCK, LANES), 1)
    own = partner_ref[0, 0].astype(f32)
    out_ref[...] = cargo_ref[...]
    out_ref[rows, :] = jnp.where(lane == OWN_LANE, own, cargo_ref[rows, :])


STATE_ROW = DIM
LIVE_ROW = DIM + 1
LIST_ROWS = (DIM + 8, DIM + 16, DIM + 24, DIM + 32)
BUCKET_ROWS = DIM + 48


def bucket_body(live_ref, source_ref, state_ref, list_s, list_t, list_r, list_n, out_ref):
    out_ref[0:DIM, :] = source_ref[...]
    live = jnp.full((7, LANES), live_ref[0, 0].astype(f32))
    out_ref[DIM : DIM + 8, :] = jnp.concatenate([state_ref[...], live], 0)
    for first, ref in zip(LIST_ROWS, (list_s, list_t, list_r, list_n)):
        for k in range(ref.shape[1] // LANES):
            row = ref[:, LANES * k : LANES * (k + 1)].astype(f32)
            out_ref[first + k : first + k + 1, :] = row


def listed(bucket_ref, which, span):
    count = (NEG if which == 3 else SPAN) // LANES
    first = LIST_ROWS[which] + count * span
    rows = [bucket_ref[first + k : first + k + 1, :] for k in range(count)]
    return jnp.concatenate(rows, 1).astype(jnp.int32)


STATE_LANE = DIM - LANES * (PIECE - 1)
OWN_LANE = STATE_LANE + 8


def partner_pick(last):
    own = last[:, OWN_LANE : OWN_LANE + 1].astype(jnp.int32)
    lane = lax.broadcasted_iota(jnp.int32, (BLOCK, BLOCK), 1)
    return jnp.where(lane == own, 1.0, 0.0)


def pick_body(spread_ref, out_ref):
    last = spread_ref[spaced(PIECE - 1, BLOCK, PIECE), :]
    pick = partner_pick(last).astype(bf16)
    for k in range(PIECE - 1):
        rows = spaced(k, BLOCK, PIECE)
        out_ref[rows, :] = moved(pick, spread_ref[rows, :])
    out_ref[spaced(PIECE - 1, BLOCK, PIECE), :] = moved(pick, last)


def counted(rows_n):
    hits = lax.broadcasted_iota(jnp.int32, (BLOCK, NEG), 0) == rows_n
    count = jnp.sum(jnp.where(hits, 1.0, 0.0), axis=1, keepdims=True)
    return jnp.broadcast_to(count, (BLOCK, BLOCK))


def span_rows(i):
    re = pl.ds(pl.multiple_of(8 * i, 8), 8)
    im = pl.ds(pl.multiple_of(HALF + 8 * i, 8), 8)
    return re, im


HALF_CHUNKS = CHUNKS // 2
HALF_REL = NREL // 2


def flat_row(chunk):
    return HALF_FLAT * (chunk // HALF_CHUNKS) + DIM * (chunk % HALF_CHUNKS)


def half_update(grad_ref, param_of, state_of, out_ref, state_out):
    for k in range(HALF_CHUNKS):
        lanes = slice(LANES * k, LANES * (k + 1))
        grad = grad_ref[DIM * k : DIM * (k + 1), :]
        out_ref[:, lanes], state_out[:, lanes] = stepped(param_of(k), state_of(k), grad)


def chunk_reader(ref, which):
    def read(k):
        first = pl.multiple_of(which * HALF_REL + LANES * k, LANES)
        return ref[:, pl.ds(first, LANES)]

    return read


def static_reader(ref):
    return lambda k: ref[:, LANES * k : LANES * (k + 1)]


def gradients(
    first,
    bucket_ref,
    target,
    pick_r,
    count_wide,
    subject_ref,
    operator_ref,
    objects_ref,
    query_ref,
    slope_ref,
    flat_ref,
    grad_subject_ref,
):
    edge = lax.broadcasted_iota(jnp.int32, (1, SPAN), 1) + first
    live_count = bucket_ref[LIVE_ROW : LIVE_ROW + 1, :]
    live_count = jnp.concatenate([live_count] * (SPAN // LANES), 1).astype(jnp.int32)
    live = jnp.where(edge < live_count, 1.0, 0.0)
    target_bf = target.astype(bf16)

    def form(i, total):
        re, im = span_rows(i)
        subject_re, subject_im = (subject_ref[re, :], subject_ref[im, :])
        operator_re, operator_im = (operator_ref[re, :], operator_ref[im, :])
        query_re = subject_re * operator_re - subject_im * operator_im
        query_im = subject_re * operator_im + subject_im * operator_re
        query_ref[re, :] = query_re
        query_ref[im, :] = query_im
        return total + query_re * objects_ref[re, :] + query_im * objects_ref[im, :]

    total = lax.fori_loop(0, HALF // 8, form, jnp.zeros((8, SPAN), f32), unroll=5)
    positive = jnp.sum(total, axis=0, keepdims=True)
    query_bf = query_ref[...].astype(bf16)
    score = dot(target.T.astype(bf16), query_bf)
    grad_pos = -sigmoid(-positive) * live
    slope = (sigmoid(score) * (live * (1.0 / NEG))).astype(bf16)
    weighted = slope.astype(f32) * count_wide[:, 0:1]
    upper = weighted.astype(bf16)
    lower = (weighted - upper.astype(f32)).astype(bf16)
    slope_ref[...] = dot(target_bf, upper) + dot(target_bf, lower)
    noise = dot_last(query_bf, slope).astype(bf16).astype(f32) * count_wide.T[0:1, :]

    def push(i, _):
        re, im = span_rows(i)
        query_gre = grad_pos * objects_ref[re, :] + slope_ref[re, :]
        query_gim = grad_pos * objects_ref[im, :] + slope_ref[im, :]
        subject_re, subject_im = (subject_ref[re, :], subject_ref[im, :])
        operator_re, operator_im = (operator_ref[re, :], operator_ref[im, :])
        grad_subject_ref[re, :] = query_gre * operator_re + query_gim * operator_im
        grad_subject_ref[im, :] = query_gim * operator_re - query_gre * operator_im
        operator_ref[re, :] = query_gre * subject_re + query_gim * subject_im
        operator_ref[im, :] = query_gim * subject_re - query_gre * subject_im
        query_ref[re, :] = grad_pos * query_ref[re, :]
        query_ref[im, :] = grad_pos * query_ref[im, :]
        return 0

    lax.fori_loop(0, HALF // 8, push, 0, unroll=5)
    grad_operator = operator_ref[...].astype(bf16)
    for k in range(0, CHUNKS, 2):
        pair = dot_last(grad_operator, pick_r[LANES * k : LANES * (k + 2), :])
        for c in range(2):
            first = flat_row(k + c)
            flat_ref[first : first + DIM, :] = pair[:, LANES * c : LANES * (c + 1)]
    rest = HALF_FLAT - DIM * HALF_CHUNKS
    for h in range(1, 3):
        flat_ref[HALF_FLAT * h - rest : HALF_FLAT * h, :] = jnp.zeros((rest, LANES), f32)
    return noise


WIDE = ((DIM, SPAN), f32)
FLAT_TABLE = ((FLAT, LANES), f32)


def halves(mine, flat_ref, keep_ref, give_ref):
    keep_ref[0:HALF_FLAT, :] = flat_ref[pl.ds(pl.multiple_of(mine * HALF_FLAT, 8), HALF_FLAT), :]
    give_ref[0:HALF_FLAT, :] = flat_ref[
        pl.ds(pl.multiple_of((1 - mine) * HALF_FLAT, 8), HALF_FLAT), :
    ]


def first_body(
    mine_ref,
    arrived_ref,
    bucket_ref,
    relations_ref,
    grad_subject_ref,
    query_ref,
    target_out,
    target_state_out,
    noise_out,
    keep_out,
    give_out,
    subject_ref,
    operator_ref,
    objects_ref,
    slope_ref,
    flat_ref,
):
    last = arrived_ref[spaced(PIECE - 1, BLOCK, PIECE), :].T
    target = jnp.concatenate(
        [arrived_ref[spaced(k, BLOCK, PIECE), :].T for k in range(PIECE - 1)]
        + [last[:STATE_LANE, :]],
        0,
    )
    source = bucket_ref[0:DIM, :]
    pick_s = one_hot(BLOCK, listed(bucket_ref, 0, 0))
    pick_t = one_hot(BLOCK, listed(bucket_ref, 1, 0))
    pick_r = one_hot(NREL, listed(bucket_ref, 2, 0))
    subject_ref[...] = dot(source.astype(bf16), pick_s)
    operator_ref[...] = dot(relations_ref[...].astype(bf16), pick_r)
    objects_ref[...] = dot(target.astype(bf16), pick_t)
    noise_out[...] = gradients(
        0,
        bucket_ref,
        target,
        pick_r,
        counted(listed(bucket_ref, 3, 0)),
        subject_ref,
        operator_ref,
        objects_ref,
        query_ref,
        slope_ref,
        flat_ref,
        grad_subject_ref,
    )
    halves(mine_ref[0, 0], flat_ref, keep_out, give_out)
    target_out[...] = target
    target_state_out[...] = last[STATE_LANE : STATE_LANE + 1, :]


def update_body(
    bucket_ref,
    grad_subject_ref,
    grad_objects_ref,
    target_ref,
    target_state_ref,
    noise_ref,
    source_out,
    source_state_out,
    target_out,
    target_state_out,
):
    pick_s = one_hot(BLOCK, listed(bucket_ref, 0, 0))
    pick_t = one_hot(BLOCK, listed(bucket_ref, 1, 0))
    grad_source = dot_last(grad_subject_ref[...].astype(bf16), pick_s)
    source_out[...], source_state_out[...] = stepped(
        bucket_ref[0:DIM, :], bucket_ref[STATE_ROW : STATE_ROW + 1, :], grad_source
    )
    grad_target = dot_last(grad_objects_ref[...].astype(bf16), pick_t) + noise_ref[...]
    target_out[...], target_state_out[...] = stepped(
        target_ref[...], target_state_ref[...], grad_target
    )


def last_source_body(bucket_ref, grad_subject_ref, source_ref, source_state_ref, source_out):
    pick_s = one_hot(BLOCK, listed(bucket_ref, 0, 1))
    grad_source = dot_last(grad_subject_ref[...].astype(bf16), pick_s)
    source, source_state = stepped(source_ref[...], source_state_ref[...], grad_source)
    source_out[0:DIM, :] = source
    source_out[DIM : DIM + 8, :] = jnp.broadcast_to(source_state, (8, LANES))


def lookup_body(
    mine_ref,
    part_ref,
    relations_ref,
    relation_state_ref,
    source_ref,
    target_ref,
    bucket_ref,
    subject_ref,
    objects_ref,
    pick_r_ref,
    count_ref,
    own_ref,
    own_state_ref,
):
    mine = mine_ref[0, 0]
    half_update(
        part_ref,
        chunk_reader(relations_ref, mine),
        chunk_reader(relation_state_ref, mine),
        own_ref,
        own_state_ref,
    )
    pick_s = one_hot(BLOCK, listed(bucket_ref, 0, 1))
    pick_t = one_hot(BLOCK, listed(bucket_ref, 1, 1))
    subject_ref[...] = dot(source_ref[...].astype(bf16), pick_s)
    objects_ref[...] = dot(target_ref[...].astype(bf16), pick_t)
    pick_r_ref[...] = one_hot(NREL, listed(bucket_ref, 2, 1))
    count_ref[...] = counted(listed(bucket_ref, 3, 1))


def second_body(
    mine_ref,
    partner_ref,
    own_ref,
    other_ref,
    target_ref,
    target_state_ref,
    relations_ref,
    relation_state_ref,
    first_subject_ref,
    objects_ref,
    pick_r_ref,
    count_ref,
    bucket_ref,
    subject_ref,
    far_out,
    far_state_out,
    keep_out,
    give_out,
    operator_ref,
    query_ref,
    slope_ref,
    flat_ref,
    turned_ref,
):
    mine = mine_ref[0, 0]
    half_update(
        other_ref,
        chunk_reader(relations_ref, 1 - mine),
        chunk_reader(relation_state_ref, 1 - mine),
        far_out,
        far_state_out,
    )
    near_rows = pl.ds(pl.multiple_of(mine * HALF_REL, LANES), HALF_REL)
    far_rows = pl.ds(pl.multiple_of((1 - mine) * HALF_REL, LANES), HALF_REL)
    operator_ref[...] = dot(own_ref[...].astype(bf16), pick_r_ref[near_rows, :]) + dot(
        far_out[...].astype(bf16), pick_r_ref[far_rows, :]
    )
    target = target_ref[...]
    noise = gradients(
        SPAN,
        bucket_ref,
        target,
        pick_r_ref[...],
        count_ref[...],
        first_subject_ref,
        operator_ref,
        objects_ref,
        query_ref,
        slope_ref,
        flat_ref,
        subject_ref,
    )
    halves(mine, flat_ref, keep_out, give_out)
    pick_t = one_hot(BLOCK, listed(bucket_ref, 1, 1))
    grad_target = dot_last(query_ref[...].astype(bf16), pick_t) + noise
    target, target_state = stepped(target, target_state_ref[...], grad_target)
    for k in range(PIECE):
        if k < PIECE - 1:
            turned_ref[...] = target[LANES * k : LANES * (k + 1), :].T
        else:
            state = jnp.broadcast_to(target_state, (8, LANES))
            own = jnp.full((8, LANES), partner_ref[0, 0].astype(f32))
            zero = jnp.zeros((LANES // 2 - STATE_LANE - 16, LANES), f32)
            tail = [target[LANES * k : DIM, :], state, own, zero]
            turned_ref[...] = jnp.concatenate(tail + tail, 0).T
        rows = slice(HALF_FLAT + 64 * k, HALF_FLAT + 64 * (k + 1))
        keep_out[rows, :] = turned_ref[spaced(mine, 64, 2), :]
        give_out[rows, :] = turned_ref[spaced(1 - mine, 64, 2), :]


FULL = PIECE - 1
TAIL = 2 * FULL
SUM_ROW = TAIL + 1
SUM_ROWS = 5
ROWS = SUM_ROW + SUM_ROWS


def low_lanes(shape):
    return lax.broadcasted_iota(jnp.int32, shape, 1) < LANES // 2


def swapped(value):
    return pltpu.roll(value, LANES // 2, 1)


def merge_body(received_ref, keep_ref, got_ref, out_ref):
    for k in range(FULL):
        rows = slice(HALF_FLAT + 64 * k, HALF_FLAT + 64 * (k + 1))
        out_ref[spaced(k, 64, ROWS), :] = keep_ref[rows, :]
        out_ref[spaced(FULL + k, 64, ROWS), :] = got_ref[rows, :]
    rows = slice(HALF_FLAT + 64 * FULL, HALF_FLAT + 64 * PIECE)
    out_ref[spaced(TAIL, 64, ROWS), :] = jnp.where(
        low_lanes((64, LANES)), keep_ref[rows, :], got_ref[rows, :]
    )
    for k in range(SUM_ROWS):
        rows = slice(64 * k, 64 * (k + 1))
        total = received_ref[0, rows, :] + received_ref[1, rows, :]
        total = total + received_ref[2, rows, :] + received_ref[3, rows, :]
        out_ref[spaced(SUM_ROW + k, 64, ROWS), :] = total


def middle_body(mine_ref, received_ref, out_ref, turned_ref):
    mine = mine_ref[0, 0]
    here, there = (spaced(mine, 64, 2), spaced(1 - mine, 64, 2))
    tail = received_ref[spaced(TAIL, 64, ROWS), :]
    turned_ref[here, :] = tail
    turned_ref[there, :] = swapped(tail)
    back = partner_pick(turned_ref[...]).T.astype(bf16)
    turned_ref[...] = moved(back, turned_ref[...])
    out_ref[spaced(TAIL, 64, ROWS), :] = jnp.where(
        low_lanes((64, LANES)), turned_ref[here, :], swapped(turned_ref[there, :])
    )
    for k in range(FULL):
        turned_ref[here, :] = received_ref[spaced(k, 64, ROWS), :]
        turned_ref[there, :] = received_ref[spaced(FULL + k, 64, ROWS), :]
        turned_ref[...] = moved(back, turned_ref[...])
        out_ref[spaced(k, 64, ROWS), :] = turned_ref[here, :]
        out_ref[spaced(FULL + k, 64, ROWS), :] = turned_ref[there, :]
    for k in range(SUM_ROW, ROWS):
        total = jnp.sum(received_ref[spaced(k, 64, ROWS), :], axis=0, keepdims=True)
        out_ref[spaced(k, 64, ROWS), :] = jnp.broadcast_to(total, (64, LANES))


def parting_body(received_ref, sums_ref, block_ref, give_ref):
    for k in range(FULL):
        rows = slice(64 * k, 64 * (k + 1))
        block_ref[rows, :] = received_ref[spaced(k, 64, ROWS), :]
        give_ref[rows, :] = received_ref[spaced(FULL + k, 64, ROWS), :]
    tail = received_ref[spaced(TAIL, 64, ROWS), :]
    block_ref[64 * FULL :, :] = tail
    give_ref[64 * FULL :, :] = swapped(tail)
    for k in range(SUM_ROWS):
        rows = received_ref[spaced(SUM_ROW + k, 64, ROWS), :]
        for x in range(4):
            sums_ref[x, 64 * k : 64 * (k + 1), :] = rows


def settle_body(mine_ref, block_ref, other_ref, out_ref, state_out, turned_ref):
    mine = mine_ref[0, 0]
    for k in range(PIECE):
        rows = slice(64 * k, 64 * (k + 1))
        turned_ref[spaced(mine, 64, 2), :] = block_ref[rows, :]
        turned_ref[spaced(1 - mine, 64, 2), :] = other_ref[rows, :]
        turned = turned_ref[...].T
        if k < PIECE - 1:
            out_ref[LANES * k : LANES * (k + 1), :] = turned
        else:
            out_ref[LANES * k : DIM, :] = turned[:STATE_LANE, :]
            state_out[...] = turned[STATE_LANE : STATE_LANE + 1, :]


def near_body(part_ref, near_ref, near_state_ref, out_ref, state_out):
    half_update(
        part_ref, static_reader(near_ref), static_reader(near_state_ref), out_ref, state_out
    )


def final_body(
    mine_ref,
    near_ref,
    near_state_ref,
    other_ref,
    far_ref,
    far_state_ref,
    source_ref,
    out_ref,
    state_out,
    source_out,
    source_state_out,
):
    source_out[...] = source_ref[0:DIM, :]
    source_state_out[...] = source_ref[DIM : DIM + 1, :]
    mine = mine_ref[0, 0]
    for k in range(HALF_CHUNKS):
        lanes = slice(LANES * k, LANES * (k + 1))
        near = pl.ds(pl.multiple_of(mine * HALF_REL + LANES * k, LANES), LANES)
        far = pl.ds(pl.multiple_of((1 - mine) * HALF_REL + LANES * k, LANES), LANES)
        out_ref[:, near] = near_ref[:, lanes]
        state_out[:, near] = near_state_ref[:, lanes]
        grad = other_ref[DIM * k : DIM * (k + 1), :]
        out_ref[:, far], state_out[:, far] = stepped(
            far_ref[:, lanes], far_state_ref[:, lanes], grad
        )


def local(
    source_emb,
    source_state,
    dest_emb,
    dest_state,
    relations,
    relation_state,
    partner,
    edge_count,
    source_rows,
    target_rows,
    relation_index,
    negative_rows,
):
    mine = lax.axis_index("core").astype(jnp.int32).reshape(1, 1)
    turned = ((BLOCK, LANES), f32)
    partner = passed_along(partner, "x", -1)
    tile = ((BLOCK * PIECE, LANES), f32)
    (cargo,) = kernel_call(pack_body, [tile], [dest_emb, dest_state.reshape(1, -1)])
    (cargo,) = kernel_call(stamp_body, [tile], [partner, cargo], scalars=1)
    lists = [
        rows.reshape(1, -1) for rows in (source_rows, target_rows, relation_index, negative_rows)
    ]
    (bucket,) = kernel_call(
        bucket_body,
        [((BUCKET_ROWS, LANES), f32)],
        [edge_count, source_emb, source_state.reshape(1, -1)] + lists,
        scalars=1,
    )
    bucket = passed_along(bucket, "x", -1)
    spread, bucket = lax.optimization_barrier((dealt(cargo, DOM, BLOCK), bucket))
    (spread,) = kernel_call(pick_body, [tile], [spread])
    arrived = dealt(spread, DOM, BLOCK)
    block = ((DIM, BLOCK), f32)
    line = ((1, BLOCK), f32)
    half = ((HALF_FLAT, LANES), f32)
    picks_r = ((NREL, SPAN), bf16)
    square = ((BLOCK, BLOCK), f32)
    half_table = ((DIM, HALF_REL), f32)
    half_types = ((1, HALF_REL), f32)
    relation_acc = relation_state.reshape(1, -1)
    grad_subject, grad_objects, target, target_acc, noise, keep, give = kernel_call(
        first_body,
        [WIDE, WIDE, block, line, block, half, half],
        [mine, arrived, bucket, relations],
        [WIDE] * 4 + [FLAT_TABLE],
        scalars=1,
    )
    source, source_acc, target, target_acc = kernel_call(
        update_body,
        [block, line, block, line],
        [bucket, grad_subject, grad_objects, target, target_acc, noise],
    )
    got, source, source_acc, target, target_acc = lax.optimization_barrier(
        (passed_along(give, "core", 1), source, source_acc, target, target_acc)
    )
    part = keep + got
    part = jnp.sum(exchange(part.reshape(4, 320, LANES), "x"), 0)
    part = jnp.sum(exchange(part.reshape(8, 40, LANES), "y"), 0)
    part = jnp.sum(gathered(part, "z"), 0)
    part = gathered(part, "y").reshape(320, LANES)
    part = gathered(part, "x").reshape(HALF_FLAT, LANES)
    other = passed_along(part, "core", 1)
    subject, objects, pick_r, count, near, near_acc = kernel_call(
        lookup_body,
        [WIDE, WIDE, picks_r, square, half_table, half_types],
        [mine, part, relations, relation_acc, source, target, bucket],
        scalars=1,
    )
    table = ((DIM, NREL), f32)
    types = ((1, NREL), f32)
    longer = ((HALF_FLAT + 64 * PIECE, LANES), f32)
    grad_subject, far, far_acc, keep, give = kernel_call(
        second_body,
        [WIDE, half_table, half_types, longer, longer],
        [mine, partner, near, other, target, target_acc, relations, relation_acc]
        + [subject, objects, pick_r, count, bucket],
        [WIDE] * 3 + [FLAT_TABLE, turned],
        scalars=2,
    )
    (source,) = kernel_call(
        last_source_body,
        [((DIM + 8, BLOCK), f32)],
        [bucket, grad_subject, source, source_acc],
    )
    got, source = lax.optimization_barrier((passed_along(give, "core", 1), source))
    source = passed_along(source, "x", 1)
    part = keep[:HALF_FLAT] + got[:HALF_FLAT]
    received = exchange(part.reshape(4, 320, LANES), "x")
    packet = ((64 * ROWS, LANES), f32)
    (packed,) = kernel_call(merge_body, [packet], [received, keep, got])
    packed = packets(packed, ("z", "y"), 64)
    packed, source = lax.optimization_barrier((packed, source))
    (packed,) = kernel_call(middle_body, [packet], [mine, packed], [turned], scalars=1)
    packed = packets(packed, ("z", "y"), 64)
    pieces = ((64 * PIECE, LANES), f32)
    sums, returned, sibling = kernel_call(
        parting_body, [((4, 320, LANES), f32), pieces, pieces], [packed]
    )
    sibling = passed_along(sibling, "core", 1)
    part = exchange(sums, "x").reshape(HALF_FLAT, LANES)
    settled, settled_acc = kernel_call(
        settle_body, [block, line], [mine, returned, sibling], [turned], scalars=1
    )
    part, settled, settled_acc = lax.optimization_barrier((part, settled, settled_acc))
    other = passed_along(part, "core", 1)
    near, near_acc = kernel_call(near_body, [half_table, half_types], [part, near, near_acc])
    relations, relation_acc, source, source_acc = kernel_call(
        final_body,
        [table, types, block, line],
        [mine, near, near_acc, other, far, far_acc, source],
        scalars=1,
    )
    return (
        source,
        source_acc.reshape(-1),
        settled,
        settled_acc.reshape(-1),
        relations,
        relation_acc.reshape(-1),
    )


def solution(mesh):
    fine = Mesh(mesh.devices.reshape(8, 8, 2, 4), ALL)
    in_specs = (
        P(None, ALL),
        P(ALL),
        P(None, ALL),
        P(ALL),
        P(),
        P(),
        P(DOM, "x"),
        P(DOM, "x"),
        P(DOM, "x", None),
        P(DOM, "x", None),
        P(DOM, "x", None),
        P(DOM, "x", None),
    )
    out_specs = (P(None, ALL), P(ALL), P(None, ALL), P(ALL), P(), P())
    return jax.shard_map(local, mesh=fine, in_specs=in_specs, out_specs=out_specs, check_vma=False)
```

```python
import jax
import jax.numpy as jnp
from jax import lax
from jax.experimental import pallas as pl
from jax.experimental.pallas import tpu as pltpu
from jax.sharding import Mesh
from jax.sharding import PartitionSpec as P

DIM = 400
HALF = 200
NREL = 768
BLOCK = 128
SPAN = 512
NEG = 1024
LANES = 128
CHUNKS = NREL // LANES
FLAT = 2560
HALF_FLAT = FLAT // 2
PIECE = 4

ALL = ("z", "y", "core", "x")
DOM = ("z", "y", "core")

learn_rate = 0.3
epsilon = 1e-08

f32 = jnp.float32
bf16 = jnp.bfloat16


def passed_along(value, axis, steps):
    count = lax.axis_size(axis)
    pairs = [(source, (source + steps) % count) for source in range(count)]
    return lax.ppermute(value, axis, pairs)


def exchange(value, axis):
    return lax.all_to_all(value, axis, split_axis=0, concat_axis=0, tiled=True)


def dealt(value, axis, count):
    rows, lanes = value.shape
    return exchange(value.reshape(count, rows // count, lanes), axis).reshape(rows, lanes)


def packets(value, axis, count):
    rows, lanes = value.shape
    parts = rows // (count * PIECE)
    return exchange(value.reshape(count, parts, PIECE, lanes), axis).reshape(rows, lanes)


def gathered(value, axis):
    count = lax.axis_size(axis)
    return exchange(jnp.broadcast_to(value[None], (count,) + value.shape), axis)


def kernel_call(body, outs, args, scratch=(), scalars=0):
    specs = [pl.BlockSpec(memory_space=pltpu.SMEM)] * scalars
    specs += [pl.BlockSpec(memory_space=pltpu.VMEM)] * (len(args) - scalars)
    return pl.pallas_call(
        body,
        out_shape=[jax.ShapeDtypeStruct(shape, dtype) for shape, dtype in outs],
        in_specs=specs,
        out_specs=[pl.BlockSpec(memory_space=pltpu.VMEM)] * len(outs),
        scratch_shapes=[pltpu.VMEM(shape, dtype) for shape, dtype in scratch],
        compiler_params=pltpu.CompilerParams(vmem_limit_bytes=24 * 2**20),
    )(*args)


def dot(left, right):
    return lax.dot_general(left, right, (((1,), (0,)), ((), ())), preferred_element_type=f32)


def dot_last(left, right):
    return lax.dot_general(left, right, (((1,), (1,)), ((), ())), preferred_element_type=f32)


def moved(pick, value):
    upper = value.astype(bf16)
    rest = value - upper.astype(f32)
    middle = rest.astype(bf16)
    lower = (rest - middle.astype(f32)).astype(bf16)
    return (dot(pick, upper) + dot(pick, middle)) + dot(pick, lower)


def one_hot(count, rows):
    hit = lax.broadcasted_iota(jnp.int32, (count, rows.shape[1]), 0) == rows
    return jnp.where(hit, 1.0, 0.0).astype(bf16)


def sigmoid(value):
    return 1.0 / (1.0 + jnp.exp(-value))


def stepped(param, state, grad):
    new_state = state + jnp.sum(grad * grad, axis=0, keepdims=True) * (1.0 / DIM)
    return (param - learn_rate * grad / (jnp.sqrt(new_state) + epsilon), new_state)


def spaced(start, size, stride):
    return pl.ds(start, size, stride=stride)


def pack_body(dest_ref, out_ref):
    for k in range(PIECE - 1):
        out_ref[spaced(k, BLOCK, PIECE), :] = dest_ref[LANES * k : LANES * (k + 1), :].T
    tail = dest_ref[LANES * (PIECE - 1) : DIM, :]
    zero = jnp.zeros((LANES - tail.shape[0], LANES), f32)
    out_ref[spaced(PIECE - 1, BLOCK, PIECE), :] = jnp.concatenate([tail, zero], 0).T


def stamp_body(partner_ref, state_ref, cargo_ref, out_ref):
    rows = spaced(PIECE - 1, BLOCK, PIECE)
    lane = lax.broadcasted_iota(jnp.int32, (BLOCK, LANES), 1)
    own = partner_ref[0, 0].astype(f32)
    out_ref[...] = cargo_ref[...]
    state = jnp.broadcast_to(state_ref[...], (BLOCK, LANES)).T
    last = jnp.where(lane == OWN_LANE, own, cargo_ref[rows, :])
    out_ref[rows, :] = jnp.where(lane == STATE_LANE, state, last)


STATE_ROW = DIM
LIVE_ROW = DIM + 1
LIST_ROWS = (DIM + 8, DIM + 16, DIM + 24, DIM + 32)
BUCKET_ROWS = DIM + 48


def bucket_body(live_ref, source_ref, state_ref, list_s, list_t, list_r, list_n, out_ref):
    out_ref[0:DIM, :] = source_ref[...]
    live = jnp.full((7, LANES), live_ref[0, 0].astype(f32))
    out_ref[DIM : DIM + 8, :] = jnp.concatenate([state_ref[...], live], 0)
    for first, ref in zip(LIST_ROWS, (list_s, list_t, list_r, list_n)):
        for k in range(ref.shape[1] // LANES):
            row = ref[:, LANES * k : LANES * (k + 1)].astype(f32)
            out_ref[first + k : first + k + 1, :] = row


def listed(bucket_ref, which, span):
    count = (NEG if which == 3 else SPAN) // LANES
    first = LIST_ROWS[which] + count * span
    rows = [bucket_ref[first + k : first + k + 1, :] for k in range(count)]
    return jnp.concatenate(rows, 1).astype(jnp.int32)


STATE_LANE = DIM - LANES * (PIECE - 1)
OWN_LANE = STATE_LANE + 8


def partner_pick(last):
    own = last[:, OWN_LANE : OWN_LANE + 1].astype(jnp.int32)
    lane = lax.broadcasted_iota(jnp.int32, (BLOCK, BLOCK), 1)
    return jnp.where(lane == own, 1.0, 0.0)


def pick_body(spread_ref, out_ref):
    last = spread_ref[spaced(PIECE - 1, BLOCK, PIECE), :]
    pick = partner_pick(last).astype(bf16)
    for k in range(PIECE - 1):
        rows = spaced(k, BLOCK, PIECE)
        out_ref[rows, :] = moved(pick, spread_ref[rows, :])
    out_ref[spaced(PIECE - 1, BLOCK, PIECE), :] = moved(pick, last)


def counted(rows_n):
    hits = lax.broadcasted_iota(jnp.int32, (BLOCK, NEG), 0) == rows_n
    count = jnp.sum(jnp.where(hits, 1.0, 0.0), axis=1, keepdims=True)
    return jnp.broadcast_to(count, (BLOCK, BLOCK))


def span_rows(i):
    re = pl.ds(pl.multiple_of(8 * i, 8), 8)
    im = pl.ds(pl.multiple_of(HALF + 8 * i, 8), 8)
    return re, im


HALF_CHUNKS = CHUNKS // 2
HALF_REL = NREL // 2


def half_update(grad_ref, param_of, state_of, out_ref, state_out):
    for k in range(HALF_CHUNKS):
        lanes = slice(LANES * k, LANES * (k + 1))
        grad = grad_ref[DIM * k : DIM * (k + 1), :]
        out_ref[:, lanes], state_out[:, lanes] = stepped(param_of(k), state_of(k), grad)


def chunk_reader(ref, which):
    def read(k):
        first = pl.multiple_of(which * HALF_REL + LANES * k, LANES)
        return ref[:, pl.ds(first, LANES)]

    return read


def static_reader(ref):
    return lambda k: ref[:, LANES * k : LANES * (k + 1)]


def gradients(
    mine,
    first,
    bucket_ref,
    target,
    pick_r_ref,
    count_wide,
    subject_ref,
    operator_ref,
    objects_ref,
    query_ref,
    slope_ref,
    keep_ref,
    give_ref,
    grad_subject_ref,
):
    edge = lax.broadcasted_iota(jnp.int32, (1, SPAN), 1) + first
    live_count = bucket_ref[LIVE_ROW : LIVE_ROW + 1, :]
    live_count = jnp.concatenate([live_count] * (SPAN // LANES), 1).astype(jnp.int32)
    live = jnp.where(edge < live_count, 1.0, 0.0)
    target_bf = target.astype(bf16)

    def form(i, total):
        re, im = span_rows(i)
        subject_re, subject_im = (subject_ref[re, :], subject_ref[im, :])
        operator_re, operator_im = (operator_ref[re, :], operator_ref[im, :])
        query_re = subject_re * operator_re - subject_im * operator_im
        query_im = subject_re * operator_im + subject_im * operator_re
        query_ref[re, :] = query_re
        query_ref[im, :] = query_im
        return total + query_re * objects_ref[re, :] + query_im * objects_ref[im, :]

    total = lax.fori_loop(0, HALF // 8, form, jnp.zeros((8, SPAN), f32), unroll=5)
    positive = jnp.sum(total, axis=0, keepdims=True)
    query_bf = query_ref[...].astype(bf16)
    score = dot(target.T.astype(bf16), query_bf)
    grad_pos = -sigmoid(-positive) * live
    slope = (sigmoid(score) * (live * (1.0 / NEG))).astype(bf16)
    weighted = slope.astype(f32) * count_wide[:, 0:1]
    upper = weighted.astype(bf16)
    lower = (weighted - upper.astype(f32)).astype(bf16)
    slope_ref[...] = dot(target_bf, upper) + dot(target_bf, lower)
    noise = dot_last(query_bf, slope).astype(bf16).astype(f32) * count_wide.T[0:1, :]

    def push(i, _):
        re, im = span_rows(i)
        query_gre = grad_pos * objects_ref[re, :] + slope_ref[re, :]
        query_gim = grad_pos * objects_ref[im, :] + slope_ref[im, :]
        subject_re, subject_im = (subject_ref[re, :], subject_ref[im, :])
        operator_re, operator_im = (operator_ref[re, :], operator_ref[im, :])
        grad_subject_ref[re, :] = query_gre * operator_re + query_gim * operator_im
        grad_subject_ref[im, :] = query_gim * operator_re - query_gre * operator_im
        operator_ref[re, :] = query_gre * subject_re + query_gim * subject_im
        operator_ref[im, :] = query_gim * subject_re - query_gre * subject_im
        query_ref[re, :] = grad_pos * query_ref[re, :]
        query_ref[im, :] = grad_pos * query_ref[im, :]
        return 0

    lax.fori_loop(0, HALF // 8, push, 0, unroll=5)
    grad_operator = operator_ref[...].astype(bf16)
    rest = HALF_FLAT - DIM * HALF_CHUNKS
    for which, out_ref in ((mine, keep_ref), (1 - mine, give_ref)):
        rows = pl.ds(pl.multiple_of(which * HALF_REL, LANES), HALF_REL)
        some = dot_last(grad_operator, pick_r_ref[rows, :])
        for k in range(HALF_CHUNKS):
            out_ref[DIM * k : DIM * (k + 1), :] = some[:, LANES * k : LANES * (k + 1)]
        out_ref[HALF_FLAT - rest : HALF_FLAT, :] = jnp.zeros((rest, LANES), f32)
    return noise


WIDE = ((DIM, SPAN), f32)


def first_body(
    mine_ref,
    arrived_ref,
    bucket_ref,
    relations_ref,
    grad_subject_ref,
    query_ref,
    target_out,
    target_state_out,
    noise_out,
    keep_out,
    give_out,
    subject_ref,
    operator_ref,
    objects_ref,
    slope_ref,
    pick_r_ref,
):
    last = arrived_ref[spaced(PIECE - 1, BLOCK, PIECE), :].T
    target = jnp.concatenate(
        [arrived_ref[spaced(k, BLOCK, PIECE), :].T for k in range(PIECE - 1)]
        + [last[:STATE_LANE, :]],
        0,
    )
    source = bucket_ref[0:DIM, :]
    pick_s = one_hot(BLOCK, listed(bucket_ref, 0, 0))
    pick_t = one_hot(BLOCK, listed(bucket_ref, 1, 0))
    pick_r_ref[...] = one_hot(NREL, listed(bucket_ref, 2, 0))
    subject_ref[...] = dot(source.astype(bf16), pick_s)
    operator_ref[...] = dot(relations_ref[...].astype(bf16), pick_r_ref[...])
    objects_ref[...] = dot(target.astype(bf16), pick_t)
    noise_out[...] = gradients(
        mine_ref[0, 0],
        0,
        bucket_ref,
        target,
        pick_r_ref,
        counted(listed(bucket_ref, 3, 0)),
        subject_ref,
        operator_ref,
        objects_ref,
        query_ref,
        slope_ref,
        keep_out,
        give_out,
        grad_subject_ref,
    )
    target_out[...] = target
    target_state_out[...] = last[STATE_LANE : STATE_LANE + 1, :]


def update_body(
    bucket_ref,
    grad_subject_ref,
    grad_objects_ref,
    target_ref,
    target_state_ref,
    noise_ref,
    source_out,
    source_state_out,
    target_out,
    target_state_out,
):
    pick_s = one_hot(BLOCK, listed(bucket_ref, 0, 0))
    pick_t = one_hot(BLOCK, listed(bucket_ref, 1, 0))
    grad_source = dot_last(grad_subject_ref[...].astype(bf16), pick_s)
    source_out[...], source_state_out[...] = stepped(
        bucket_ref[0:DIM, :], bucket_ref[STATE_ROW : STATE_ROW + 1, :], grad_source
    )
    grad_target = dot_last(grad_objects_ref[...].astype(bf16), pick_t) + noise_ref[...]
    target_out[...], target_state_out[...] = stepped(
        target_ref[...], target_state_ref[...], grad_target
    )


def last_source_body(bucket_ref, grad_subject_ref, source_ref, source_state_ref, source_out):
    pick_s = one_hot(BLOCK, listed(bucket_ref, 0, 1))
    grad_source = dot_last(grad_subject_ref[...].astype(bf16), pick_s)
    source, source_state = stepped(source_ref[...], source_state_ref[...], grad_source)
    source_out[0:DIM, :] = source
    source_out[DIM : DIM + 8, :] = jnp.broadcast_to(source_state, (8, LANES))


def lookup_body(
    mine_ref,
    part_ref,
    relations_ref,
    relation_state_ref,
    source_ref,
    target_ref,
    bucket_ref,
    subject_ref,
    objects_ref,
    pick_r_ref,
    count_ref,
    own_ref,
    own_state_ref,
):
    mine = mine_ref[0, 0]
    half_update(
        part_ref,
        chunk_reader(relations_ref, mine),
        chunk_reader(relation_state_ref, mine),
        own_ref,
        own_state_ref,
    )
    pick_s = one_hot(BLOCK, listed(bucket_ref, 0, 1))
    pick_t = one_hot(BLOCK, listed(bucket_ref, 1, 1))
    subject_ref[...] = dot(source_ref[...].astype(bf16), pick_s)
    objects_ref[...] = dot(target_ref[...].astype(bf16), pick_t)
    pick_r_ref[...] = one_hot(NREL, listed(bucket_ref, 2, 1))
    count_ref[...] = counted(listed(bucket_ref, 3, 1))


def second_body(
    mine_ref,
    partner_ref,
    own_ref,
    other_ref,
    target_ref,
    target_state_ref,
    relations_ref,
    relation_state_ref,
    first_subject_ref,
    objects_ref,
    pick_r_ref,
    count_ref,
    bucket_ref,
    subject_ref,
    far_out,
    far_state_out,
    keep_out,
    give_out,
    operator_ref,
    query_ref,
    slope_ref,
    turned_ref,
):
    mine = mine_ref[0, 0]
    half_update(
        other_ref,
        chunk_reader(relations_ref, 1 - mine),
        chunk_reader(relation_state_ref, 1 - mine),
        far_out,
        far_state_out,
    )
    near_rows = pl.ds(pl.multiple_of(mine * HALF_REL, LANES), HALF_REL)
    far_rows = pl.ds(pl.multiple_of((1 - mine) * HALF_REL, LANES), HALF_REL)
    operator_ref[...] = dot(own_ref[...].astype(bf16), pick_r_ref[near_rows, :]) + dot(
        far_out[...].astype(bf16), pick_r_ref[far_rows, :]
    )
    target = target_ref[...]
    noise = gradients(
        mine,
        SPAN,
        bucket_ref,
        target,
        pick_r_ref,
        count_ref[...],
        first_subject_ref,
        operator_ref,
        objects_ref,
        query_ref,
        slope_ref,
        keep_out,
        give_out,
        subject_ref,
    )
    pick_t = one_hot(BLOCK, listed(bucket_ref, 1, 1))
    grad_target = dot_last(query_ref[...].astype(bf16), pick_t) + noise
    target, target_state = stepped(target, target_state_ref[...], grad_target)
    for k in range(PIECE):
        if k < PIECE - 1:
            turned_ref[...] = target[LANES * k : LANES * (k + 1), :].T
        else:
            state = jnp.broadcast_to(target_state, (8, LANES))
            own = jnp.full((8, LANES), partner_ref[0, 0].astype(f32))
            zero = jnp.zeros((LANES // 2 - STATE_LANE - 16, LANES), f32)
            tail = [target[LANES * k : DIM, :], state, own, zero]
            turned_ref[...] = jnp.concatenate(tail + tail, 0).T
        rows = slice(HALF_FLAT + 64 * k, HALF_FLAT + 64 * (k + 1))
        keep_out[rows, :] = turned_ref[spaced(mine, 64, 2), :]
        give_out[rows, :] = turned_ref[spaced(1 - mine, 64, 2), :]


FULL = PIECE - 1
TAIL = 2 * FULL
SUM_ROW = TAIL + 1
SUM_ROWS = 5
ROWS = SUM_ROW + SUM_ROWS


def low_lanes(shape):
    return lax.broadcasted_iota(jnp.int32, shape, 1) < LANES // 2


def swapped(value):
    return pltpu.roll(value, LANES // 2, 1)


def merge_body(received_ref, keep_ref, got_ref, out_ref):
    for k in range(FULL):
        rows = slice(HALF_FLAT + 64 * k, HALF_FLAT + 64 * (k + 1))
        out_ref[spaced(k, 64, ROWS), :] = keep_ref[rows, :]
        out_ref[spaced(FULL + k, 64, ROWS), :] = got_ref[rows, :]
    rows = slice(HALF_FLAT + 64 * FULL, HALF_FLAT + 64 * PIECE)
    out_ref[spaced(TAIL, 64, ROWS), :] = jnp.where(
        low_lanes((64, LANES)), keep_ref[rows, :], got_ref[rows, :]
    )
    for k in range(SUM_ROWS):
        rows = slice(64 * k, 64 * (k + 1))
        total = received_ref[0, rows, :] + received_ref[1, rows, :]
        total = total + received_ref[2, rows, :] + received_ref[3, rows, :]
        out_ref[spaced(SUM_ROW + k, 64, ROWS), :] = total


def middle_body(mine_ref, received_ref, out_ref, turned_ref):
    mine = mine_ref[0, 0]
    here, there = (spaced(mine, 64, 2), spaced(1 - mine, 64, 2))
    tail = received_ref[spaced(TAIL, 64, ROWS), :]
    turned_ref[here, :] = tail
    turned_ref[there, :] = swapped(tail)
    back = partner_pick(turned_ref[...]).T.astype(bf16)
    turned_ref[...] = moved(back, turned_ref[...])
    out_ref[spaced(TAIL, 64, ROWS), :] = jnp.where(
        low_lanes((64, LANES)), turned_ref[here, :], swapped(turned_ref[there, :])
    )
    for k in range(FULL):
        turned_ref[here, :] = received_ref[spaced(k, 64, ROWS), :]
        turned_ref[there, :] = received_ref[spaced(FULL + k, 64, ROWS), :]
        turned_ref[...] = moved(back, turned_ref[...])
        out_ref[spaced(k, 64, ROWS), :] = turned_ref[here, :]
        out_ref[spaced(FULL + k, 64, ROWS), :] = turned_ref[there, :]
    for k in range(SUM_ROW, ROWS):
        total = jnp.sum(received_ref[spaced(k, 64, ROWS), :], axis=0, keepdims=True)
        out_ref[spaced(k, 64, ROWS), :] = jnp.broadcast_to(total, (64, LANES))


def parting_body(received_ref, sums_ref, block_ref, give_ref):
    for k in range(FULL):
        rows = slice(64 * k, 64 * (k + 1))
        block_ref[rows, :] = received_ref[spaced(k, 64, ROWS), :]
        give_ref[rows, :] = received_ref[spaced(FULL + k, 64, ROWS), :]
    tail = received_ref[spaced(TAIL, 64, ROWS), :]
    block_ref[64 * FULL :, :] = tail
    give_ref[64 * FULL :, :] = swapped(tail)
    for k in range(SUM_ROWS):
        rows = received_ref[spaced(SUM_ROW + k, 64, ROWS), :]
        for x in range(4):
            sums_ref[x, 64 * k : 64 * (k + 1), :] = rows


def settle_body(mine_ref, block_ref, other_ref, out_ref, state_out, turned_ref):
    mine = mine_ref[0, 0]
    for k in range(PIECE):
        rows = slice(64 * k, 64 * (k + 1))
        turned_ref[spaced(mine, 64, 2), :] = block_ref[rows, :]
        turned_ref[spaced(1 - mine, 64, 2), :] = other_ref[rows, :]
        turned = turned_ref[...].T
        if k < PIECE - 1:
            out_ref[LANES * k : LANES * (k + 1), :] = turned
        else:
            out_ref[LANES * k : DIM, :] = turned[:STATE_LANE, :]
            state_out[...] = turned[STATE_LANE : STATE_LANE + 1, :]


def near_body(part_ref, near_ref, near_state_ref, out_ref, state_out):
    half_update(
        part_ref, static_reader(near_ref), static_reader(near_state_ref), out_ref, state_out
    )


def final_body(
    mine_ref,
    near_ref,
    near_state_ref,
    other_ref,
    far_ref,
    far_state_ref,
    source_ref,
    out_ref,
    state_out,
    source_out,
    source_state_out,
):
    source_out[...] = source_ref[0:DIM, :]
    source_state_out[...] = source_ref[DIM : DIM + 1, :]
    mine = mine_ref[0, 0]
    for k in range(HALF_CHUNKS):
        lanes = slice(LANES * k, LANES * (k + 1))
        near = pl.ds(pl.multiple_of(mine * HALF_REL + LANES * k, LANES), LANES)
        far = pl.ds(pl.multiple_of((1 - mine) * HALF_REL + LANES * k, LANES), LANES)
        out_ref[:, near] = near_ref[:, lanes]
        state_out[:, near] = near_state_ref[:, lanes]
        grad = other_ref[DIM * k : DIM * (k + 1), :]
        out_ref[:, far], state_out[:, far] = stepped(
            far_ref[:, lanes], far_state_ref[:, lanes], grad
        )


def local(
    source_emb,
    source_state,
    dest_emb,
    dest_state,
    relations,
    relation_state,
    partner,
    edge_count,
    source_rows,
    target_rows,
    relation_index,
    negative_rows,
):
    mine = lax.axis_index("core").astype(jnp.int32).reshape(1, 1)
    turned = ((BLOCK, LANES), f32)
    partner = passed_along(partner, "x", -1)
    tile = ((BLOCK * PIECE, LANES), f32)
    (cargo,) = kernel_call(pack_body, [tile], [dest_emb])
    (cargo,) = kernel_call(
        stamp_body, [tile], [partner, dest_state.reshape(1, -1), cargo], scalars=1
    )
    lists = [
        rows.reshape(1, -1) for rows in (source_rows, target_rows, relation_index, negative_rows)
    ]
    (bucket,) = kernel_call(
        bucket_body,
        [((BUCKET_ROWS, LANES), f32)],
        [edge_count, source_emb, source_state.reshape(1, -1)] + lists,
        scalars=1,
    )
    bucket = passed_along(bucket, "x", -1)
    spread = dealt(cargo, DOM, BLOCK)
    (spread,) = kernel_call(pick_body, [tile], [spread])
    arrived = dealt(spread, DOM, BLOCK)
    block = ((DIM, BLOCK), f32)
    line = ((1, BLOCK), f32)
    half = ((HALF_FLAT, LANES), f32)
    picks_r = ((NREL, SPAN), bf16)
    square = ((BLOCK, BLOCK), f32)
    half_table = ((DIM, HALF_REL), f32)
    half_types = ((1, HALF_REL), f32)
    relation_acc = relation_state.reshape(1, -1)
    grad_subject, grad_objects, target, target_acc, noise, keep, give = kernel_call(
        first_body,
        [WIDE, WIDE, block, line, block, half, half],
        [mine, arrived, bucket, relations],
        [WIDE] * 4 + [picks_r],
        scalars=1,
    )
    source, source_acc, target, target_acc = kernel_call(
        update_body,
        [block, line, block, line],
        [bucket, grad_subject, grad_objects, target, target_acc, noise],
    )
    got, source, source_acc, target, target_acc = lax.optimization_barrier(
        (passed_along(give, "core", 1), source, source_acc, target, target_acc)
    )
    part = keep + got
    part = jnp.sum(exchange(part.reshape(4, 320, LANES), "x"), 0)
    part = jnp.sum(exchange(part.reshape(8, 40, LANES), "y"), 0)
    part = jnp.sum(gathered(part, "z"), 0)
    part = gathered(part, "y").reshape(320, LANES)
    part = gathered(part, "x").reshape(HALF_FLAT, LANES)
    other = passed_along(part, "core", 1)
    subject, objects, pick_r, count, near, near_acc = kernel_call(
        lookup_body,
        [WIDE, WIDE, picks_r, square, half_table, half_types],
        [mine, part, relations, relation_acc, source, target, bucket],
        scalars=1,
    )
    table = ((DIM, NREL), f32)
    types = ((1, NREL), f32)
    longer = ((HALF_FLAT + 64 * PIECE, LANES), f32)
    grad_subject, far, far_acc, keep, give = kernel_call(
        second_body,
        [WIDE, half_table, half_types, longer, longer],
        [mine, partner, near, other, target, target_acc, relations, relation_acc]
        + [subject, objects, pick_r, count, bucket],
        [WIDE] * 3 + [turned],
        scalars=2,
    )
    (source,) = kernel_call(
        last_source_body,
        [((DIM + 8, BLOCK), f32)],
        [bucket, grad_subject, source, source_acc],
    )
    got, source = lax.optimization_barrier((passed_along(give, "core", 1), source))
    source = passed_along(source, "x", 1)
    part = keep[:HALF_FLAT] + got[:HALF_FLAT]
    received = exchange(part.reshape(4, 320, LANES), "x")
    packet = ((64 * ROWS, LANES), f32)
    (packed,) = kernel_call(merge_body, [packet], [received, keep, got])
    packed = packets(packed, ("z", "y"), 64)
    packed, source = lax.optimization_barrier((packed, source))
    (packed,) = kernel_call(middle_body, [packet], [mine, packed], [turned], scalars=1)
    packed = packets(packed, ("z", "y"), 64)
    pieces = ((64 * PIECE, LANES), f32)
    sums, returned, sibling = kernel_call(
        parting_body, [((4, 320, LANES), f32), pieces, pieces], [packed]
    )
    sibling = passed_along(sibling, "core", 1)
    part = exchange(sums, "x").reshape(HALF_FLAT, LANES)
    settled, settled_acc = kernel_call(
        settle_body, [block, line], [mine, returned, sibling], [turned], scalars=1
    )
    part, settled, settled_acc = lax.optimization_barrier((part, settled, settled_acc))
    other = passed_along(part, "core", 1)
    near, near_acc = kernel_call(near_body, [half_table, half_types], [part, near, near_acc])
    relations, relation_acc, source, source_acc = kernel_call(
        final_body,
        [table, types, block, line],
        [mine, near, near_acc, other, far, far_acc, source],
        scalars=1,
    )
    return (
        source,
        source_acc.reshape(-1),
        settled,
        settled_acc.reshape(-1),
        relations,
        relation_acc.reshape(-1),
    )


def solution(mesh):
    fine = Mesh(mesh.devices.reshape(8, 8, 2, 4), ALL)
    in_specs = (
        P(None, ALL),
        P(ALL),
        P(None, ALL),
        P(ALL),
        P(),
        P(),
        P(DOM, "x"),
        P(DOM, "x"),
        P(DOM, "x", None),
        P(DOM, "x", None),
        P(DOM, "x", None),
        P(DOM, "x", None),
    )
    out_specs = (P(None, ALL), P(ALL), P(None, ALL), P(ALL), P(), P())
    return jax.shard_map(local, mesh=fine, in_specs=in_specs, out_specs=out_specs, check_vma=False)
```

```python
import jax
import jax.numpy as jnp
from jax import lax
from jax.experimental import pallas as pl
from jax.experimental.pallas import tpu as pltpu
from jax.sharding import Mesh
from jax.sharding import PartitionSpec as P

DIM = 400
HALF = 200
NREL = 768
BLOCK = 128
SPAN = 512
NEG = 1024
LANES = 128
CHUNKS = NREL // LANES
FLAT = 2560
HALF_FLAT = FLAT // 2
PIECE = 4

ALL = ("z", "y", "core", "x")
DOM = ("z", "y", "core")

learn_rate = 0.3
epsilon = 1e-08

f32 = jnp.float32
bf16 = jnp.bfloat16


def passed_along(value, axis, steps):
    count = lax.axis_size(axis)
    pairs = [(source, (source + steps) % count) for source in range(count)]
    return lax.ppermute(value, axis, pairs)


def exchange(value, axis):
    return lax.all_to_all(value, axis, split_axis=0, concat_axis=0, tiled=True)


def dealt(value, axis, count):
    rows, lanes = value.shape
    return exchange(value.reshape(count, rows // count, lanes), axis).reshape(rows, lanes)


def packets(value, axis, count):
    rows, lanes = value.shape
    parts = rows // (count * PIECE)
    return exchange(value.reshape(count, parts, PIECE, lanes), axis).reshape(rows, lanes)


def gathered(value, axis):
    count = lax.axis_size(axis)
    return exchange(jnp.broadcast_to(value[None], (count,) + value.shape), axis)


def kernel_call(body, outs, args, scratch=(), scalars=0):
    specs = [pl.BlockSpec(memory_space=pltpu.SMEM)] * scalars
    specs += [pl.BlockSpec(memory_space=pltpu.VMEM)] * (len(args) - scalars)
    return pl.pallas_call(
        body,
        out_shape=[jax.ShapeDtypeStruct(shape, dtype) for shape, dtype in outs],
        in_specs=specs,
        out_specs=[pl.BlockSpec(memory_space=pltpu.VMEM)] * len(outs),
        scratch_shapes=[pltpu.VMEM(shape, dtype) for shape, dtype in scratch],
        compiler_params=pltpu.CompilerParams(vmem_limit_bytes=24 * 2**20),
    )(*args)


def dot(left, right):
    return lax.dot_general(left, right, (((1,), (0,)), ((), ())), preferred_element_type=f32)


def dot_last(left, right):
    return lax.dot_general(left, right, (((1,), (1,)), ((), ())), preferred_element_type=f32)


def moved(pick, value):
    upper = value.astype(bf16)
    rest = value - upper.astype(f32)
    middle = rest.astype(bf16)
    lower = (rest - middle.astype(f32)).astype(bf16)
    return (dot(pick, upper) + dot(pick, middle)) + dot(pick, lower)


def one_hot(count, rows):
    hit = lax.broadcasted_iota(jnp.int32, (count, rows.shape[1]), 0) == rows
    return jnp.where(hit, 1.0, 0.0).astype(bf16)


def sigmoid(value):
    return 1.0 / (1.0 + jnp.exp(-value))


def stepped(param, state, grad):
    new_state = state + jnp.sum(grad * grad, axis=0, keepdims=True) * (1.0 / DIM)
    return (param - learn_rate * grad / (jnp.sqrt(new_state) + epsilon), new_state)


def spaced(start, size, stride):
    return pl.ds(start, size, stride=stride)


def pack_body(dest_ref, out_ref):
    for k in range(PIECE - 1):
        out_ref[spaced(k, BLOCK, PIECE), :] = dest_ref[LANES * k : LANES * (k + 1), :].T
    tail = dest_ref[LANES * (PIECE - 1) : DIM, :]
    zero = jnp.zeros((LANES - tail.shape[0], LANES), f32)
    out_ref[spaced(PIECE - 1, BLOCK, PIECE), :] = jnp.concatenate([tail, zero], 0).T


def stamp_body(partner_ref, state_ref, cargo_ref, out_ref):
    rows = spaced(PIECE - 1, BLOCK, PIECE)
    lane = lax.broadcasted_iota(jnp.int32, (BLOCK, LANES), 1)
    own = partner_ref[0, 0].astype(f32)
    out_ref[...] = cargo_ref[...]
    state = jnp.broadcast_to(state_ref[...], (BLOCK, LANES)).T
    last = jnp.where(lane == OWN_LANE, own, cargo_ref[rows, :])
    out_ref[rows, :] = jnp.where(lane == STATE_LANE, state, last)


STATE_ROW = DIM
LIVE_ROW = DIM + 1
LIST_ROWS = (DIM + 8, DIM + 16, DIM + 24, DIM + 32)
BUCKET_ROWS = DIM + 48


def bucket_body(live_ref, source_ref, state_ref, list_s, list_t, list_r, list_n, out_ref):
    out_ref[0:DIM, :] = source_ref[...]
    live = jnp.full((7, LANES), live_ref[0, 0].astype(f32))
    out_ref[DIM : DIM + 8, :] = jnp.concatenate([state_ref[...], live], 0)
    for first, ref in zip(LIST_ROWS, (list_s, list_t, list_r, list_n)):
        for k in range(ref.shape[1] // LANES):
            row = ref[:, LANES * k : LANES * (k + 1)].astype(f32)
            out_ref[first + k : first + k + 1, :] = row


def listed(bucket_ref, which, span):
    count = (NEG if which == 3 else SPAN) // LANES
    first = LIST_ROWS[which] + count * span
    rows = [bucket_ref[first + k : first + k + 1, :] for k in range(count)]
    return jnp.concatenate(rows, 1).astype(jnp.int32)


STATE_LANE = DIM - LANES * (PIECE - 1)
OWN_LANE = STATE_LANE + 8


def partner_pick(last):
    own = last[:, OWN_LANE : OWN_LANE + 1].astype(jnp.int32)
    lane = lax.broadcasted_iota(jnp.int32, (BLOCK, BLOCK), 1)
    return jnp.where(lane == own, 1.0, 0.0)


def pick_body(spread_ref, out_ref):
    last = spread_ref[spaced(PIECE - 1, BLOCK, PIECE), :]
    pick = partner_pick(last).astype(bf16)
    for k in range(PIECE - 1):
        rows = spaced(k, BLOCK, PIECE)
        out_ref[rows, :] = moved(pick, spread_ref[rows, :])
    out_ref[spaced(PIECE - 1, BLOCK, PIECE), :] = moved(pick, last)


def counted(rows_n):
    hits = lax.broadcasted_iota(jnp.int32, (BLOCK, NEG), 0) == rows_n
    count = jnp.sum(jnp.where(hits, 1.0, 0.0), axis=1, keepdims=True)
    return jnp.broadcast_to(count, (BLOCK, BLOCK))


def span_rows(i):
    re = pl.ds(pl.multiple_of(8 * i, 8), 8)
    im = pl.ds(pl.multiple_of(HALF + 8 * i, 8), 8)
    return re, im


HALF_CHUNKS = CHUNKS // 2
HALF_REL = NREL // 2


def half_update(grad_ref, param_of, state_of, out_ref, state_out):
    for k in range(HALF_CHUNKS):
        lanes = slice(LANES * k, LANES * (k + 1))
        grad = grad_ref[DIM * k : DIM * (k + 1), :]
        out_ref[:, lanes], state_out[:, lanes] = stepped(param_of(k), state_of(k), grad)


def chunk_reader(ref, which):
    def read(k):
        first = pl.multiple_of(which * HALF_REL + LANES * k, LANES)
        return ref[:, pl.ds(first, LANES)]

    return read


def static_reader(ref):
    return lambda k: ref[:, LANES * k : LANES * (k + 1)]


def gradients(
    mine,
    first,
    bucket_ref,
    target,
    pick_r_ref,
    count_wide,
    subject_ref,
    operator_ref,
    objects_ref,
    query_ref,
    slope_ref,
    keep_ref,
    give_ref,
    grad_subject_ref,
):
    edge = lax.broadcasted_iota(jnp.int32, (1, SPAN), 1) + first
    live_count = bucket_ref[LIVE_ROW : LIVE_ROW + 1, :]
    live_count = jnp.concatenate([live_count] * (SPAN // LANES), 1).astype(jnp.int32)
    live = jnp.where(edge < live_count, 1.0, 0.0)
    target_bf = target.astype(bf16)

    def form(i, total):
        re, im = span_rows(i)
        subject_re, subject_im = (subject_ref[re, :], subject_ref[im, :])
        operator_re, operator_im = (operator_ref[re, :], operator_ref[im, :])
        query_re = subject_re * operator_re - subject_im * operator_im
        query_im = subject_re * operator_im + subject_im * operator_re
        query_ref[re, :] = query_re
        query_ref[im, :] = query_im
        return total + query_re * objects_ref[re, :] + query_im * objects_ref[im, :]

    total = lax.fori_loop(0, HALF // 8, form, jnp.zeros((8, SPAN), f32), unroll=5)
    positive = jnp.sum(total, axis=0, keepdims=True)
    query_bf = query_ref[...].astype(bf16)
    score = dot(target.T.astype(bf16), query_bf)
    grad_pos = -sigmoid(-positive) * live
    slope = (sigmoid(score) * (live * (1.0 / NEG))).astype(bf16)
    weighted = slope.astype(f32) * count_wide[:, 0:1]
    upper = weighted.astype(bf16)
    lower = (weighted - upper.astype(f32)).astype(bf16)
    slope_ref[...] = dot(target_bf, upper) + dot(target_bf, lower)
    noise = dot_last(query_bf, slope).astype(bf16).astype(f32) * count_wide.T[0:1, :]

    def push(i, _):
        re, im = span_rows(i)
        query_gre = grad_pos * objects_ref[re, :] + slope_ref[re, :]
        query_gim = grad_pos * objects_ref[im, :] + slope_ref[im, :]
        subject_re, subject_im = (subject_ref[re, :], subject_ref[im, :])
        operator_re, operator_im = (operator_ref[re, :], operator_ref[im, :])
        grad_subject_ref[re, :] = query_gre * operator_re + query_gim * operator_im
        grad_subject_ref[im, :] = query_gim * operator_re - query_gre * operator_im
        operator_ref[re, :] = query_gre * subject_re + query_gim * subject_im
        operator_ref[im, :] = query_gim * subject_re - query_gre * subject_im
        query_ref[re, :] = grad_pos * query_ref[re, :]
        query_ref[im, :] = grad_pos * query_ref[im, :]
        return 0

    lax.fori_loop(0, HALF // 8, push, 0, unroll=5)
    grad_operator = operator_ref[...].astype(bf16)
    rest = HALF_FLAT - DIM * HALF_CHUNKS
    for which, out_ref in ((mine, keep_ref), (1 - mine, give_ref)):
        rows = pl.ds(pl.multiple_of(which * HALF_REL, LANES), HALF_REL)
        some = dot_last(grad_operator, pick_r_ref[rows, :])
        for k in range(HALF_CHUNKS):
            out_ref[DIM * k : DIM * (k + 1), :] = some[:, LANES * k : LANES * (k + 1)]
        out_ref[HALF_FLAT - rest : HALF_FLAT, :] = jnp.zeros((rest, LANES), f32)
    return noise


WIDE = ((DIM, SPAN), f32)


def first_body(
    mine_ref,
    arrived_ref,
    bucket_ref,
    relations_ref,
    grad_subject_ref,
    query_ref,
    target_out,
    target_state_out,
    noise_out,
    keep_out,
    give_out,
    subject_ref,
    operator_ref,
    objects_ref,
    slope_ref,
    pick_r_ref,
):
    last = arrived_ref[spaced(PIECE - 1, BLOCK, PIECE), :].T
    target = jnp.concatenate(
        [arrived_ref[spaced(k, BLOCK, PIECE), :].T for k in range(PIECE - 1)]
        + [last[:STATE_LANE, :]],
        0,
    )
    source = bucket_ref[0:DIM, :]
    pick_s = one_hot(BLOCK, listed(bucket_ref, 0, 0))
    pick_t = one_hot(BLOCK, listed(bucket_ref, 1, 0))
    pick_r_ref[...] = one_hot(NREL, listed(bucket_ref, 2, 0))
    subject_ref[...] = dot(source.astype(bf16), pick_s)
    operator_ref[...] = dot(relations_ref[...].astype(bf16), pick_r_ref[...])
    objects_ref[...] = dot(target.astype(bf16), pick_t)
    noise_out[...] = gradients(
        mine_ref[0, 0],
        0,
        bucket_ref,
        target,
        pick_r_ref,
        counted(listed(bucket_ref, 3, 0)),
        subject_ref,
        operator_ref,
        objects_ref,
        query_ref,
        slope_ref,
        keep_out,
        give_out,
        grad_subject_ref,
    )
    target_out[...] = target
    target_state_out[...] = last[STATE_LANE : STATE_LANE + 1, :]


def update_body(
    bucket_ref,
    grad_subject_ref,
    grad_objects_ref,
    target_ref,
    target_state_ref,
    noise_ref,
    source_out,
    source_state_out,
    target_out,
    target_state_out,
):
    pick_s = one_hot(BLOCK, listed(bucket_ref, 0, 0))
    pick_t = one_hot(BLOCK, listed(bucket_ref, 1, 0))
    grad_source = dot_last(grad_subject_ref[...].astype(bf16), pick_s)
    source_out[...], source_state_out[...] = stepped(
        bucket_ref[0:DIM, :], bucket_ref[STATE_ROW : STATE_ROW + 1, :], grad_source
    )
    grad_target = dot_last(grad_objects_ref[...].astype(bf16), pick_t) + noise_ref[...]
    target_out[...], target_state_out[...] = stepped(
        target_ref[...], target_state_ref[...], grad_target
    )


def last_source_body(bucket_ref, grad_subject_ref, source_ref, source_state_ref, source_out):
    pick_s = one_hot(BLOCK, listed(bucket_ref, 0, 1))
    grad_source = dot_last(grad_subject_ref[...].astype(bf16), pick_s)
    source, source_state = stepped(source_ref[...], source_state_ref[...], grad_source)
    source_out[0:DIM, :] = source
    source_out[DIM : DIM + 8, :] = jnp.broadcast_to(source_state, (8, LANES))


def lookup_body(
    mine_ref,
    part_ref,
    relations_ref,
    relation_state_ref,
    source_ref,
    target_ref,
    bucket_ref,
    subject_ref,
    objects_ref,
    pick_r_ref,
    count_ref,
    own_ref,
    own_state_ref,
):
    mine = mine_ref[0, 0]
    half_update(
        part_ref,
        chunk_reader(relations_ref, mine),
        chunk_reader(relation_state_ref, mine),
        own_ref,
        own_state_ref,
    )
    pick_s = one_hot(BLOCK, listed(bucket_ref, 0, 1))
    pick_t = one_hot(BLOCK, listed(bucket_ref, 1, 1))
    subject_ref[...] = dot(source_ref[...].astype(bf16), pick_s)
    objects_ref[...] = dot(target_ref[...].astype(bf16), pick_t)
    pick_r_ref[...] = one_hot(NREL, listed(bucket_ref, 2, 1))
    count_ref[...] = counted(listed(bucket_ref, 3, 1))


def second_body(
    mine_ref,
    partner_ref,
    own_ref,
    other_ref,
    target_ref,
    target_state_ref,
    relations_ref,
    relation_state_ref,
    first_subject_ref,
    objects_ref,
    pick_r_ref,
    count_ref,
    bucket_ref,
    subject_ref,
    far_out,
    far_state_out,
    keep_out,
    give_out,
    operator_ref,
    query_ref,
    slope_ref,
    turned_ref,
):
    mine = mine_ref[0, 0]
    half_update(
        other_ref,
        chunk_reader(relations_ref, 1 - mine),
        chunk_reader(relation_state_ref, 1 - mine),
        far_out,
        far_state_out,
    )
    near_rows = pl.ds(pl.multiple_of(mine * HALF_REL, LANES), HALF_REL)
    far_rows = pl.ds(pl.multiple_of((1 - mine) * HALF_REL, LANES), HALF_REL)
    operator_ref[...] = dot(own_ref[...].astype(bf16), pick_r_ref[near_rows, :]) + dot(
        far_out[...].astype(bf16), pick_r_ref[far_rows, :]
    )
    target = target_ref[...]
    noise = gradients(
        mine,
        SPAN,
        bucket_ref,
        target,
        pick_r_ref,
        count_ref[...],
        first_subject_ref,
        operator_ref,
        objects_ref,
        query_ref,
        slope_ref,
        keep_out,
        give_out,
        subject_ref,
    )
    pick_t = one_hot(BLOCK, listed(bucket_ref, 1, 1))
    grad_target = dot_last(query_ref[...].astype(bf16), pick_t) + noise
    target, target_state = stepped(target, target_state_ref[...], grad_target)
    for k in range(PIECE):
        if k < PIECE - 1:
            turned_ref[...] = target[LANES * k : LANES * (k + 1), :].T
        else:
            state = jnp.broadcast_to(target_state, (8, LANES))
            own = jnp.full((8, LANES), partner_ref[0, 0].astype(f32))
            zero = jnp.zeros((LANES // 2 - STATE_LANE - 16, LANES), f32)
            tail = [target[LANES * k : DIM, :], state, own, zero]
            turned_ref[...] = jnp.concatenate(tail + tail, 0).T
        rows = slice(HALF_FLAT + 64 * k, HALF_FLAT + 64 * (k + 1))
        keep_out[rows, :] = turned_ref[spaced(mine, 64, 2), :]
        give_out[rows, :] = turned_ref[spaced(1 - mine, 64, 2), :]


FULL = PIECE - 1
TAIL = 2 * FULL
SUM_ROW = TAIL + 1
SUM_ROWS = 5
ROWS = SUM_ROW + SUM_ROWS


def low_lanes(shape):
    return lax.broadcasted_iota(jnp.int32, shape, 1) < LANES // 2


def swapped(value):
    return pltpu.roll(value, LANES // 2, 1)


def merge_body(received_ref, keep_ref, got_ref, out_ref):
    for k in range(FULL):
        rows = slice(HALF_FLAT + 64 * k, HALF_FLAT + 64 * (k + 1))
        out_ref[spaced(k, 64, ROWS), :] = keep_ref[rows, :]
        out_ref[spaced(FULL + k, 64, ROWS), :] = got_ref[rows, :]
    rows = slice(HALF_FLAT + 64 * FULL, HALF_FLAT + 64 * PIECE)
    out_ref[spaced(TAIL, 64, ROWS), :] = jnp.where(
        low_lanes((64, LANES)), keep_ref[rows, :], got_ref[rows, :]
    )
    for k in range(SUM_ROWS):
        rows = slice(64 * k, 64 * (k + 1))
        total = received_ref[0, rows, :] + received_ref[1, rows, :]
        total = total + received_ref[2, rows, :] + received_ref[3, rows, :]
        out_ref[spaced(SUM_ROW + k, 64, ROWS), :] = total


def middle_body(mine_ref, received_ref, out_ref, turned_ref):
    mine = mine_ref[0, 0]
    here, there = (spaced(mine, 64, 2), spaced(1 - mine, 64, 2))
    tail = received_ref[spaced(TAIL, 64, ROWS), :]
    turned_ref[here, :] = tail
    turned_ref[there, :] = swapped(tail)
    back = partner_pick(turned_ref[...]).T.astype(bf16)
    turned_ref[...] = moved(back, turned_ref[...])
    out_ref[spaced(TAIL, 64, ROWS), :] = jnp.where(
        low_lanes((64, LANES)), turned_ref[here, :], swapped(turned_ref[there, :])
    )
    for k in range(FULL):
        turned_ref[here, :] = received_ref[spaced(k, 64, ROWS), :]
        turned_ref[there, :] = received_ref[spaced(FULL + k, 64, ROWS), :]
        turned_ref[...] = moved(back, turned_ref[...])
        out_ref[spaced(k, 64, ROWS), :] = turned_ref[here, :]
        out_ref[spaced(FULL + k, 64, ROWS), :] = turned_ref[there, :]
    for k in range(SUM_ROW, ROWS):
        total = jnp.sum(received_ref[spaced(k, 64, ROWS), :], axis=0, keepdims=True)
        out_ref[spaced(k, 64, ROWS), :] = jnp.broadcast_to(total, (64, LANES))


def parting_body(received_ref, sums_ref, block_ref, give_ref):
    for k in range(FULL):
        rows = slice(64 * k, 64 * (k + 1))
        block_ref[rows, :] = received_ref[spaced(k, 64, ROWS), :]
        give_ref[rows, :] = received_ref[spaced(FULL + k, 64, ROWS), :]
    tail = received_ref[spaced(TAIL, 64, ROWS), :]
    block_ref[64 * FULL :, :] = tail
    give_ref[64 * FULL :, :] = swapped(tail)
    for k in range(SUM_ROWS):
        rows = received_ref[spaced(SUM_ROW + k, 64, ROWS), :]
        for x in range(4):
            sums_ref[x, 64 * k : 64 * (k + 1), :] = rows


def settle_body(mine_ref, block_ref, other_ref, out_ref, state_out, turned_ref):
    mine = mine_ref[0, 0]
    for k in range(PIECE):
        rows = slice(64 * k, 64 * (k + 1))
        turned_ref[spaced(mine, 64, 2), :] = block_ref[rows, :]
        turned_ref[spaced(1 - mine, 64, 2), :] = other_ref[rows, :]
        turned = turned_ref[...].T
        if k < PIECE - 1:
            out_ref[LANES * k : LANES * (k + 1), :] = turned
        else:
            out_ref[LANES * k : DIM, :] = turned[:STATE_LANE, :]
            state_out[...] = turned[STATE_LANE : STATE_LANE + 1, :]


def near_body(part_ref, near_ref, near_state_ref, out_ref, state_out):
    half_update(
        part_ref, static_reader(near_ref), static_reader(near_state_ref), out_ref, state_out
    )


def final_body(
    mine_ref,
    near_ref,
    near_state_ref,
    other_ref,
    far_ref,
    far_state_ref,
    source_ref,
    out_ref,
    state_out,
    source_out,
    source_state_out,
):
    source_out[...] = source_ref[0:DIM, :]
    source_state_out[...] = source_ref[DIM : DIM + 1, :]
    mine = mine_ref[0, 0]
    for k in range(HALF_CHUNKS):
        lanes = slice(LANES * k, LANES * (k + 1))
        near = pl.ds(pl.multiple_of(mine * HALF_REL + LANES * k, LANES), LANES)
        far = pl.ds(pl.multiple_of((1 - mine) * HALF_REL + LANES * k, LANES), LANES)
        out_ref[:, near] = near_ref[:, lanes]
        state_out[:, near] = near_state_ref[:, lanes]
        grad = other_ref[DIM * k : DIM * (k + 1), :]
        out_ref[:, far], state_out[:, far] = stepped(
            far_ref[:, lanes], far_state_ref[:, lanes], grad
        )


def local(
    source_emb,
    source_state,
    dest_emb,
    dest_state,
    relations,
    relation_state,
    partner,
    edge_count,
    source_rows,
    target_rows,
    relation_index,
    negative_rows,
):
    mine = lax.axis_index("core").astype(jnp.int32).reshape(1, 1)
    turned = ((BLOCK, LANES), f32)
    partner = passed_along(partner, "x", -1)
    tile = ((BLOCK * PIECE, LANES), f32)
    (cargo,) = kernel_call(pack_body, [tile], [dest_emb])
    (cargo,) = kernel_call(
        stamp_body, [tile], [partner, dest_state.reshape(1, -1), cargo], scalars=1
    )
    lists = [
        rows.reshape(1, -1) for rows in (source_rows, target_rows, relation_index, negative_rows)
    ]
    (bucket,) = kernel_call(
        bucket_body,
        [((BUCKET_ROWS, LANES), f32)],
        [edge_count, source_emb, source_state.reshape(1, -1)] + lists,
        scalars=1,
    )
    bucket = passed_along(bucket, "x", -1)
    spread, bucket = lax.optimization_barrier((dealt(cargo, DOM, BLOCK), bucket))
    (spread,) = kernel_call(pick_body, [tile], [spread])
    arrived = dealt(spread, DOM, BLOCK)
    block = ((DIM, BLOCK), f32)
    line = ((1, BLOCK), f32)
    half = ((HALF_FLAT, LANES), f32)
    picks_r = ((NREL, SPAN), bf16)
    square = ((BLOCK, BLOCK), f32)
    half_table = ((DIM, HALF_REL), f32)
    half_types = ((1, HALF_REL), f32)
    relation_acc = relation_state.reshape(1, -1)
    grad_subject, grad_objects, target, target_acc, noise, keep, give = kernel_call(
        first_body,
        [WIDE, WIDE, block, line, block, half, half],
        [mine, arrived, bucket, relations],
        [WIDE] * 4 + [picks_r],
        scalars=1,
    )
    source, source_acc, target, target_acc = kernel_call(
        update_body,
        [block, line, block, line],
        [bucket, grad_subject, grad_objects, target, target_acc, noise],
    )
    got, source, source_acc, target, target_acc = lax.optimization_barrier(
        (passed_along(give, "core", 1), source, source_acc, target, target_acc)
    )
    part = keep + got
    part = jnp.sum(exchange(part.reshape(4, 320, LANES), "x"), 0)
    part = jnp.sum(exchange(part.reshape(8, 40, LANES), "y"), 0)
    part = jnp.sum(gathered(part, "z"), 0)
    part = gathered(part, "y").reshape(320, LANES)
    part = gathered(part, "x").reshape(HALF_FLAT, LANES)
    other = passed_along(part, "core", 1)
    subject, objects, pick_r, count, near, near_acc = kernel_call(
        lookup_body,
        [WIDE, WIDE, picks_r, square, half_table, half_types],
        [mine, part, relations, relation_acc, source, target, bucket],
        scalars=1,
    )
    table = ((DIM, NREL), f32)
    types = ((1, NREL), f32)
    longer = ((HALF_FLAT + 64 * PIECE, LANES), f32)
    grad_subject, far, far_acc, keep, give = kernel_call(
        second_body,
        [WIDE, half_table, half_types, longer, longer],
        [mine, partner, near, other, target, target_acc, relations, relation_acc]
        + [subject, objects, pick_r, count, bucket],
        [WIDE] * 3 + [turned],
        scalars=2,
    )
    (source,) = kernel_call(
        last_source_body,
        [((DIM + 8, BLOCK), f32)],
        [bucket, grad_subject, source, source_acc],
    )
    got, source = lax.optimization_barrier((passed_along(give, "core", 1), source))
    source = passed_along(source, "x", 1)
    part = keep[:HALF_FLAT] + got[:HALF_FLAT]
    received = exchange(part.reshape(4, 320, LANES), "x")
    packet = ((64 * ROWS, LANES), f32)
    (packed,) = kernel_call(merge_body, [packet], [received, keep, got])
    packed = packets(packed, ("z", "y"), 64)
    packed, source = lax.optimization_barrier((packed, source))
    (packed,) = kernel_call(middle_body, [packet], [mine, packed], [turned], scalars=1)
    packed = packets(packed, ("z", "y"), 64)
    pieces = ((64 * PIECE, LANES), f32)
    sums, returned, sibling = kernel_call(
        parting_body, [((4, 320, LANES), f32), pieces, pieces], [packed]
    )
    sibling = passed_along(sibling, "core", 1)
    part = exchange(sums, "x").reshape(HALF_FLAT, LANES)
    settled, settled_acc = kernel_call(
        settle_body, [block, line], [mine, returned, sibling], [turned], scalars=1
    )
    part, settled, settled_acc = lax.optimization_barrier((part, settled, settled_acc))
    other = passed_along(part, "core", 1)
    near, near_acc = kernel_call(near_body, [half_table, half_types], [part, near, near_acc])
    relations, relation_acc, source, source_acc = kernel_call(
        final_body,
        [table, types, block, line],
        [mine, near, near_acc, other, far, far_acc, source],
        scalars=1,
    )
    return (
        source,
        source_acc.reshape(-1),
        settled,
        settled_acc.reshape(-1),
        relations,
        relation_acc.reshape(-1),
    )


def solution(mesh):
    fine = Mesh(mesh.devices.reshape(8, 8, 2, 4), ALL)
    in_specs = (
        P(None, ALL),
        P(ALL),
        P(None, ALL),
        P(ALL),
        P(),
        P(),
        P(DOM, "x"),
        P(DOM, "x"),
        P(DOM, "x", None),
        P(DOM, "x", None),
        P(DOM, "x", None),
        P(DOM, "x", None),
    )
    out_specs = (P(None, ALL), P(ALL), P(None, ALL), P(ALL), P(), P())
    return jax.shard_map(local, mesh=fine, in_specs=in_specs, out_specs=out_specs, check_vma=False)
```

```python
import jax
import jax.numpy as jnp
from jax import lax
from jax.experimental import pallas as pl
from jax.experimental.pallas import tpu as pltpu
from jax.sharding import Mesh
from jax.sharding import PartitionSpec as P

DIM = 400
HALF = 200
NREL = 768
BLOCK = 128
SPAN = 512
NEG = 1024
LANES = 128
CHUNKS = NREL // LANES
FLAT = 2560
HALF_FLAT = FLAT // 2
PIECE = 4

ALL = ("z", "y", "core", "x")
DOM = ("z", "y", "core")

learn_rate = 0.3
epsilon = 1e-08

f32 = jnp.float32
bf16 = jnp.bfloat16


def passed_along(value, axis, steps):
    count = lax.axis_size(axis)
    pairs = [(source, (source + steps) % count) for source in range(count)]
    return lax.ppermute(value, axis, pairs)


def exchange(value, axis):
    return lax.all_to_all(value, axis, split_axis=0, concat_axis=0, tiled=True)


def dealt(value, axis, count):
    rows, lanes = value.shape
    return exchange(value.reshape(count, rows // count, lanes), axis).reshape(rows, lanes)


def packets(value, axis, count):
    rows, lanes = value.shape
    parts = rows // (count * PIECE)
    return exchange(value.reshape(count, parts, PIECE, lanes), axis).reshape(rows, lanes)


def gathered(value, axis):
    count = lax.axis_size(axis)
    return exchange(jnp.broadcast_to(value[None], (count,) + value.shape), axis)


def kernel_call(body, outs, args, scratch=(), scalars=0):
    specs = [pl.BlockSpec(memory_space=pltpu.SMEM)] * scalars
    specs += [pl.BlockSpec(memory_space=pltpu.VMEM)] * (len(args) - scalars)
    return pl.pallas_call(
        body,
        out_shape=[jax.ShapeDtypeStruct(shape, dtype) for shape, dtype in outs],
        in_specs=specs,
        out_specs=[pl.BlockSpec(memory_space=pltpu.VMEM)] * len(outs),
        scratch_shapes=[pltpu.VMEM(shape, dtype) for shape, dtype in scratch],
        compiler_params=pltpu.CompilerParams(vmem_limit_bytes=24 * 2**20),
    )(*args)


def dot(left, right):
    return lax.dot_general(left, right, (((1,), (0,)), ((), ())), preferred_element_type=f32)


def dot_last(left, right):
    return lax.dot_general(left, right, (((1,), (1,)), ((), ())), preferred_element_type=f32)


def moved(pick, value):
    upper = value.astype(bf16)
    rest = value - upper.astype(f32)
    middle = rest.astype(bf16)
    lower = (rest - middle.astype(f32)).astype(bf16)
    return (dot(pick, upper) + dot(pick, middle)) + dot(pick, lower)


def one_hot(count, rows):
    hit = lax.broadcasted_iota(jnp.int32, (count, rows.shape[1]), 0) == rows
    return jnp.where(hit, 1.0, 0.0).astype(bf16)


def sigmoid(value):
    return 1.0 / (1.0 + jnp.exp(-value))


def stepped(param, state, grad):
    new_state = state + jnp.sum(grad * grad, axis=0, keepdims=True) * (1.0 / DIM)
    return (param - learn_rate * grad / (jnp.sqrt(new_state) + epsilon), new_state)


def spaced(start, size, stride):
    return pl.ds(start, size, stride=stride)


def pack_body(dest_ref, state_ref, out_ref):
    for k in range(PIECE - 1):
        out_ref[spaced(k, BLOCK, PIECE), :] = dest_ref[LANES * k : LANES * (k + 1), :].T
    tail = dest_ref[LANES * (PIECE - 1) : DIM, :]
    state = jnp.broadcast_to(state_ref[...], (8, LANES))
    zero = jnp.zeros((LANES - tail.shape[0] - 8, LANES), f32)
    out_ref[spaced(PIECE - 1, BLOCK, PIECE), :] = jnp.concatenate([tail, state, zero], 0).T


def stamp_body(partner_ref, cargo_ref, out_ref):
    rows = spaced(PIECE - 1, BLOCK, PIECE)
    lane = lax.broadcasted_iota(jnp.int32, (BLOCK, LANES), 1)
    own = partner_ref[0, 0].astype(f32)
    out_ref[...] = cargo_ref[...]
    out_ref[rows, :] = jnp.where(lane == OWN_LANE, own, cargo_ref[rows, :])


STATE_ROW = DIM
LIVE_ROW = DIM + 1
LIST_ROWS = (DIM + 8, DIM + 16, DIM + 24, DIM + 32)
BUCKET_ROWS = DIM + 48


def bucket_body(live_ref, source_ref, state_ref, list_s, list_t, list_r, list_n, out_ref):
    out_ref[0:DIM, :] = source_ref[...]
    live = jnp.full((7, LANES), live_ref[0, 0].astype(f32))
    out_ref[DIM : DIM + 8, :] = jnp.concatenate([state_ref[...], live], 0)
    for first, ref in zip(LIST_ROWS, (list_s, list_t, list_r, list_n)):
        for k in range(ref.shape[1] // LANES):
            row = ref[:, LANES * k : LANES * (k + 1)].astype(f32)
            out_ref[first + k : first + k + 1, :] = row


def listed(bucket_ref, which, span):
    count = (NEG if which == 3 else SPAN) // LANES
    first = LIST_ROWS[which] + count * span
    rows = [bucket_ref[first + k : first + k + 1, :] for k in range(count)]
    return jnp.concatenate(rows, 1).astype(jnp.int32)


STATE_LANE = DIM - LANES * (PIECE - 1)
OWN_LANE = STATE_LANE + 8


def partner_pick(last):
    own = last[:, OWN_LANE : OWN_LANE + 1].astype(jnp.int32)
    lane = lax.broadcasted_iota(jnp.int32, (BLOCK, BLOCK), 1)
    return jnp.where(lane == own, 1.0, 0.0)


def pick_body(spread_ref, out_ref):
    last = spread_ref[spaced(PIECE - 1, BLOCK, PIECE), :]
    pick = partner_pick(last).astype(bf16)
    for k in range(PIECE - 1):
        rows = spaced(k, BLOCK, PIECE)
        out_ref[rows, :] = moved(pick, spread_ref[rows, :])
    out_ref[spaced(PIECE - 1, BLOCK, PIECE), :] = moved(pick, last)


def counted(rows_n):
    hits = lax.broadcasted_iota(jnp.int32, (BLOCK, NEG), 0) == rows_n
    count = jnp.sum(jnp.where(hits, 1.0, 0.0), axis=1, keepdims=True)
    return jnp.broadcast_to(count, (BLOCK, BLOCK))


def span_rows(i):
    re = pl.ds(pl.multiple_of(8 * i, 8), 8)
    im = pl.ds(pl.multiple_of(HALF + 8 * i, 8), 8)
    return re, im


HALF_CHUNKS = CHUNKS // 2
HALF_REL = NREL // 2


def flat_row(chunk):
    return HALF_FLAT * (chunk // HALF_CHUNKS) + DIM * (chunk % HALF_CHUNKS)


def half_update(grad_ref, param_of, state_of, out_ref, state_out):
    for k in range(HALF_CHUNKS):
        lanes = slice(LANES * k, LANES * (k + 1))
        grad = grad_ref[DIM * k : DIM * (k + 1), :]
        out_ref[:, lanes], state_out[:, lanes] = stepped(param_of(k), state_of(k), grad)


def chunk_reader(ref, which):
    def read(k):
        first = pl.multiple_of(which * HALF_REL + LANES * k, LANES)
        return ref[:, pl.ds(first, LANES)]

    return read


def static_reader(ref):
    return lambda k: ref[:, LANES * k : LANES * (k + 1)]


def gradients(
    first,
    bucket_ref,
    target,
    pick_r,
    count_wide,
    subject_ref,
    operator_ref,
    objects_ref,
    query_ref,
    slope_ref,
    flat_ref,
    grad_subject_ref,
):
    edge = lax.broadcasted_iota(jnp.int32, (1, SPAN), 1) + first
    live_count = bucket_ref[LIVE_ROW : LIVE_ROW + 1, :]
    live_count = jnp.concatenate([live_count] * (SPAN // LANES), 1).astype(jnp.int32)
    live = jnp.where(edge < live_count, 1.0, 0.0)
    target_bf = target.astype(bf16)

    def form(i, total):
        re, im = span_rows(i)
        subject_re, subject_im = (subject_ref[re, :], subject_ref[im, :])
        operator_re, operator_im = (operator_ref[re, :], operator_ref[im, :])
        query_re = subject_re * operator_re - subject_im * operator_im
        query_im = subject_re * operator_im + subject_im * operator_re
        query_ref[re, :] = query_re
        query_ref[im, :] = query_im
        return total + query_re * objects_ref[re, :] + query_im * objects_ref[im, :]

    total = lax.fori_loop(0, HALF // 8, form, jnp.zeros((8, SPAN), f32), unroll=5)
    positive = jnp.sum(total, axis=0, keepdims=True)
    query_bf = query_ref[...].astype(bf16)
    score = dot(target.T.astype(bf16), query_bf)
    grad_pos = -sigmoid(-positive) * live
    slope = (sigmoid(score) * (live * (1.0 / NEG))).astype(bf16)
    weighted = slope.astype(f32) * count_wide[:, 0:1]
    upper = weighted.astype(bf16)
    lower = (weighted - upper.astype(f32)).astype(bf16)
    slope_ref[...] = dot(target_bf, upper) + dot(target_bf, lower)
    noise = dot_last(query_bf, slope).astype(bf16).astype(f32) * count_wide.T[0:1, :]

    def push(i, _):
        re, im = span_rows(i)
        query_gre = grad_pos * objects_ref[re, :] + slope_ref[re, :]
        query_gim = grad_pos * objects_ref[im, :] + slope_ref[im, :]
        subject_re, subject_im = (subject_ref[re, :], subject_ref[im, :])
        operator_re, operator_im = (operator_ref[re, :], operator_ref[im, :])
        grad_subject_ref[re, :] = query_gre * operator_re + query_gim * operator_im
        grad_subject_ref[im, :] = query_gim * operator_re - query_gre * operator_im
        operator_ref[re, :] = query_gre * subject_re + query_gim * subject_im
        operator_ref[im, :] = query_gim * subject_re - query_gre * subject_im
        query_ref[re, :] = grad_pos * query_ref[re, :]
        query_ref[im, :] = grad_pos * query_ref[im, :]
        return 0

    lax.fori_loop(0, HALF // 8, push, 0, unroll=5)
    grad_operator = operator_ref[...].astype(bf16)
    for k in range(0, CHUNKS, 2):
        pair = dot_last(grad_operator, pick_r[LANES * k : LANES * (k + 2), :])
        for c in range(2):
            first = flat_row(k + c)
            flat_ref[first : first + DIM, :] = pair[:, LANES * c : LANES * (c + 1)]
    rest = HALF_FLAT - DIM * HALF_CHUNKS
    for h in range(1, 3):
        flat_ref[HALF_FLAT * h - rest : HALF_FLAT * h, :] = jnp.zeros((rest, LANES), f32)
    return noise


WIDE = ((DIM, SPAN), f32)
FLAT_TABLE = ((FLAT, LANES), f32)


def halves(mine, flat_ref, keep_ref, give_ref):
    keep_ref[0:HALF_FLAT, :] = flat_ref[pl.ds(pl.multiple_of(mine * HALF_FLAT, 8), HALF_FLAT), :]
    give_ref[0:HALF_FLAT, :] = flat_ref[
        pl.ds(pl.multiple_of((1 - mine) * HALF_FLAT, 8), HALF_FLAT), :
    ]


def first_body(
    mine_ref,
    arrived_ref,
    bucket_ref,
    relations_ref,
    grad_subject_ref,
    query_ref,
    target_out,
    target_state_out,
    noise_out,
    keep_out,
    give_out,
    subject_ref,
    operator_ref,
    objects_ref,
    slope_ref,
    flat_ref,
):
    last = arrived_ref[spaced(PIECE - 1, BLOCK, PIECE), :].T
    target = jnp.concatenate(
        [arrived_ref[spaced(k, BLOCK, PIECE), :].T for k in range(PIECE - 1)]
        + [last[:STATE_LANE, :]],
        0,
    )
    source = bucket_ref[0:DIM, :]
    pick_s = one_hot(BLOCK, listed(bucket_ref, 0, 0))
    pick_t = one_hot(BLOCK, listed(bucket_ref, 1, 0))
    pick_r = one_hot(NREL, listed(bucket_ref, 2, 0))
    subject_ref[...] = dot(source.astype(bf16), pick_s)
    operator_ref[...] = dot(relations_ref[...].astype(bf16), pick_r)
    objects_ref[...] = dot(target.astype(bf16), pick_t)
    noise_out[...] = gradients(
        0,
        bucket_ref,
        target,
        pick_r,
        counted(listed(bucket_ref, 3, 0)),
        subject_ref,
        operator_ref,
        objects_ref,
        query_ref,
        slope_ref,
        flat_ref,
        grad_subject_ref,
    )
    halves(mine_ref[0, 0], flat_ref, keep_out, give_out)
    target_out[...] = target
    target_state_out[...] = last[STATE_LANE : STATE_LANE + 1, :]


def update_body(
    bucket_ref,
    grad_subject_ref,
    grad_objects_ref,
    target_ref,
    target_state_ref,
    noise_ref,
    source_out,
    source_state_out,
    target_out,
    target_state_out,
):
    pick_s = one_hot(BLOCK, listed(bucket_ref, 0, 0))
    pick_t = one_hot(BLOCK, listed(bucket_ref, 1, 0))
    grad_source = dot_last(grad_subject_ref[...].astype(bf16), pick_s)
    source_out[...], source_state_out[...] = stepped(
        bucket_ref[0:DIM, :], bucket_ref[STATE_ROW : STATE_ROW + 1, :], grad_source
    )
    grad_target = dot_last(grad_objects_ref[...].astype(bf16), pick_t) + noise_ref[...]
    target_out[...], target_state_out[...] = stepped(
        target_ref[...], target_state_ref[...], grad_target
    )


def last_source_body(bucket_ref, grad_subject_ref, source_ref, source_state_ref, source_out):
    pick_s = one_hot(BLOCK, listed(bucket_ref, 0, 1))
    grad_source = dot_last(grad_subject_ref[...].astype(bf16), pick_s)
    source, source_state = stepped(source_ref[...], source_state_ref[...], grad_source)
    source_out[0:DIM, :] = source
    source_out[DIM : DIM + 8, :] = jnp.broadcast_to(source_state, (8, LANES))


def lookup_body(
    mine_ref,
    part_ref,
    relations_ref,
    relation_state_ref,
    source_ref,
    target_ref,
    bucket_ref,
    subject_ref,
    objects_ref,
    pick_r_ref,
    count_ref,
    own_ref,
    own_state_ref,
):
    mine = mine_ref[0, 0]
    half_update(
        part_ref,
        chunk_reader(relations_ref, mine),
        chunk_reader(relation_state_ref, mine),
        own_ref,
        own_state_ref,
    )
    pick_s = one_hot(BLOCK, listed(bucket_ref, 0, 1))
    pick_t = one_hot(BLOCK, listed(bucket_ref, 1, 1))
    subject_ref[...] = dot(source_ref[...].astype(bf16), pick_s)
    objects_ref[...] = dot(target_ref[...].astype(bf16), pick_t)
    pick_r_ref[...] = one_hot(NREL, listed(bucket_ref, 2, 1))
    count_ref[...] = counted(listed(bucket_ref, 3, 1))


def second_body(
    mine_ref,
    partner_ref,
    own_ref,
    other_ref,
    target_ref,
    target_state_ref,
    relations_ref,
    relation_state_ref,
    first_subject_ref,
    objects_ref,
    pick_r_ref,
    count_ref,
    bucket_ref,
    subject_ref,
    far_out,
    far_state_out,
    keep_out,
    give_out,
    operator_ref,
    query_ref,
    slope_ref,
    flat_ref,
    turned_ref,
):
    mine = mine_ref[0, 0]
    half_update(
        other_ref,
        chunk_reader(relations_ref, 1 - mine),
        chunk_reader(relation_state_ref, 1 - mine),
        far_out,
        far_state_out,
    )
    near_rows = pl.ds(pl.multiple_of(mine * HALF_REL, LANES), HALF_REL)
    far_rows = pl.ds(pl.multiple_of((1 - mine) * HALF_REL, LANES), HALF_REL)
    operator_ref[...] = dot(own_ref[...].astype(bf16), pick_r_ref[near_rows, :]) + dot(
        far_out[...].astype(bf16), pick_r_ref[far_rows, :]
    )
    target = target_ref[...]
    noise = gradients(
        SPAN,
        bucket_ref,
        target,
        pick_r_ref[...],
        count_ref[...],
        first_subject_ref,
        operator_ref,
        objects_ref,
        query_ref,
        slope_ref,
        flat_ref,
        subject_ref,
    )
    halves(mine, flat_ref, keep_out, give_out)
    pick_t = one_hot(BLOCK, listed(bucket_ref, 1, 1))
    grad_target = dot_last(query_ref[...].astype(bf16), pick_t) + noise
    target, target_state = stepped(target, target_state_ref[...], grad_target)
    for k in range(PIECE):
        if k < PIECE - 1:
            turned_ref[...] = target[LANES * k : LANES * (k + 1), :].T
        else:
            state = jnp.broadcast_to(target_state, (8, LANES))
            own = jnp.full((8, LANES), partner_ref[0, 0].astype(f32))
            zero = jnp.zeros((LANES // 2 - STATE_LANE - 16, LANES), f32)
            tail = [target[LANES * k : DIM, :], state, own, zero]
            turned_ref[...] = jnp.concatenate(tail + tail, 0).T
        rows = slice(HALF_FLAT + 64 * k, HALF_FLAT + 64 * (k + 1))
        keep_out[rows, :] = turned_ref[spaced(mine, 64, 2), :]
        give_out[rows, :] = turned_ref[spaced(1 - mine, 64, 2), :]


FULL = PIECE - 1
TAIL = 2 * FULL
SUM_ROW = TAIL + 1
SUM_ROWS = 5
ROWS = SUM_ROW + SUM_ROWS


def low_lanes(shape):
    return lax.broadcasted_iota(jnp.int32, shape, 1) < LANES // 2


def swapped(value):
    return pltpu.roll(value, LANES // 2, 1)


def merge_body(received_ref, keep_ref, got_ref, out_ref):
    for k in range(FULL):
        rows = slice(HALF_FLAT + 64 * k, HALF_FLAT + 64 * (k + 1))
        out_ref[spaced(k, 64, ROWS), :] = keep_ref[rows, :]
        out_ref[spaced(FULL + k, 64, ROWS), :] = got_ref[rows, :]
    rows = slice(HALF_FLAT + 64 * FULL, HALF_FLAT + 64 * PIECE)
    out_ref[spaced(TAIL, 64, ROWS), :] = jnp.where(
        low_lanes((64, LANES)), keep_ref[rows, :], got_ref[rows, :]
    )
    for k in range(SUM_ROWS):
        rows = slice(64 * k, 64 * (k + 1))
        total = received_ref[0, rows, :] + received_ref[1, rows, :]
        total = total + received_ref[2, rows, :] + received_ref[3, rows, :]
        out_ref[spaced(SUM_ROW + k, 64, ROWS), :] = total


def middle_body(mine_ref, received_ref, out_ref, turned_ref):
    mine = mine_ref[0, 0]
    here, there = (spaced(mine, 64, 2), spaced(1 - mine, 64, 2))
    tail = received_ref[spaced(TAIL, 64, ROWS), :]
    turned_ref[here, :] = tail
    turned_ref[there, :] = swapped(tail)
    back = partner_pick(turned_ref[...]).T.astype(bf16)
    turned_ref[...] = moved(back, turned_ref[...])
    out_ref[spaced(TAIL, 64, ROWS), :] = jnp.where(
        low_lanes((64, LANES)), turned_ref[here, :], swapped(turned_ref[there, :])
    )
    for k in range(FULL):
        turned_ref[here, :] = received_ref[spaced(k, 64, ROWS), :]
        turned_ref[there, :] = received_ref[spaced(FULL + k, 64, ROWS), :]
        turned_ref[...] = moved(back, turned_ref[...])
        out_ref[spaced(k, 64, ROWS), :] = turned_ref[here, :]
        out_ref[spaced(FULL + k, 64, ROWS), :] = turned_ref[there, :]
    for k in range(SUM_ROW, ROWS):
        total = jnp.sum(received_ref[spaced(k, 64, ROWS), :], axis=0, keepdims=True)
        out_ref[spaced(k, 64, ROWS), :] = jnp.broadcast_to(total, (64, LANES))


def parting_body(received_ref, sums_ref, block_ref, give_ref):
    for k in range(FULL):
        rows = slice(64 * k, 64 * (k + 1))
        block_ref[rows, :] = received_ref[spaced(k, 64, ROWS), :]
        give_ref[rows, :] = received_ref[spaced(FULL + k, 64, ROWS), :]
    tail = received_ref[spaced(TAIL, 64, ROWS), :]
    block_ref[64 * FULL :, :] = tail
    give_ref[64 * FULL :, :] = swapped(tail)
    for k in range(SUM_ROWS):
        rows = received_ref[spaced(SUM_ROW + k, 64, ROWS), :]
        for x in range(4):
            sums_ref[x, 64 * k : 64 * (k + 1), :] = rows


def settle_body(mine_ref, block_ref, other_ref, out_ref, state_out, turned_ref):
    mine = mine_ref[0, 0]
    for k in range(PIECE):
        rows = slice(64 * k, 64 * (k + 1))
        turned_ref[spaced(mine, 64, 2), :] = block_ref[rows, :]
        turned_ref[spaced(1 - mine, 64, 2), :] = other_ref[rows, :]
        turned = turned_ref[...].T
        if k < PIECE - 1:
            out_ref[LANES * k : LANES * (k + 1), :] = turned
        else:
            out_ref[LANES * k : DIM, :] = turned[:STATE_LANE, :]
            state_out[...] = turned[STATE_LANE : STATE_LANE + 1, :]


def near_body(part_ref, near_ref, near_state_ref, out_ref, state_out):
    half_update(
        part_ref, static_reader(near_ref), static_reader(near_state_ref), out_ref, state_out
    )


def final_body(
    mine_ref,
    near_ref,
    near_state_ref,
    other_ref,
    far_ref,
    far_state_ref,
    source_ref,
    out_ref,
    state_out,
    source_out,
    source_state_out,
):
    source_out[...] = source_ref[0:DIM, :]
    source_state_out[...] = source_ref[DIM : DIM + 1, :]
    mine = mine_ref[0, 0]
    for k in range(HALF_CHUNKS):
        lanes = slice(LANES * k, LANES * (k + 1))
        near = pl.ds(pl.multiple_of(mine * HALF_REL + LANES * k, LANES), LANES)
        far = pl.ds(pl.multiple_of((1 - mine) * HALF_REL + LANES * k, LANES), LANES)
        out_ref[:, near] = near_ref[:, lanes]
        state_out[:, near] = near_state_ref[:, lanes]
        grad = other_ref[DIM * k : DIM * (k + 1), :]
        out_ref[:, far], state_out[:, far] = stepped(
            far_ref[:, lanes], far_state_ref[:, lanes], grad
        )


def local(
    source_emb,
    source_state,
    dest_emb,
    dest_state,
    relations,
    relation_state,
    partner,
    edge_count,
    source_rows,
    target_rows,
    relation_index,
    negative_rows,
):
    mine = lax.axis_index("core").astype(jnp.int32).reshape(1, 1)
    turned = ((BLOCK, LANES), f32)
    partner = passed_along(partner, "x", -1)
    tile = ((BLOCK * PIECE, LANES), f32)
    (cargo,) = kernel_call(pack_body, [tile], [dest_emb, dest_state.reshape(1, -1)])
    (cargo,) = kernel_call(stamp_body, [tile], [partner, cargo], scalars=1)
    lists = [
        rows.reshape(1, -1) for rows in (source_rows, target_rows, relation_index, negative_rows)
    ]
    (bucket,) = kernel_call(
        bucket_body,
        [((BUCKET_ROWS, LANES), f32)],
        [edge_count, source_emb, source_state.reshape(1, -1)] + lists,
        scalars=1,
    )
    bucket = passed_along(bucket, "x", -1)
    spread = dealt(cargo, DOM, BLOCK)
    (spread,) = kernel_call(pick_body, [tile], [spread])
    arrived = dealt(spread, DOM, BLOCK)
    block = ((DIM, BLOCK), f32)
    line = ((1, BLOCK), f32)
    half = ((HALF_FLAT, LANES), f32)
    picks_r = ((NREL, SPAN), bf16)
    square = ((BLOCK, BLOCK), f32)
    half_table = ((DIM, HALF_REL), f32)
    half_types = ((1, HALF_REL), f32)
    relation_acc = relation_state.reshape(1, -1)
    grad_subject, grad_objects, target, target_acc, noise, keep, give = kernel_call(
        first_body,
        [WIDE, WIDE, block, line, block, half, half],
        [mine, arrived, bucket, relations],
        [WIDE] * 4 + [FLAT_TABLE],
        scalars=1,
    )
    source, source_acc, target, target_acc = kernel_call(
        update_body,
        [block, line, block, line],
        [bucket, grad_subject, grad_objects, target, target_acc, noise],
    )
    got, source, source_acc, target, target_acc = lax.optimization_barrier(
        (passed_along(give, "core", 1), source, source_acc, target, target_acc)
    )
    part = keep + got
    part = jnp.sum(exchange(part.reshape(4, 320, LANES), "x"), 0)
    part = jnp.sum(exchange(part.reshape(8, 40, LANES), "y"), 0)
    part = jnp.sum(gathered(part, "z"), 0)
    part = gathered(part, "y").reshape(320, LANES)
    part = gathered(part, "x").reshape(HALF_FLAT, LANES)
    other = passed_along(part, "core", 1)
    subject, objects, pick_r, count, near, near_acc = kernel_call(
        lookup_body,
        [WIDE, WIDE, picks_r, square, half_table, half_types],
        [mine, part, relations, relation_acc, source, target, bucket],
        scalars=1,
    )
    table = ((DIM, NREL), f32)
    types = ((1, NREL), f32)
    longer = ((HALF_FLAT + 64 * PIECE, LANES), f32)
    grad_subject, far, far_acc, keep, give = kernel_call(
        second_body,
        [WIDE, half_table, half_types, longer, longer],
        [mine, partner, near, other, target, target_acc, relations, relation_acc]
        + [subject, objects, pick_r, count, bucket],
        [WIDE] * 3 + [FLAT_TABLE, turned],
        scalars=2,
    )
    (source,) = kernel_call(
        last_source_body,
        [((DIM + 8, BLOCK), f32)],
        [bucket, grad_subject, source, source_acc],
    )
    got, source = lax.optimization_barrier((passed_along(give, "core", 1), source))
    source = passed_along(source, "x", 1)
    part = keep[:HALF_FLAT] + got[:HALF_FLAT]
    received = exchange(part.reshape(4, 320, LANES), "x")
    packet = ((64 * ROWS, LANES), f32)
    (packed,) = kernel_call(merge_body, [packet], [received, keep, got])
    packed = packets(packed, ("z", "y"), 64)
    (packed,) = kernel_call(middle_body, [packet], [mine, packed], [turned], scalars=1)
    packed = packets(packed, ("z", "y"), 64)
    pieces = ((64 * PIECE, LANES), f32)
    packed, source = lax.optimization_barrier((packed, source))
    sums, returned, sibling = kernel_call(
        parting_body, [((4, 320, LANES), f32), pieces, pieces], [packed]
    )
    sibling = passed_along(sibling, "core", 1)
    part = exchange(sums, "x").reshape(HALF_FLAT, LANES)
    settled, settled_acc = kernel_call(
        settle_body, [block, line], [mine, returned, sibling], [turned], scalars=1
    )
    part, settled, settled_acc = lax.optimization_barrier((part, settled, settled_acc))
    other = passed_along(part, "core", 1)
    near, near_acc = kernel_call(near_body, [half_table, half_types], [part, near, near_acc])
    relations, relation_acc, source, source_acc = kernel_call(
        final_body,
        [table, types, block, line],
        [mine, near, near_acc, other, far, far_acc, source],
        scalars=1,
    )
    return (
        source,
        source_acc.reshape(-1),
        settled,
        settled_acc.reshape(-1),
        relations,
        relation_acc.reshape(-1),
    )


def solution(mesh):
    fine = Mesh(mesh.devices.reshape(8, 8, 2, 4), ALL)
    in_specs = (
        P(None, ALL),
        P(ALL),
        P(None, ALL),
        P(ALL),
        P(),
        P(),
        P(DOM, "x"),
        P(DOM, "x"),
        P(DOM, "x", None),
        P(DOM, "x", None),
        P(DOM, "x", None),
        P(DOM, "x", None),
    )
    out_specs = (P(None, ALL), P(ALL), P(None, ALL), P(ALL), P(), P())
    return jax.shard_map(local, mesh=fine, in_specs=in_specs, out_specs=out_specs, check_vma=False)
```
